256 devices in a mesh: lat: 4 (over y_lo, core), lon: 64 (over x, y_hi, z).
Axes of the slice: x: 4, y: 4 (y_hi: 2, y_lo: 2; y = y_hi * 2 + y_lo), z: 8, core: 2. Of those that a mesh axis runs over, the one named last changes fastest.
Arguments:
- inputs: bfloat16 [48, 1536, 2, 512], P('lat', 'lon'), may hold values from -6 to 6
- shift_lat: int32 [1], replicated, may hold values from 1 to 5
- shift_lon: int32 [1], replicated, may hold values from 1 to 11
- gain_attn: float32 [512], replicated, may hold values from 0.1 to 1.9
- w_qkv: bfloat16 [512, 1536], replicated, may hold values from -0.25 to 0.25
- w_out: bfloat16 [512, 512], replicated, may hold values from -0.25 to 0.25
- gain_merge: float32 [2048], replicated, may hold values from 0.1 to 1.9
- w_merge: bfloat16 [2048, 1024], replicated, may hold values from -0.125 to 0.125
- cot_coarse: bfloat16 [24, 768, 2, 1024], P('lat', 'lon'), may hold values from -6 to 6
- cot_skip: bfloat16 [48, 1536, 2, 512], P('lat', 'lon'), may hold values from -6 to 6
Outputs:
- coarse: bfloat16 [24, 768, 2, 1024], P('lat', 'lon')
- skip: bfloat16 [48, 1536, 2, 512], P('lat', 'lon')
- grad_input: bfloat16 [48, 1536, 2, 512], P('lat', 'lon')
The draws below stay inside these ranges and needn't reach their ends.
All inputs are finite; a program needn't handle non-finite values.
Results may differ from the reference program's by a relative error of at most 0.015.
Values may be sent and summed in bfloat16 or wider, within the bound.
A program may use at most 128 MiB of HBM per device.

```python
import jax
import jax.numpy as jnp
from jax import lax

C1 = 512
C2 = 1024
HEADS = 8
WLAT = 6
WLON = 12
LEV = 2
NLAT = 48
NLON = 1536


def block_levels(own_key, extent, split, least, high):
    def one(dim, blocks):
        draws = jax.random.uniform(jax.random.fold_in(jax.random.fold_in(own_key, 6), dim), (blocks,), jnp.float32, least / len(split), high / len(split))
        return jnp.repeat(jnp.exp(draws), extent[dim] // blocks).reshape((-1,) + (1,) * (len(extent) - dim - 1))

    factor_of = one(*split[0])
    for cut in split[1:]:
        factor_of = factor_of * one(*cut)
    return factor_of


def noise(own_key, extent, deviation, limit, shards=(), kind=jnp.bfloat16):
    loudness = block_levels(own_key, extent, shards, -0.22, 0.18) if shards else 1.0
    entries = jax.random.normal(own_key, extent, jnp.float32) * deviation * loudness
    return jnp.minimum(jnp.maximum(entries, -limit), limit).astype(kind)


def setup_inputs(seed: int = 0) -> dict:
    streams_of = jax.random.split(jax.random.key(seed), 11)
    return {
        "inputs": noise(streams_of[0], (NLAT, NLON, LEV, C1), 1.0, 6.0, ((0, 4), (1, 64))),
        "shift_lat": jax.random.randint(streams_of[1], (1,), 1, WLAT).astype(jnp.int32),
        "shift_lon": jax.random.randint(streams_of[2], (1,), 1, WLON).astype(jnp.int32),
        "gain_attn": jnp.clip(1.0 + 0.18 * jax.random.normal(streams_of[3], (C1,), jnp.float32), 0.1, 1.9),
        "w_qkv": noise(streams_of[4], (C1, 3 * C1), C1 ** -0.5, 0.25),
        "w_out": noise(streams_of[5], (C1, C1), C1 ** -0.5, 0.25),
        "gain_merge": jnp.clip(1.0 + 0.18 * jax.random.normal(streams_of[6], (4 * C1,), jnp.float32), 0.1, 1.9),
        "w_merge": noise(streams_of[7], (4 * C1, C2), (4 * C1) ** -0.5, 0.125),
        "cot_coarse": noise(streams_of[8], (NLAT // 2, NLON // 2, LEV, C2), 1.0, 6.0, ((0, 4), (1, 64))),
        "cot_skip": noise(streams_of[9], (NLAT, NLON, LEV, C1), 1.0, 6.0, ((0, 4), (1, 64))),
    }


def normalize(values_in):
    row_mean = lax.optimization_barrier(jnp.mean(values_in, -1, keepdims=True))
    centred = values_in - row_mean
    variance = lax.optimization_barrier(jnp.mean(centred * centred, -1, keepdims=True))
    return centred * lax.rsqrt(variance + 1e-05)

def to_windows(field):
    lat_rows, lon_cols, level_count, feature_width = field.shape
    shaped = field.reshape(lat_rows // WLAT, WLAT, lon_cols // WLON, WLON, level_count, feature_width)
    return shaped.transpose(0, 2, 1, 3, 4, 5).reshape(-1, WLAT * WLON * level_count, feature_width)

def from_windows(field, lat_rows, lon_cols, level_count):
    feature_width = field.shape[-1]
    shaped = field.reshape(lat_rows // WLAT, lon_cols // WLON, WLAT, WLON, level_count, feature_width)
    return shaped.transpose(0, 2, 1, 3, 4, 5).reshape(lat_rows, lon_cols, level_count, feature_width)

def attend(windows, regions, head_count):
    window_count, token_count, triple_width = windows.shape
    feature_width = triple_width // 3
    head_size = feature_width // head_count
    query_part = windows[..., :feature_width].reshape(window_count, token_count, head_count, head_size).astype(jnp.float32)
    key_part = windows[..., feature_width:2 * feature_width].reshape(window_count, token_count, head_count, head_size).astype(jnp.float32)
    value_part = windows[..., 2 * feature_width:].reshape(window_count, token_count, head_count, head_size).astype(jnp.float32)
    scores = jnp.einsum('wthd,wshd->whts', query_part, key_part) * head_size ** (-0.5)
    same_region = regions[:, None, :, None] == regions[:, None, None, :]
    scores = jnp.where(same_region, scores, jnp.float32(-1e+30))
    row_top = lax.stop_gradient(lax.optimization_barrier(jnp.max(scores, -1, keepdims=True)))
    exp_scores = jnp.exp(scores - row_top)
    soft_weights = (exp_scores / lax.optimization_barrier(jnp.sum(exp_scores, -1, keepdims=True))).astype(jnp.bfloat16)
    mixed = jnp.einsum('whts,wshd->wthd', soft_weights.astype(jnp.float32), value_part)
    return mixed.astype(jnp.bfloat16).reshape(window_count, token_count, feature_width)

def attention_branch(rolled, region_rows, gain_attn, w_qkv, w_out):
    lat_rows, lon_cols, level_count, feature_width = rolled.shape
    normed_tokens = (normalize(rolled.astype(jnp.float32)) * gain_attn).astype(jnp.bfloat16)
    projected = jnp.dot(normed_tokens, w_qkv, preferred_element_type=jnp.float32).astype(jnp.bfloat16)
    windows = to_windows(projected)
    region_field = jnp.broadcast_to(region_rows[:, None, None, None], (lat_rows, lon_cols, level_count, 1))
    regions = to_windows(region_field)[..., 0]
    token_count = windows.shape[1]
    window_groups = windows.reshape(lat_rows // WLAT, lon_cols // WLON, token_count, 3 * feature_width)
    region_groups = regions.reshape(lat_rows // WLAT, lon_cols // WLON, token_count)
    group_fn = jax.checkpoint(lambda pair: attend(pair[0], pair[1], HEADS))
    mixed = lax.map(group_fn, (window_groups, region_groups))
    unwindowed = from_windows(mixed.reshape(-1, token_count, feature_width), lat_rows, lon_cols, level_count)
    return jnp.dot(unwindowed, w_out, preferred_element_type=jnp.float32).astype(jnp.bfloat16)

def merge_patches(skip, gain_merge, w_merge):
    lat_rows, lon_cols, level_count, feature_width = skip.shape
    grouped = skip.reshape(lat_rows // 2, 2, lon_cols // 2, 2, level_count, feature_width)
    grouped = grouped.transpose(0, 2, 4, 1, 3, 5).reshape(lat_rows // 2, lon_cols // 2, level_count, 4 * feature_width)
    merged = (normalize(grouped.astype(jnp.float32)) * gain_merge).astype(jnp.bfloat16)
    return jnp.dot(merged, w_merge, preferred_element_type=jnp.float32).astype(jnp.bfloat16)

def forward(inputs, lat_shift, lon_shift, gain_attn, w_qkv, w_out, gain_merge, w_merge):
    lat_rows = inputs.shape[0]
    rolled = jnp.roll(inputs, (-lat_shift, -lon_shift), axis=(0, 1))
    lat_pos = jnp.arange(lat_rows, dtype=jnp.int32)
    region_rows = (lat_pos >= lat_rows - lat_shift).astype(jnp.int32)
    branch = attention_branch(rolled, region_rows, gain_attn, w_qkv, w_out)
    placed = jnp.roll(branch, (lat_shift, lon_shift), axis=(0, 1))
    skip = (inputs.astype(jnp.float32) + placed.astype(jnp.float32)).astype(jnp.bfloat16)
    coarse = merge_patches(skip, gain_merge, w_merge)
    return (coarse, skip)

def reference(inputs, shift_lat, shift_lon, gain_attn, w_qkv, w_out, gain_merge, w_merge, cot_coarse, cot_skip):
    lat_shift = shift_lat[0].astype(jnp.int32)
    lon_shift = shift_lon[0].astype(jnp.int32)

    def whole(field):
        return forward(field, lat_shift, lon_shift, gain_attn, w_qkv, w_out, gain_merge, w_merge)
    outputs, backward = jax.vjp(whole, inputs)
    grad_input = backward((cot_coarse, cot_skip))[0]
    return (outputs[0], outputs[1], grad_input)
```

```python
import functools

import jax
import jax.numpy as jnp
from jax import lax
from jax.experimental import pallas as pl
from jax.experimental.pallas import tpu as pltpu
from jax.sharding import PartitionSpec as P

WLAT = 6
WLON = 12
PAIRS = 4
TOK = 144
FEAT = 512
EPS = 1e-05
BF = jnp.bfloat16
F32 = jnp.float32
MESH = pl.DeviceIdType.MESH


def dot(a, b):
    return jnp.dot(a, b, preferred_element_type=F32)


def dot_t(a, b):
    return lax.dot_general(a, b, (((1,), (1,)), ((), ())), preferred_element_type=F32)


def t_dot(a, b):
    return lax.dot_general(a, b, (((0,), (0,)), ((), ())), preferred_element_type=F32)


def kernel(
    behind_lat, behind_lon, halo_lat, halo_lon,
    shift_lat, shift_lon, gain_attn, gain_merge,
    inputs, w_qkv_hbm, w_out_hbm, w_merge_hbm, cot_coarse_hbm, cot_skip_hbm,
    coarse_hbm, skip_hbm, grad_hbm,
    own, ext, bext, gext, rext, gskip, skip, cot_skip, cot_coarse, coarse, out,
    w_qkv, w_out, w_merge,
    gm, merged, normed, norm, rstd, proj, mixed, soft, dproj, bias,
    local_sem, out_sem, send_sem, recv_sem,
):
    rows, cols = own.shape[0], own.shape[1]
    lat, lon = lax.axis_index("lat"), lax.axis_index("lon")
    nlat, nlon = lax.axis_size("lat"), lax.axis_size("lon")
    band = rows * nlat

    def device(step_lat, step_lon):
        return (lax.rem(lat + step_lat + nlat, nlat), lax.rem(lon + step_lon + nlon, nlon))

    dlat, dlon = (-1 if behind_lat else 1), (-1 if behind_lon else 1)
    steps = ((dlat, 0), (0, dlon), (dlat, dlon))
    own_r, own_c = (halo_lat if behind_lat else 0), (halo_lon if behind_lon else 0)
    halo_r, halo_c = (0 if behind_lat else rows), (0 if behind_lon else cols)
    back_r, back_c = (0 if behind_lat else halo_lat), (0 if behind_lon else halo_lon)
    bhalo_r, bhalo_c = (rows if behind_lat else 0), (cols if behind_lon else 0)
    edge_r, edge_c = (rows - halo_lat if behind_lat else 0), (cols - halo_lon if behind_lon else 0)
    bedge_r, bedge_c = (0 if behind_lat else rows - halo_lat), (0 if behind_lon else cols - halo_lon)

    def piece(ref, which, r, c, fr, fc):
        rr = pl.ds(fr, rows) if which == 1 else pl.ds(r, halo_lat)
        cc = pl.ds(fc, cols) if which == 0 else pl.ds(c, halo_lon)
        return ref.at[rr, cc]

    def ahead(phase, source, base_r, base_c, target):
        copies = []
        for which, (sr, sc) in enumerate(steps):
            copies.append(pltpu.make_async_remote_copy(
                src_ref=piece(source, which, base_r + edge_r, base_c + edge_c, base_r, base_c),
                dst_ref=piece(target, which, halo_r, halo_c, own_r, own_c),
                send_sem=send_sem.at[phase, which],
                recv_sem=recv_sem.at[phase, which],
                device_id=device(-sr, -sc),
                device_id_type=MESH,
            ))
        return copies

    def back(phase, ref):
        copies = []
        for which, (sr, sc) in enumerate(steps):
            copies.append(pltpu.make_async_remote_copy(
                src_ref=piece(ref, which, back_r + bedge_r, back_c + bedge_c, back_r, back_c),
                dst_ref=piece(ref, which, bhalo_r, bhalo_c, back_r, back_c),
                send_sem=send_sem.at[phase, which],
                recv_sem=recv_sem.at[phase, which],
                device_id=device(sr, sc),
                device_id_type=MESH,
            ))
        return copies

    loads = [
        pltpu.make_async_copy(src, dst, local_sem.at[i])
        for i, (src, dst) in enumerate((
            (cot_coarse_hbm, cot_coarse),
            (w_merge_hbm, w_merge),
            (inputs, own),
            (w_qkv_hbm, w_qkv),
            (w_out_hbm, w_out),
            (inputs, ext.at[pl.ds(own_r, rows), pl.ds(own_c, cols)]),
            (cot_skip_hbm, cot_skip),
        ))
    ]
    barrier = pltpu.get_barrier_semaphore()
    for sr, sc in steps:
        pl.semaphore_signal(barrier, inc=1, device_id=device(sr, sc), device_id_type=MESH)
        pl.semaphore_signal(barrier, inc=1, device_id=device(-sr, -sc), device_id_type=MESH)
    for load in loads:
        load.start()
    pl.semaphore_wait(barrier, 6)
    first = ahead(0, inputs, 0, 0, ext)
    for copy in first:
        copy.start()

    s_lat, s_lon = shift_lat[0], shift_lon[0]
    t_lat = s_lat - (WLAT - halo_lat) if behind_lat else s_lat
    t_lon = s_lon - (WLON - halo_lon) if behind_lon else s_lon
    li, lj = int(behind_lat), int(behind_lon)
    places = ((li, lj), (li, 1 - lj), (1 - li, lj), (1 - li, 1 - lj))

    def tile(slot):
        return pl.ds(slot * TOK, TOK)

    low = lax.broadcasted_iota(jnp.int32, (TOK, 128), 1) < 64
    zero = jnp.zeros((TOK, 128), BF)

    def both(x):
        return jnp.concatenate([jnp.where(low, x, zero), jnp.where(low, zero, x)], 0)

    def unite(x):
        return jnp.where(low, x[:TOK], x[TOK:])

    for wi in range(2):
        base = lax.rem(rows * lat - WLAT * li + WLAT * wi + band, band)
        edge = 2 * WLON * (band - s_lat - base)
        row_in = lax.broadcasted_iota(jnp.int32, (TOK, TOK), 0) >= edge
        col_in = lax.broadcasted_iota(jnp.int32, (TOK, TOK), 1) >= edge
        bias[wi] = jnp.where(row_in != col_in, F32(-1e30), F32(0.0))

    def norm_tokens(x, slot):
        mean = jnp.mean(x, -1, keepdims=True)
        centred = x - mean
        inv = lax.rsqrt(jnp.mean(centred * centred, -1, keepdims=True) + EPS)
        n = centred * inv
        norm[tile(slot)] = n
        rstd[tile(slot)] = jnp.broadcast_to(inv, (TOK, 128))
        normed[tile(slot)] = (n * gain_attn[...]).astype(BF)

    def attend(slot, p):
        at = pl.multiple_of(p * 128, 128)
        rr = tile(slot)
        q = both(proj[rr, pl.ds(at, 128)] * BF(0.125))
        k = proj[rr, pl.ds(FEAT + at, 128)]
        v = proj[rr, pl.ds(2 * FEAT + at, 128)]
        b = bias[places[slot][0]]
        scores = dot_t(q, k) + jnp.concatenate([b, b], 0)
        e = jnp.exp(scores - jnp.max(scores, -1, keepdims=True))
        w = (e * (1.0 / jnp.sum(e, -1, keepdims=True))).astype(BF)
        soft[slot, p] = w
        mixed[rr, pl.ds(at, 128)] = unite(dot(w, v)).astype(BF)

    def attend_back(slot, p):
        at = pl.multiple_of(p * 128, 128)
        rr = tile(slot)
        q = both(proj[rr, pl.ds(at, 128)] * BF(0.125))
        k = proj[rr, pl.ds(FEAT + at, 128)]
        v = proj[rr, pl.ds(2 * FEAT + at, 128)]
        g = both(mixed[rr, pl.ds(at, 128)])
        w = soft[slot, p]
        dw = dot_t(g, v)
        wf = w.astype(F32)
        ds = (wf * (dw - jnp.sum(dw * wf, -1, keepdims=True))).astype(BF)
        dproj[rr, pl.ds(at, 128)] = (unite(dot(ds, k)) * 0.125).astype(BF)
        dproj[rr, pl.ds(FEAT + at, 128)] = t_dot(ds, q).astype(BF)
        dproj[rr, pl.ds(2 * FEAT + at, 128)] = t_dot(w, g).astype(BF)

    def pairs(step, slots):
        if len(slots) == 1:
            for p in range(PAIRS):
                step(slots[0], p)
        else:
            def body(p, carry):
                for slot in slots:
                    step(slot, p)
                return carry
            lax.fori_loop(0, PAIRS, body, 0)

    def window(ref, slot):
        wi, wj = places[slot]
        x = ref[pl.ds(t_lat + WLAT * wi, WLAT), pl.ds(t_lon + WLON * wj, WLON)]
        return x.reshape(TOK, FEAT)

    def local_window(ref):
        return ref[pl.ds(s_lat, WLAT), pl.ds(s_lon, WLON)].reshape(TOK, FEAT)

    def put_window(ref, slot, x):
        wi, wj = places[slot]
        ref[pl.ds(back_r + WLAT * wi, WLAT), pl.ds(back_c + WLON * wj, WLON)] = x.reshape(
            WLAT, WLON, 2, FEAT
        )

    def run_forward(slots, fetch):
        lo, n = slots[0] * TOK, len(slots) * TOK
        for slot in slots:
            norm_tokens(fetch(slot).astype(F32), slot)
        proj[pl.ds(lo, n)] = dot(normed[pl.ds(lo, n)], w_qkv[...]).astype(BF)
        pairs(attend, slots)
        branch = dot(mixed[pl.ds(lo, n)], w_out[...]).astype(BF)
        for i, slot in enumerate(slots):
            put_window(bext, slot, branch[i * TOK:(i + 1) * TOK])

    def run_backward(slots, fetch):
        lo, n = slots[0] * TOK, len(slots) * TOK
        for slot in slots:
            normed[tile(slot)] = fetch(slot)
        mixed[pl.ds(lo, n)] = dot_t(normed[pl.ds(lo, n)], w_out[...]).astype(BF)
        pairs(attend_back, slots)
        dnormed = dot_t(dproj[pl.ds(lo, n)], w_qkv[...]).astype(BF)
        for i, slot in enumerate(slots):
            d = dnormed[i * TOK:(i + 1) * TOK].astype(F32) * gain_attn[...]
            nn = norm[tile(slot)]
            inv = rstd[tile(slot)][:, :1]
            dx = inv * (
                d - jnp.mean(d, -1, keepdims=True) - nn * jnp.mean(d * nn, -1, keepdims=True)
            )
            put_window(rext, slot, dx.astype(BF))

    loads[0].wait()
    loads[1].wait()
    gm[...] = dot_t(cot_coarse.reshape(TOK, 2 * FEAT)[...], w_merge[...]).astype(BF)
    loads[2].wait()
    loads[3].wait()
    loads[4].wait()
    run_forward((0,), lambda slot: local_window(own))
    loads[5].wait()
    for copy in first:
        copy.wait_recv()
    run_forward((1, 2, 3), lambda slot: window(ext, slot))
    second = back(1, bext)
    for copy in second:
        copy.start()
    loads[6].wait()
    for copy in second:
        copy.wait_recv()

    start_r, start_c = halo_lat - t_lat, halo_lon - t_lon
    skip[...] = (
        own[...].astype(F32)
        + bext[pl.ds(start_r, rows), pl.ds(start_c, cols)].astype(F32)
    ).astype(BF)
    skip_out = pltpu.make_async_copy(skip, skip_hbm, out_sem.at[0])
    skip_out.start()

    patches = (rows // 2, 2, cols // 2, 2, 2, FEAT)
    quarters = [(a, b) for a in range(2) for b in range(2)]

    def quarter(ref, a, b):
        return ref.reshape(*patches)[:, a, :, b].reshape(TOK, FEAT)

    parts = [quarter(skip, a, b).astype(F32) for a, b in quarters]
    width = 4 * FEAT
    mean = sum(jnp.sum(x, -1, keepdims=True) for x in parts) / width
    parts = [x - mean for x in parts]
    inv = lax.rsqrt(sum(jnp.sum(x * x, -1, keepdims=True) for x in parts) / width + EPS)
    parts = [x * inv for x in parts]
    grads = []
    for i, x in enumerate(parts):
        gain = gain_merge[:, pl.ds(i * FEAT, FEAT)]
        merged[:, pl.ds(i * FEAT, FEAT)] = (x * gain).astype(BF)
        grads.append(gm[:, pl.ds(i * FEAT, FEAT)].astype(F32) * gain)
    mean_g = sum(jnp.sum(g, -1, keepdims=True) for g in grads) / width
    mean_gx = sum(jnp.sum(g * x, -1, keepdims=True) for g, x in zip(grads, parts)) / width
    for (a, b), g, x in zip(quarters, grads, parts):
        d = (inv * (g - mean_g - x * mean_gx)).astype(BF) + quarter(cot_skip, a, b)
        gskip.reshape(*patches)[:, a, :, b] = d.reshape(rows // 2, cols // 2, 2, FEAT)
    gext[pl.ds(own_r, rows), pl.ds(own_c, cols)] = gskip[...]
    third = ahead(2, gext, own_r, own_c, gext)
    for copy in third:
        copy.start()

    coarse.reshape(TOK, 2 * FEAT)[...] = dot(merged[...], w_merge[...]).astype(BF)
    coarse_out = pltpu.make_async_copy(coarse, coarse_hbm, out_sem.at[1])
    coarse_out.start()
    run_backward((0,), lambda slot: local_window(gskip))
    for copy in third:
        copy.wait_recv()
    run_backward((1, 2, 3), lambda slot: window(gext, slot))
    fourth = back(3, rext)
    for copy in fourth:
        copy.start()
    for copy in fourth:
        copy.wait_recv()
    out[...] = gskip[...] + rext[pl.ds(start_r, rows), pl.ds(start_c, cols)]
    grad_out = pltpu.make_async_copy(out, grad_hbm, out_sem.at[2])
    grad_out.start()
    for copy in first + second + third + fourth:
        copy.wait_send()
    skip_out.wait()
    coarse_out.wait()
    grad_out.wait()


def block(behind_lat, behind_lon, halo_lat, halo_lon, ident, args):
    (inputs, shift_lat, shift_lon, gain_attn, w_qkv, w_out, gain_merge, w_merge,
     cot_coarse, cot_skip) = args
    rows, cols, lev, feat = inputs.shape
    wide = (rows + halo_lat, cols + halo_lon, lev, feat)
    tokens = rows * cols * lev
    smem = pl.BlockSpec(memory_space=pltpu.SMEM)
    vmem = pl.BlockSpec(memory_space=pltpu.VMEM)
    anyw = pl.BlockSpec(memory_space=pl.ANY)
    return pl.pallas_call(
        functools.partial(kernel, behind_lat, behind_lon, halo_lat, halo_lon),
        out_shape=(
            jax.ShapeDtypeStruct(cot_coarse.shape, BF),
            jax.ShapeDtypeStruct(inputs.shape, BF),
            jax.ShapeDtypeStruct(inputs.shape, BF),
        ),
        in_specs=[smem, smem, vmem, vmem] + [anyw] * 6,
        out_specs=(anyw, anyw, anyw),
        scratch_shapes=[
            pltpu.VMEM(inputs.shape, BF),
            pltpu.VMEM(wide, BF),
            pltpu.VMEM(wide, BF),
            pltpu.VMEM(wide, BF),
            pltpu.VMEM(wide, BF),
            pltpu.VMEM(inputs.shape, BF),
            pltpu.VMEM(inputs.shape, BF),
            pltpu.VMEM(inputs.shape, BF),
            pltpu.VMEM(cot_coarse.shape, BF),
            pltpu.VMEM(cot_coarse.shape, BF),
            pltpu.VMEM(inputs.shape, BF),
            pltpu.VMEM(w_qkv.shape, BF),
            pltpu.VMEM(w_out.shape, BF),
            pltpu.VMEM(w_merge.shape, BF),
            pltpu.VMEM((TOK, 4 * FEAT), BF),
            pltpu.VMEM((TOK, 4 * FEAT), BF),
            pltpu.VMEM((tokens, FEAT), BF),
            pltpu.VMEM((tokens, FEAT), F32),
            pltpu.VMEM((tokens, 128), F32),
            pltpu.VMEM((tokens, 3 * FEAT), BF),
            pltpu.VMEM((tokens, FEAT), BF),
            pltpu.VMEM((4, PAIRS, 2 * TOK, TOK), BF),
            pltpu.VMEM((tokens, 3 * FEAT), BF),
            pltpu.VMEM((2, TOK, TOK), F32),
            pltpu.SemaphoreType.DMA((7,)),
            pltpu.SemaphoreType.DMA((3,)),
            pltpu.SemaphoreType.DMA((4, 3)),
            pltpu.SemaphoreType.DMA((4, 3)),
        ],
        compiler_params=pltpu.CompilerParams(
            collective_id=ident, has_side_effects=True, vmem_limit_bytes=48 * 2**20
        ),
    )(
        shift_lat, shift_lon, gain_attn.reshape(1, -1), gain_merge.reshape(1, -1),
        inputs, w_qkv, w_out, w_merge, cot_coarse, cot_skip,
    )


def local(*args):
    return block(False, False, WLAT - 1, WLON - 1, 0, args)


def solution(mesh):
    tile = P("lat", "lon", None, None)
    return jax.shard_map(
        local,
        mesh=mesh,
        in_specs=(tile, P(), P(), P(), P(), P(), P(), P(), tile, tile),
        out_specs=(tile, tile, tile),
        check_vma=False,
    )
```

```python
import functools

import jax
import jax.numpy as jnp
from jax import lax
from jax.experimental import pallas as pl
from jax.experimental.pallas import tpu as pltpu
from jax.sharding import PartitionSpec as P

WLAT = 6
WLON = 12
PAIRS = 4
TOK = 144
FEAT = 512
EPS = 1e-05
BF = jnp.bfloat16
F32 = jnp.float32
MESH = pl.DeviceIdType.MESH


def dot(a, b):
    return jnp.dot(a, b, preferred_element_type=F32)


def dot_t(a, b):
    return lax.dot_general(a, b, (((1,), (1,)), ((), ())), preferred_element_type=F32)


def t_dot(a, b):
    return lax.dot_general(a, b, (((0,), (0,)), ((), ())), preferred_element_type=F32)


def kernel(
    behind_lat, behind_lon, halo_lat, halo_lon,
    shift_lat, shift_lon, gain_attn, gain_merge,
    inputs, w_qkv_hbm, w_out_hbm, w_merge_hbm, cot_coarse_hbm, cot_skip_hbm,
    coarse_hbm, skip_hbm, grad_hbm,
    own, ext, bext, gext, rext, gskip, skip, cot_skip, cot_coarse, coarse, out,
    w_qkv, w_out, w_merge,
    gm, merged, normed, norm, rstd, proj, mixed, soft, dproj, bias,
    local_sem, out_sem, send_sem, recv_sem,
):
    rows, cols = own.shape[0], own.shape[1]
    lat, lon = lax.axis_index("lat"), lax.axis_index("lon")
    nlat, nlon = lax.axis_size("lat"), lax.axis_size("lon")
    band = rows * nlat

    def device(step_lat, step_lon):
        return (lax.rem(lat + step_lat + nlat, nlat), lax.rem(lon + step_lon + nlon, nlon))

    dlat, dlon = (-1 if behind_lat else 1), (-1 if behind_lon else 1)
    steps = ((dlat, 0), (0, dlon), (dlat, dlon))
    own_r, own_c = (halo_lat if behind_lat else 0), (halo_lon if behind_lon else 0)
    halo_r, halo_c = (0 if behind_lat else rows), (0 if behind_lon else cols)
    back_r, back_c = (0 if behind_lat else halo_lat), (0 if behind_lon else halo_lon)
    bhalo_r, bhalo_c = (rows if behind_lat else 0), (cols if behind_lon else 0)
    edge_r, edge_c = (rows - halo_lat if behind_lat else 0), (cols - halo_lon if behind_lon else 0)
    bedge_r, bedge_c = (0 if behind_lat else rows - halo_lat), (0 if behind_lon else cols - halo_lon)

    def piece(ref, which, r, c, fr, fc):
        rr = pl.ds(fr, rows) if which == 1 else pl.ds(r, halo_lat)
        cc = pl.ds(fc, cols) if which == 0 else pl.ds(c, halo_lon)
        return ref.at[rr, cc]

    def ahead(phase, source, base_r, base_c, target):
        copies = []
        for which, (sr, sc) in enumerate(steps):
            copies.append(pltpu.make_async_remote_copy(
                src_ref=piece(source, which, base_r + edge_r, base_c + edge_c, base_r, base_c),
                dst_ref=piece(target, which, halo_r, halo_c, own_r, own_c),
                send_sem=send_sem.at[phase, which],
                recv_sem=recv_sem.at[phase, which],
                device_id=device(-sr, -sc),
                device_id_type=MESH,
            ))
        return copies

    def back(phase, ref):
        copies = []
        for which, (sr, sc) in enumerate(steps):
            copies.append(pltpu.make_async_remote_copy(
                src_ref=piece(ref, which, back_r + bedge_r, back_c + bedge_c, back_r, back_c),
                dst_ref=piece(ref, which, bhalo_r, bhalo_c, back_r, back_c),
                send_sem=send_sem.at[phase, which],
                recv_sem=recv_sem.at[phase, which],
                device_id=device(sr, sc),
                device_id_type=MESH,
            ))
        return copies

    loads = [
        pltpu.make_async_copy(src, dst, local_sem.at[i])
        for i, (src, dst) in enumerate((
            (cot_coarse_hbm, cot_coarse),
            (w_merge_hbm, w_merge),
            (inputs, own),
            (w_qkv_hbm, w_qkv),
            (w_out_hbm, w_out),
            (inputs, ext.at[pl.ds(own_r, rows), pl.ds(own_c, cols)]),
            (cot_skip_hbm, cot_skip),
        ))
    ]
    barrier = pltpu.get_barrier_semaphore()
    for sr, sc in steps:
        pl.semaphore_signal(barrier, inc=1, device_id=device(sr, sc), device_id_type=MESH)
        pl.semaphore_signal(barrier, inc=1, device_id=device(-sr, -sc), device_id_type=MESH)
    for load in loads:
        load.start()
    pl.semaphore_wait(barrier, 6)
    first = ahead(0, inputs, 0, 0, ext)
    for copy in first:
        copy.start()

    s_lat, s_lon = shift_lat[0], shift_lon[0]
    t_lat = jnp.clip(s_lat - (WLAT - halo_lat) if behind_lat else s_lat, 0, halo_lat)
    t_lon = jnp.clip(s_lon - (WLON - halo_lon) if behind_lon else s_lon, 0, halo_lon)
    li, lj = int(behind_lat), int(behind_lon)
    places = ((li, lj), (li, 1 - lj), (1 - li, lj), (1 - li, 1 - lj))

    def tile(slot):
        return pl.ds(slot * TOK, TOK)

    low = lax.broadcasted_iota(jnp.int32, (TOK, 128), 1) < 64
    zero = jnp.zeros((TOK, 128), BF)

    def both(x):
        return jnp.concatenate([jnp.where(low, x, zero), jnp.where(low, zero, x)], 0)

    def unite(x):
        return jnp.where(low, x[:TOK], x[TOK:])

    for wi in range(2):
        base = lax.rem(rows * lat - WLAT * li + WLAT * wi + band, band)
        edge = 2 * WLON * (band - s_lat - base)
        row_in = lax.broadcasted_iota(jnp.int32, (TOK, TOK), 0) >= edge
        col_in = lax.broadcasted_iota(jnp.int32, (TOK, TOK), 1) >= edge
        bias[wi] = jnp.where(row_in != col_in, F32(-1e30), F32(0.0))

    def norm_tokens(x, slot):
        mean = jnp.mean(x, -1, keepdims=True)
        centred = x - mean
        inv = lax.rsqrt(jnp.mean(centred * centred, -1, keepdims=True) + EPS)
        n = centred * inv
        norm[tile(slot)] = n
        rstd[tile(slot)] = jnp.broadcast_to(inv, (TOK, 128))
        normed[tile(slot)] = (n * gain_attn[...]).astype(BF)

    def attend(slot, p):
        at = pl.multiple_of(p * 128, 128)
        rr = tile(slot)
        q = both(proj[rr, pl.ds(at, 128)] * BF(0.125))
        k = proj[rr, pl.ds(FEAT + at, 128)]
        v = proj[rr, pl.ds(2 * FEAT + at, 128)]
        b = bias[places[slot][0]]
        scores = dot_t(q, k) + jnp.concatenate([b, b], 0)
        e = jnp.exp(scores - jnp.max(scores, -1, keepdims=True))
        w = (e * (1.0 / jnp.sum(e, -1, keepdims=True))).astype(BF)
        soft[slot, p] = w
        mixed[rr, pl.ds(at, 128)] = unite(dot(w, v)).astype(BF)

    def attend_back(slot, p):
        at = pl.multiple_of(p * 128, 128)
        rr = tile(slot)
        q = both(proj[rr, pl.ds(at, 128)] * BF(0.125))
        k = proj[rr, pl.ds(FEAT + at, 128)]
        v = proj[rr, pl.ds(2 * FEAT + at, 128)]
        g = both(mixed[rr, pl.ds(at, 128)])
        w = soft[slot, p]
        dw = dot_t(g, v)
        wf = w.astype(F32)
        ds = (wf * (dw - jnp.sum(dw * wf, -1, keepdims=True))).astype(BF)
        dproj[rr, pl.ds(at, 128)] = (unite(dot(ds, k)) * 0.125).astype(BF)
        dproj[rr, pl.ds(FEAT + at, 128)] = t_dot(ds, q).astype(BF)
        dproj[rr, pl.ds(2 * FEAT + at, 128)] = t_dot(w, g).astype(BF)

    def pairs(step, slots):
        if len(slots) == 1:
            for p in range(PAIRS):
                step(slots[0], p)
        else:
            def body(p, carry):
                for slot in slots:
                    step(slot, p)
                return carry
            lax.fori_loop(0, PAIRS, body, 0)

    def window(ref, slot):
        wi, wj = places[slot]
        x = ref[pl.ds(t_lat + WLAT * wi, WLAT), pl.ds(t_lon + WLON * wj, WLON)]
        return x.reshape(TOK, FEAT)

    def local_window(ref):
        return ref[pl.ds(s_lat, WLAT), pl.ds(s_lon, WLON)].reshape(TOK, FEAT)

    def put_window(ref, slot, x):
        wi, wj = places[slot]
        ref[pl.ds(back_r + WLAT * wi, WLAT), pl.ds(back_c + WLON * wj, WLON)] = x.reshape(
            WLAT, WLON, 2, FEAT
        )

    def run_forward(slots, fetch):
        lo, n = slots[0] * TOK, len(slots) * TOK
        for slot in slots:
            norm_tokens(fetch(slot).astype(F32), slot)
        proj[pl.ds(lo, n)] = dot(normed[pl.ds(lo, n)], w_qkv[...]).astype(BF)
        pairs(attend, slots)
        branch = dot(mixed[pl.ds(lo, n)], w_out[...]).astype(BF)
        for i, slot in enumerate(slots):
            put_window(bext, slot, branch[i * TOK:(i + 1) * TOK])

    def run_backward(slots, fetch):
        lo, n = slots[0] * TOK, len(slots) * TOK
        for slot in slots:
            normed[tile(slot)] = fetch(slot)
        mixed[pl.ds(lo, n)] = dot_t(normed[pl.ds(lo, n)], w_out[...]).astype(BF)
        pairs(attend_back, slots)
        dnormed = dot_t(dproj[pl.ds(lo, n)], w_qkv[...]).astype(BF)
        for i, slot in enumerate(slots):
            d = dnormed[i * TOK:(i + 1) * TOK].astype(F32) * gain_attn[...]
            nn = norm[tile(slot)]
            inv = rstd[tile(slot)][:, :1]
            dx = inv * (
                d - jnp.mean(d, -1, keepdims=True) - nn * jnp.mean(d * nn, -1, keepdims=True)
            )
            put_window(rext, slot, dx.astype(BF))

    loads[0].wait()
    loads[1].wait()
    gm[...] = dot_t(cot_coarse.reshape(TOK, 2 * FEAT)[...], w_merge[...]).astype(BF)
    loads[2].wait()
    loads[3].wait()
    loads[4].wait()
    run_forward((0,), lambda slot: local_window(own))
    loads[5].wait()
    for copy in first:
        copy.wait_recv()
    run_forward((1, 2, 3), lambda slot: window(ext, slot))
    second = back(1, bext)
    for copy in second:
        copy.start()
    loads[6].wait()
    for copy in second:
        copy.wait_recv()

    start_r, start_c = halo_lat - t_lat, halo_lon - t_lon
    skip[...] = (
        own[...].astype(F32)
        + bext[pl.ds(start_r, rows), pl.ds(start_c, cols)].astype(F32)
    ).astype(BF)
    skip_out = pltpu.make_async_copy(skip, skip_hbm, out_sem.at[0])
    skip_out.start()

    patches = (rows // 2, 2, cols // 2, 2, 2, FEAT)
    quarters = [(a, b) for a in range(2) for b in range(2)]

    def quarter(ref, a, b):
        return ref.reshape(*patches)[:, a, :, b].reshape(TOK, FEAT)

    parts = [quarter(skip, a, b).astype(F32) for a, b in quarters]
    width = 4 * FEAT
    mean = sum(jnp.sum(x, -1, keepdims=True) for x in parts) / width
    parts = [x - mean for x in parts]
    inv = lax.rsqrt(sum(jnp.sum(x * x, -1, keepdims=True) for x in parts) / width + EPS)
    parts = [x * inv for x in parts]
    grads = []
    for i, x in enumerate(parts):
        gain = gain_merge[:, pl.ds(i * FEAT, FEAT)]
        merged[:, pl.ds(i * FEAT, FEAT)] = (x * gain).astype(BF)
        grads.append(gm[:, pl.ds(i * FEAT, FEAT)].astype(F32) * gain)
    mean_g = sum(jnp.sum(g, -1, keepdims=True) for g in grads) / width
    mean_gx = sum(jnp.sum(g * x, -1, keepdims=True) for g, x in zip(grads, parts)) / width
    for (a, b), g, x in zip(quarters, grads, parts):
        d = (inv * (g - mean_g - x * mean_gx)).astype(BF) + quarter(cot_skip, a, b)
        gskip.reshape(*patches)[:, a, :, b] = d.reshape(rows // 2, cols // 2, 2, FEAT)
    gext[pl.ds(own_r, rows), pl.ds(own_c, cols)] = gskip[...]
    third = ahead(2, gext, own_r, own_c, gext)
    for copy in third:
        copy.start()

    coarse.reshape(TOK, 2 * FEAT)[...] = dot(merged[...], w_merge[...]).astype(BF)
    coarse_out = pltpu.make_async_copy(coarse, coarse_hbm, out_sem.at[1])
    coarse_out.start()
    run_backward((0,), lambda slot: local_window(gskip))
    for copy in third:
        copy.wait_recv()
    run_backward((1, 2, 3), lambda slot: window(gext, slot))
    fourth = back(3, rext)
    for copy in fourth:
        copy.start()
    for copy in fourth:
        copy.wait_recv()
    out[...] = gskip[...] + rext[pl.ds(start_r, rows), pl.ds(start_c, cols)]
    grad_out = pltpu.make_async_copy(out, grad_hbm, out_sem.at[2])
    grad_out.start()
    for copy in first + second + third + fourth:
        copy.wait_send()
    skip_out.wait()
    coarse_out.wait()
    grad_out.wait()


def block(behind_lat, behind_lon, halo_lat, halo_lon, ident, args):
    (inputs, shift_lat, shift_lon, gain_attn, w_qkv, w_out, gain_merge, w_merge,
     cot_coarse, cot_skip) = args
    rows, cols, lev, feat = inputs.shape
    wide = (rows + halo_lat, cols + halo_lon, lev, feat)
    tokens = rows * cols * lev
    smem = pl.BlockSpec(memory_space=pltpu.SMEM)
    vmem = pl.BlockSpec(memory_space=pltpu.VMEM)
    anyw = pl.BlockSpec(memory_space=pl.ANY)
    hbm = pl.BlockSpec(memory_space=pltpu.HBM)
    return pl.pallas_call(
        functools.partial(kernel, behind_lat, behind_lon, halo_lat, halo_lon),
        out_shape=(
            jax.ShapeDtypeStruct(cot_coarse.shape, BF),
            jax.ShapeDtypeStruct(inputs.shape, BF),
            jax.ShapeDtypeStruct(inputs.shape, BF),
        ),
        in_specs=[smem, smem, vmem, vmem] + [hbm] * 6,
        out_specs=(anyw, anyw, anyw),
        scratch_shapes=[
            pltpu.VMEM(inputs.shape, BF),
            pltpu.VMEM(wide, BF),
            pltpu.VMEM(wide, BF),
            pltpu.VMEM(wide, BF),
            pltpu.VMEM(wide, BF),
            pltpu.VMEM(inputs.shape, BF),
            pltpu.VMEM(inputs.shape, BF),
            pltpu.VMEM(inputs.shape, BF),
            pltpu.VMEM(cot_coarse.shape, BF),
            pltpu.VMEM(cot_coarse.shape, BF),
            pltpu.VMEM(inputs.shape, BF),
            pltpu.VMEM(w_qkv.shape, BF),
            pltpu.VMEM(w_out.shape, BF),
            pltpu.VMEM(w_merge.shape, BF),
            pltpu.VMEM((TOK, 4 * FEAT), BF),
            pltpu.VMEM((TOK, 4 * FEAT), BF),
            pltpu.VMEM((tokens, FEAT), BF),
            pltpu.VMEM((tokens, FEAT), F32),
            pltpu.VMEM((tokens, 128), F32),
            pltpu.VMEM((tokens, 3 * FEAT), BF),
            pltpu.VMEM((tokens, FEAT), BF),
            pltpu.VMEM((4, PAIRS, 2 * TOK, TOK), BF),
            pltpu.VMEM((tokens, 3 * FEAT), BF),
            pltpu.VMEM((2, TOK, TOK), F32),
            pltpu.SemaphoreType.DMA((7,)),
            pltpu.SemaphoreType.DMA((3,)),
            pltpu.SemaphoreType.DMA((4, 3)),
            pltpu.SemaphoreType.DMA((4, 3)),
        ],
        compiler_params=pltpu.CompilerParams(
            collective_id=ident, has_side_effects=True, vmem_limit_bytes=48 * 2**20
        ),
    )(
        shift_lat, shift_lon, gain_attn.reshape(1, -1), gain_merge.reshape(1, -1),
        inputs, w_qkv, w_out, w_merge, cot_coarse, cot_skip,
    )


def local(*args):
    half_lat, half_lon = WLAT // 2, WLON // 2
    behind_lat = (args[1][0] > half_lat).astype(jnp.int32)
    behind_lon = (args[2][0] > half_lon).astype(jnp.int32)
    return lax.switch(
        2 * behind_lat + behind_lon,
        [
            functools.partial(block, bool(i // 2), bool(i % 2), half_lat, half_lon, i)
            for i in range(4)
        ],
        args,
    )


def solution(mesh):
    tile = P("lat", "lon", None, None)
    return jax.shard_map(
        local,
        mesh=mesh,
        in_specs=(tile, P(), P(), P(), P(), P(), P(), P(), tile, tile),
        out_specs=(tile, tile, tile),
        check_vma=False,
    )
```

```python
import jax
import jax.numpy as jnp
from jax import lax
from jax.experimental import pallas as pl
from jax.experimental.pallas import tpu as pltpu
from jax.sharding import PartitionSpec as P

WLAT = 6
WLON = 12
PAIRS = 4
TOK = 144
FEAT = 512
EPS = 1e-05
BF = jnp.bfloat16
F32 = jnp.float32
MESH = pl.DeviceIdType.MESH
VMEM = 62 * 2**20
HLAT = WLAT // 2
HLON = WLON // 2
AROUND = ((0, 1), (0, -1), (1, 0), (-1, 0), (1, 1), (-1, -1), (1, -1), (-1, 1))


def dot(a, b):
    return jnp.dot(a, b, preferred_element_type=F32)


def dot_t(a, b):
    return lax.dot_general(a, b, (((1,), (1,)), ((), ())), preferred_element_type=F32)


def t_dot(a, b):
    return lax.dot_general(a, b, (((0,), (0,)), ((), ())), preferred_element_type=F32)


def kernel(
    shift_lat_hbm, shift_lon_hbm, gain_attn_hbm, gain_merge_hbm,
    inputs, w_qkv_hbm, w_out_hbm, w_merge_hbm, cot_coarse_hbm, cot_skip_hbm,
    coarse_hbm, skip_hbm, grad_hbm,
    shift_lat, shift_lon, gain_attn, gain_merge,
    own, ext, bext, gext, rext, wins, gskip, skip, cot_skip, cot_coarse, coarse, out,
    w_qkv, w_out, w_merge,
    gm, merged, normed, norm, rstd, proj, mixed, soft, dproj, bias,
    local_sem, out_sem, send_sem, recv_sem,
):
    rows, cols = own.shape[0], own.shape[1]
    lat, lon = lax.axis_index("lat"), lax.axis_index("lon")
    nlat, nlon = lax.axis_size("lat"), lax.axis_size("lon")
    band = rows * nlat

    def device(step_lat, step_lon):
        return (lax.rem(lat + step_lat + nlat, nlat), lax.rem(lon + step_lon + nlon, nlon))

    def span(step, size, halo, base):
        if step == 0:
            return pl.ds(base, size), pl.ds(halo, size)
        if step > 0:
            return pl.ds(base + size - halo, halo), pl.ds(0, halo)
        return pl.ds(base, halo), pl.ds(halo + size, halo)

    def exchange(phase, source, base_r, base_c, target):
        copies = []
        for i, (dr, dc) in enumerate(AROUND):
            sr, tr = span(dr, rows, HLAT, base_r)
            sc, tc = span(dc, cols, HLON, base_c)
            copies.append(pltpu.make_async_remote_copy(
                src_ref=source.at[sr, sc],
                dst_ref=target.at[tr, tc],
                send_sem=send_sem.at[phase, i],
                recv_sem=recv_sem.at[phase, i],
                device_id=device(dr, dc),
                device_id_type=MESH,
            ))
        return copies

    inner = (pl.ds(HLAT, rows), pl.ds(HLON, cols))
    loads = [
        pltpu.make_async_copy(src, dst, local_sem.at[i])
        for i, (src, dst) in enumerate((
            (shift_lat_hbm, shift_lat),
            (shift_lon_hbm, shift_lon),
            (cot_coarse_hbm, cot_coarse),
            (w_merge_hbm, w_merge),
            (gain_attn_hbm, gain_attn),
            (inputs, own),
            (w_qkv_hbm, w_qkv),
            (w_out_hbm, w_out),
            (inputs, ext.at[inner]),
            (cot_skip_hbm, cot_skip),
            (gain_merge_hbm, gain_merge),
        ))
    ]
    barrier = pltpu.get_barrier_semaphore()
    for dr, dc in AROUND:
        pl.semaphore_signal(barrier, inc=1, device_id=device(dr, dc), device_id_type=MESH)
    for load in loads:
        load.start()
    pl.semaphore_wait(barrier, len(AROUND))
    first = exchange(0, inputs, 0, 0, ext)
    for copy in first:
        copy.start()

    loads[0].wait()
    loads[1].wait()
    s_lat, s_lon = shift_lat[0], shift_lon[0]
    back_lat = (s_lat > HLAT).astype(jnp.int32)
    back_lon = (s_lon > HLON).astype(jnp.int32)
    ahead_r = HLAT + s_lat - WLAT * back_lat
    ahead_c = HLON + s_lon - WLON * back_lon
    home_r = HLAT - s_lat + WLAT * back_lat
    home_c = HLON - s_lon + WLON * back_lon
    places = tuple(
        (jnp.abs(a - back_lat), jnp.abs(b - back_lon)) for a in range(2) for b in range(2)
    )

    def tile(slot):
        return pl.ds(slot * TOK, TOK)

    low = lax.broadcasted_iota(jnp.int32, (TOK, 128), 1) < 64
    zero = jnp.zeros((TOK, 128), BF)

    def both(x):
        return jnp.concatenate([jnp.where(low, x, zero), jnp.where(low, zero, x)], 0)

    def unite(x):
        return jnp.where(low, x[:TOK], x[TOK:])

    start = rows * lat + WLAT * (1 - 2 * back_lat)
    start = jnp.where(start < 0, start + band, start)
    edge = 2 * WLON * (band - s_lat - start)
    row_in = lax.broadcasted_iota(jnp.int32, (TOK, TOK), 0) >= edge
    col_in = lax.broadcasted_iota(jnp.int32, (TOK, TOK), 1) >= edge
    apart = jnp.where(row_in != col_in, F32(-1e30), F32(0.0))
    bias[...] = jnp.concatenate([apart, apart], 1)

    def norm_tokens(x, slot):
        mean = jnp.mean(x, -1, keepdims=True)
        centred = x - mean
        inv = lax.rsqrt(jnp.mean(centred * centred, -1, keepdims=True) + EPS)
        n = centred * inv
        norm[tile(slot)] = n
        rstd[tile(slot)] = jnp.broadcast_to(inv, (TOK, 128))
        normed[tile(slot)] = (n * gain_attn[...]).astype(BF)

    def attend(slot, p):
        at = p * 128
        rr = tile(slot)
        q = both(proj[rr, pl.ds(at, 128)] * BF(0.125))
        k = proj[rr, pl.ds(FEAT + at, 128)]
        v = proj[rr, pl.ds(2 * FEAT + at, 128)]
        scores = dot_t(k, q)
        if slot >= 2:
            scores = scores + bias[...]
        e = jnp.exp(scores - jnp.max(scores, 0, keepdims=True))
        w = (e * (1.0 / jnp.sum(e, 0, keepdims=True))).astype(BF)
        soft[slot, p] = w
        mixed[rr, pl.ds(at, 128)] = unite(t_dot(w, v)).astype(BF)

    def attend_back(slot, p):
        at = p * 128
        rr = tile(slot)
        q = both(proj[rr, pl.ds(at, 128)] * BF(0.125))
        k = proj[rr, pl.ds(FEAT + at, 128)]
        v = proj[rr, pl.ds(2 * FEAT + at, 128)]
        g = both(mixed[rr, pl.ds(at, 128)])
        w = soft[slot, p]
        dw = dot_t(v, g)
        wf = w.astype(F32)
        ds = (wf * (dw - jnp.sum(dw * wf, 0, keepdims=True))).astype(BF)
        dproj[rr, pl.ds(at, 128)] = (unite(t_dot(ds, k)) * 0.125).astype(BF)
        dproj[rr, pl.ds(FEAT + at, 128)] = dot(ds, q).astype(BF)
        dproj[rr, pl.ds(2 * FEAT + at, 128)] = dot(w, g).astype(BF)

    def pairs(step, slots):
        for slot in slots:
            for p in range(PAIRS):
                step(slot, p)

    def window(ref, slot):
        wi, wj = places[slot]
        x = ref[pl.ds(ahead_r + WLAT * wi, WLAT), pl.ds(ahead_c + WLON * wj, WLON)]
        return x.reshape(TOK, FEAT)

    def local_window(ref):
        return ref[pl.ds(s_lat, WLAT), pl.ds(s_lon, WLON)].reshape(TOK, FEAT)

    def place(ref):
        for a in range(2):
            for b in range(2):
                slot = 2 * jnp.abs(a - back_lat) + jnp.abs(b - back_lon)
                ref[pl.ds(HLAT + WLAT * a, WLAT), pl.ds(HLON + WLON * b, WLON)] = wins[slot]

    def run_forward(slots, fetch):
        lo, n = slots[0] * TOK, len(slots) * TOK
        for slot in slots:
            norm_tokens(fetch(slot).astype(F32), slot)
        proj[pl.ds(lo, n)] = dot(normed[pl.ds(lo, n)], w_qkv[...]).astype(BF)
        pairs(attend, slots)
        branch = dot(mixed[pl.ds(lo, n)], w_out[...]).astype(BF)
        for i, slot in enumerate(slots):
            wins[slot] = branch[i * TOK:(i + 1) * TOK].reshape(WLAT, WLON, 2, FEAT)

    def run_backward(slots, fetch):
        lo, n = slots[0] * TOK, len(slots) * TOK
        for slot in slots:
            normed[tile(slot)] = fetch(slot)
        mixed[pl.ds(lo, n)] = dot_t(normed[pl.ds(lo, n)], w_out[...]).astype(BF)
        pairs(attend_back, slots)
        dnormed = dot_t(dproj[pl.ds(lo, n)], w_qkv[...]).astype(BF)
        for i, slot in enumerate(slots):
            d = dnormed[i * TOK:(i + 1) * TOK].astype(F32) * gain_attn[...]
            nn = norm[tile(slot)]
            inv = rstd[tile(slot)][:, :1]
            dx = inv * (
                d - jnp.mean(d, -1, keepdims=True) - nn * jnp.mean(d * nn, -1, keepdims=True)
            )
            wins[slot] = dx.astype(BF).reshape(WLAT, WLON, 2, FEAT)

    loads[2].wait()
    loads[3].wait()
    gm[...] = dot_t(cot_coarse.reshape(TOK, 2 * FEAT)[...], w_merge[...]).astype(BF)
    for load in loads[4:8]:
        load.wait()
    run_forward((0,), lambda slot: local_window(own))
    loads[8].wait()
    for copy in first:
        copy.wait_recv()
    run_forward((1, 2, 3), lambda slot: window(ext, slot))
    place(bext)
    second = exchange(1, bext, HLAT, HLON, bext)
    for copy in second:
        copy.start()
    loads[9].wait()
    loads[10].wait()
    for copy in second:
        copy.wait_recv()

    skip[...] = (
        own[...].astype(F32) + bext[pl.ds(home_r, rows), pl.ds(home_c, cols)].astype(F32)
    ).astype(BF)
    skip_out = pltpu.make_async_copy(skip, skip_hbm, out_sem.at[0])
    skip_out.start()

    patches = (rows // 2, 2, cols // 2, 2, 2, FEAT)
    quarters = [(a, b) for a in range(2) for b in range(2)]

    def quarter(ref, a, b):
        return ref.reshape(*patches)[:, a, :, b].reshape(TOK, FEAT)

    parts = [quarter(skip, a, b).astype(F32) for a, b in quarters]
    width = 4 * FEAT
    mean = sum(jnp.sum(x, -1, keepdims=True) for x in parts) / width
    parts = [x - mean for x in parts]
    inv = lax.rsqrt(sum(jnp.sum(x * x, -1, keepdims=True) for x in parts) / width + EPS)
    parts = [x * inv for x in parts]
    grads = []
    for i, x in enumerate(parts):
        gain = gain_merge[:, pl.ds(i * FEAT, FEAT)]
        merged[:, pl.ds(i * FEAT, FEAT)] = (x * gain).astype(BF)
        grads.append(gm[:, pl.ds(i * FEAT, FEAT)].astype(F32) * gain)
    mean_g = sum(jnp.sum(g, -1, keepdims=True) for g in grads) / width
    mean_gx = sum(jnp.sum(g * x, -1, keepdims=True) for g, x in zip(grads, parts)) / width
    for (a, b), g, x in zip(quarters, grads, parts):
        d = (inv * (g - mean_g - x * mean_gx)).astype(BF) + quarter(cot_skip, a, b)
        gskip.reshape(*patches)[:, a, :, b] = d.reshape(rows // 2, cols // 2, 2, FEAT)
    gext[inner] = gskip[...]
    third = exchange(2, gext, HLAT, HLON, gext)
    for copy in third:
        copy.start()

    coarse.reshape(TOK, 2 * FEAT)[...] = dot(merged[...], w_merge[...]).astype(BF)
    coarse_out = pltpu.make_async_copy(coarse, coarse_hbm, out_sem.at[1])
    coarse_out.start()
    run_backward((0,), lambda slot: local_window(gskip))
    for copy in third:
        copy.wait_recv()
    run_backward((1, 2, 3), lambda slot: window(gext, slot))
    place(rext)
    fourth = exchange(3, rext, HLAT, HLON, rext)
    for copy in fourth:
        copy.start()
    for copy in fourth:
        copy.wait_recv()
    out[...] = gskip[...] + rext[pl.ds(home_r, rows), pl.ds(home_c, cols)]
    grad_out = pltpu.make_async_copy(out, grad_hbm, out_sem.at[2])
    grad_out.start()
    for copy in first + second + third + fourth:
        copy.wait_send()
    skip_out.wait()
    coarse_out.wait()
    grad_out.wait()


def local(
    inputs, shift_lat, shift_lon, gain_attn, w_qkv, w_out, gain_merge, w_merge, cot_coarse, cot_skip
):
    rows, cols, lev, feat = inputs.shape
    wide = (rows + 2 * HLAT, cols + 2 * HLON, lev, feat)
    tokens = rows * cols * lev
    hbm = pl.BlockSpec(memory_space=pltpu.HBM)
    anyw = pl.BlockSpec(memory_space=pl.ANY)
    return pl.pallas_call(
        kernel,
        out_shape=(
            jax.ShapeDtypeStruct(cot_coarse.shape, BF),
            jax.ShapeDtypeStruct(inputs.shape, BF),
            jax.ShapeDtypeStruct(inputs.shape, BF),
        ),
        in_specs=[hbm] * 10,
        out_specs=(anyw, anyw, anyw),
        scratch_shapes=[
            pltpu.SMEM((1,), jnp.int32),
            pltpu.SMEM((1,), jnp.int32),
            pltpu.VMEM((1, feat), F32),
            pltpu.VMEM((1, 4 * feat), F32),
            pltpu.VMEM(inputs.shape, BF),
            pltpu.VMEM(wide, BF),
            pltpu.VMEM(wide, BF),
            pltpu.VMEM(wide, BF),
            pltpu.VMEM(wide, BF),
            pltpu.VMEM((4, WLAT, WLON, lev, feat), BF),
            pltpu.VMEM(inputs.shape, BF),
            pltpu.VMEM(inputs.shape, BF),
            pltpu.VMEM(inputs.shape, BF),
            pltpu.VMEM(cot_coarse.shape, BF),
            pltpu.VMEM(cot_coarse.shape, BF),
            pltpu.VMEM(inputs.shape, BF),
            pltpu.VMEM(w_qkv.shape, BF),
            pltpu.VMEM(w_out.shape, BF),
            pltpu.VMEM(w_merge.shape, BF),
            pltpu.VMEM((TOK, 4 * FEAT), BF),
            pltpu.VMEM((TOK, 4 * FEAT), BF),
            pltpu.VMEM((tokens, FEAT), BF),
            pltpu.VMEM((tokens, FEAT), F32),
            pltpu.VMEM((tokens, 128), F32),
            pltpu.VMEM((tokens, 3 * FEAT), BF),
            pltpu.VMEM((tokens, FEAT), BF),
            pltpu.VMEM((4, PAIRS, TOK, 2 * TOK), BF),
            pltpu.VMEM((tokens, 3 * FEAT), BF),
            pltpu.VMEM((TOK, 2 * TOK), F32),
            pltpu.SemaphoreType.DMA((11,)),
            pltpu.SemaphoreType.DMA((3,)),
            pltpu.SemaphoreType.DMA((4, len(AROUND))),
            pltpu.SemaphoreType.DMA((4, len(AROUND))),
        ],
        compiler_params=pltpu.CompilerParams(
            collective_id=0, has_side_effects=True, vmem_limit_bytes=VMEM
        ),
    )(
        shift_lat, shift_lon, gain_attn.reshape(1, -1), gain_merge.reshape(1, -1),
        inputs, w_qkv, w_out, w_merge, cot_coarse, cot_skip,
    )


def solution(mesh):
    tile = P("lat", "lon", None, None)
    return jax.shard_map(
        local,
        mesh=mesh,
        in_specs=(tile, P(), P(), P(), P(), P(), P(), P(), tile, tile),
        out_specs=(tile, tile, tile),
        check_vma=False,
    )
```

```python
import functools

import jax
import jax.numpy as jnp
from jax import lax
from jax.experimental import pallas as pl
from jax.experimental.pallas import tpu as pltpu
from jax.sharding import PartitionSpec as P

WLAT = 6
WLON = 12
PAIRS = 4
TOK = 144
FEAT = 512
EPS = 1e-05
BF = jnp.bfloat16
F32 = jnp.float32
MESH = pl.DeviceIdType.MESH
VMEM = 48 * 2**20
STRIPS = 3


def dot(a, b):
    return jnp.dot(a, b, preferred_element_type=F32)


def dot_t(a, b):
    return lax.dot_general(a, b, (((1,), (1,)), ((), ())), preferred_element_type=F32)


def t_dot(a, b):
    return lax.dot_general(a, b, (((0,), (0,)), ((), ())), preferred_element_type=F32)


def kernel(
    behind_lat, behind_lon, halo_lat, halo_lon,
    shift_lat, shift_lon, gain_attn_hbm, gain_merge_hbm,
    inputs, w_qkv_hbm, w_out_hbm, w_merge_hbm, cot_coarse_hbm, cot_skip_hbm,
    coarse_hbm, skip_hbm, grad_hbm,
    gain_attn, gain_merge,
    own, ext, bext, gext, rext, gskip, skip, cot_skip, cot_coarse, coarse, out,
    w_qkv, w_out, w_merge,
    gm, merged, token, norm, rstd, proj, mixed, soft, dproj, bias,
    local_sem, out_sem, send_sem, recv_sem,
):
    rows, cols = own.shape[0], own.shape[1]
    lat, lon = lax.axis_index("lat"), lax.axis_index("lon")
    nlat, nlon = lax.axis_size("lat"), lax.axis_size("lon")
    band = rows * nlat
    li, lj = int(behind_lat), int(behind_lon)

    def device(step_lat, step_lon):
        return (lax.rem(lat + step_lat + nlat, nlat), lax.rem(lon + step_lon + nlon, nlon))

    dlat, dlon = 1 - 2 * li, 1 - 2 * lj
    steps = ((dlat, 0), (0, dlon), (dlat, dlon))
    own_r, own_c = li * halo_lat, lj * halo_lon
    halo_r, halo_c = (1 - li) * rows, (1 - lj) * cols
    back_r, back_c = (1 - li) * halo_lat, (1 - lj) * halo_lon
    bhalo_r, bhalo_c = li * rows, lj * cols
    edge_r, edge_c = li * (rows - halo_lat), lj * (cols - halo_lon)
    bedge_r, bedge_c = (1 - li) * (rows - halo_lat), (1 - lj) * (cols - halo_lon)

    def send(phase, i, source, src, target, dst, step_lat, step_lon):
        (r, c, n, m), (tr, tc) = src, dst
        return pltpu.make_async_remote_copy(
            src_ref=source.at[pl.ds(r, n), pl.ds(c, m)],
            dst_ref=target.at[pl.ds(tr, n), pl.ds(tc, m)],
            send_sem=send_sem.at[phase, i],
            recv_sem=recv_sem.at[phase, i],
            device_id=device(step_lat, step_lon),
            device_id_type=MESH,
        )

    def ahead(phase, source, r, c, target):
        er, ec = r + edge_r, c + edge_c
        return (
            send(phase, 0, source, (er, c, halo_lat, cols), target, (halo_r, own_c), -dlat, 0),
            send(phase, 1, source, (r, ec, rows, halo_lon), target, (own_r, halo_c), 0, -dlon),
            send(phase, 2, source, (er, ec, halo_lat, halo_lon), target, (halo_r, halo_c), -dlat, -dlon),
        )

    def back(phase, ref):
        er, ec = back_r + bedge_r, back_c + bedge_c
        far_r, far_c = back_r + (1 - li) * WLAT, back_c + (1 - lj) * WLON
        near_r, near_c = back_r + li * WLAT, back_c + lj * WLON
        return (
            send(phase, 0, ref, (er, ec, halo_lat, halo_lon), ref, (bhalo_r, bhalo_c), dlat, dlon),
            send(phase, 1, ref, (far_r, ec, WLAT, halo_lon), ref, (far_r, bhalo_c), 0, dlon),
            send(phase, 2, ref, (er, far_c, halo_lat, WLON), ref, (bhalo_r, far_c), dlat, 0),
            send(phase, 3, ref, (near_r, ec, WLAT, halo_lon), ref, (near_r, bhalo_c), 0, dlon),
            send(phase, 4, ref, (er, near_c, halo_lat, WLON), ref, (bhalo_r, near_c), dlat, 0),
        )

    inner = (pl.ds(own_r, rows), pl.ds(own_c, cols))
    loads = [
        pltpu.make_async_copy(src, dst, local_sem.at[i])
        for i, (src, dst) in enumerate((
            (cot_coarse_hbm, cot_coarse),
            (w_merge_hbm, w_merge),
            (gain_attn_hbm, gain_attn),
            (inputs, own),
            (w_qkv_hbm, w_qkv),
            (w_out_hbm, w_out),
            (inputs, ext.at[inner]),
            (cot_skip_hbm, cot_skip),
            (gain_merge_hbm, gain_merge),
        ))
    ]
    barrier = pltpu.get_barrier_semaphore()
    for sr, sc in steps:
        pl.semaphore_signal(barrier, inc=1, device_id=device(sr, sc), device_id_type=MESH)
        pl.semaphore_signal(barrier, inc=1, device_id=device(-sr, -sc), device_id_type=MESH)
    for load in loads:
        load.start()
    pl.semaphore_wait(barrier, 6)
    first = ahead(0, inputs, 0, 0, ext)
    for copy in first:
        copy.start()
    second = back(1, bext)
    third = ahead(2, gext, own_r, own_c, gext)
    fourth = back(3, rext)

    s_lat, s_lon = shift_lat[0], shift_lon[0]
    t_lat = jnp.clip(s_lat - li * (WLAT - halo_lat), 0, halo_lat)
    t_lon = jnp.clip(s_lon - lj * (WLON - halo_lon), 0, halo_lon)

    low = lax.broadcasted_iota(jnp.int32, (TOK, 128), 1) < 64
    zero = jnp.zeros((TOK, 128), BF)

    def both(x):
        return jnp.concatenate([jnp.where(low, x, zero), jnp.where(low, zero, x)], 0)

    def unite(x):
        return jnp.where(low, x[:TOK], x[TOK:])

    start = lax.rem(rows * lat + WLAT * (1 - 2 * li) + band, band)
    edge = 2 * WLON * (band - s_lat - start)
    row_in = lax.broadcasted_iota(jnp.int32, (TOK, TOK), 0) >= edge
    col_in = lax.broadcasted_iota(jnp.int32, (TOK, TOK), 1) >= edge
    apart = jnp.where(row_in != col_in, F32(-1e30), F32(0.0))
    bias[0] = jnp.zeros((TOK, 2 * TOK), F32)
    bias[1] = jnp.concatenate([apart, apart], 1)

    def attend(i, across, p):
        at = p * 128
        q = both(proj[i, :, pl.ds(at, 128)] * BF(0.125))
        k = proj[i, :, pl.ds(FEAT + at, 128)]
        v = proj[i, :, pl.ds(2 * FEAT + at, 128)]
        scores = dot_t(k, q) + bias[across]
        e = jnp.exp(scores - jnp.max(scores, 0, keepdims=True))
        w = (e * (1.0 / jnp.sum(e, 0, keepdims=True))).astype(BF)
        soft[i, p] = w
        mixed[:, pl.ds(at, 128)] = unite(t_dot(w, v)).astype(BF)

    def attend_back(i, p):
        at = p * 128
        q = both(proj[i, :, pl.ds(at, 128)] * BF(0.125))
        k = proj[i, :, pl.ds(FEAT + at, 128)]
        v = proj[i, :, pl.ds(2 * FEAT + at, 128)]
        g = both(mixed[:, pl.ds(at, 128)])
        w = soft[i, p]
        dw = dot_t(v, g)
        wf = w.astype(F32)
        ds = (wf * (dw - jnp.sum(dw * wf, 0, keepdims=True))).astype(BF)
        dproj[:, pl.ds(at, 128)] = (unite(t_dot(ds, k)) * 0.125).astype(BF)
        dproj[:, pl.ds(FEAT + at, 128)] = dot(ds, q).astype(BF)
        dproj[:, pl.ds(2 * FEAT + at, 128)] = dot(w, g).astype(BF)

    def windows(forward, ready, local_ref, wide_ref, result_ref, copies):
        def step(i, carry):
            across_lat, across_lon = i % 2, ((i + 1) // 2) % 2
            wr = WLAT * (li + dlat * across_lat)
            wc = WLON * (lj + dlon * across_lon)

            @pl.when(i == 0)
            def _():
                x = local_ref[pl.ds(s_lat, WLAT), pl.ds(s_lon, WLON)]
                token[...] = x.reshape(TOK, FEAT)

            @pl.when(i == 1)
            def _():
                for copy in ready:
                    copy.wait_recv()

            @pl.when(i > 0)
            def _():
                x = wide_ref[pl.ds(t_lat + wr, WLAT), pl.ds(t_lon + wc, WLON)]
                token[...] = x.reshape(TOK, FEAT)

            if forward:
                x = token[...].astype(F32)
                mean = jnp.mean(x, -1, keepdims=True)
                x = x - mean
                inv = lax.rsqrt(jnp.mean(x * x, -1, keepdims=True) + EPS)
                x = x * inv
                norm[i] = x
                rstd[i] = jnp.broadcast_to(inv, (TOK, 128))
                proj[i] = dot((x * gain_attn[...]).astype(BF), w_qkv[...]).astype(BF)
                for p in range(PAIRS):
                    attend(i, across_lat, p)
                result = dot(mixed[...], w_out[...]).astype(BF)
            else:
                mixed[...] = dot_t(token[...], w_out[...]).astype(BF)
                for p in range(PAIRS):
                    attend_back(i, p)
                d = dot_t(dproj[...], w_qkv[...]).astype(BF).astype(F32) * gain_attn[...]
                nn = norm[i]
                inv = rstd[i][:, :1]
                result = (inv * (
                    d - jnp.mean(d, -1, keepdims=True) - nn * jnp.mean(d * nn, -1, keepdims=True)
                )).astype(BF)
            result_ref[pl.ds(back_r + wr, WLAT), pl.ds(back_c + wc, WLON)] = result.reshape(
                WLAT, WLON, 2, FEAT
            )
            for turn, part in ((1, copies[:3]), (2, copies[3:4]), (3, copies[4:])):
                @pl.when(i == turn)
                def _(part=part):
                    for copy in part:
                        copy.start()
            return carry

        lax.fori_loop(0, 4, step, 0)

    loads[0].wait()
    loads[1].wait()
    strip = TOK // STRIPS

    def quarter_back(j, carry):
        at = pl.multiple_of(j * FEAT, FEAT)
        x = cot_coarse.reshape(TOK, 2 * FEAT)[...]
        y = dot_t(x, w_merge[pl.ds(at, FEAT), :]).astype(BF)
        gm[:, :, pl.ds(at, FEAT)] = y.reshape(STRIPS, strip, FEAT)
        return carry

    lax.fori_loop(0, 4, quarter_back, 0)
    for load in loads[2:7]:
        load.wait()
    windows(True, first, own, ext, bext, second)
    loads[7].wait()
    loads[8].wait()
    for copy in second:
        copy.wait_recv()

    start_r, start_c = halo_lat - t_lat, halo_lon - t_lon
    high = rows // STRIPS
    width = 4 * FEAT
    patches = (rows // 2, 2, cols // 2, 2, 2, FEAT)
    quarters = [(a, b) for a in range(2) for b in range(2)]

    def merge(turn, carry):
        j = (STRIPS - 1 - turn) if li else turn
        mine = pl.ds(high * j, high)
        skip[mine] = (
            own[mine].astype(F32)
            + bext[pl.ds(start_r + high * j, high), pl.ds(start_c, cols)].astype(F32)
        ).astype(BF)

        def quarter(ref, a, b):
            return ref.reshape(*patches)[pl.ds(high // 2 * j, high // 2), a, :, b].reshape(strip, FEAT)

        parts = [quarter(skip, a, b).astype(F32) for a, b in quarters]
        mean = sum(jnp.sum(x, -1, keepdims=True) for x in parts) / width
        parts = [x - mean for x in parts]
        inv = lax.rsqrt(sum(jnp.sum(x * x, -1, keepdims=True) for x in parts) / width + EPS)
        parts = [x * inv for x in parts]
        grads = []
        for i, x in enumerate(parts):
            gain = gain_merge[:, pl.ds(i * FEAT, FEAT)]
            merged[j, :, pl.ds(i * FEAT, FEAT)] = (x * gain).astype(BF)
            grads.append(gm[j, :, pl.ds(i * FEAT, FEAT)].astype(F32) * gain)
        mean_g = sum(jnp.sum(g, -1, keepdims=True) for g in grads) / width
        mean_gx = sum(jnp.sum(g * x, -1, keepdims=True) for g, x in zip(grads, parts)) / width
        for (a, b), g, x in zip(quarters, grads, parts):
            d = (inv * (g - mean_g - x * mean_gx)).astype(BF) + quarter(cot_skip, a, b)
            gskip.reshape(*patches)[pl.ds(high // 2 * j, high // 2), a, :, b] = d.reshape(
                high // 2, cols // 2, 2, FEAT
            )
        gext[pl.ds(own_r + high * j, high), pl.ds(own_c, cols)] = gskip[mine]

        @pl.when(turn == 0)
        def _():
            third[0].start()
            third[2].start()

        return carry

    lax.fori_loop(0, STRIPS, merge, 0)
    third[1].start()
    skip_out = pltpu.make_async_copy(skip, skip_hbm, out_sem.at[0])
    skip_out.start()
    windows(False, third, gskip, gext, rext, fourth)

    def coarse_part(j, carry):
        at = pl.multiple_of(j * FEAT, FEAT)
        x = merged.reshape(TOK, width)[...]
        coarse.reshape(TOK, 2 * FEAT)[:, pl.ds(at, FEAT)] = dot(
            x, w_merge[:, pl.ds(at, FEAT)]
        ).astype(BF)
        return carry

    lax.fori_loop(0, 2, coarse_part, 0)
    coarse_out = pltpu.make_async_copy(coarse, coarse_hbm, out_sem.at[1])
    coarse_out.start()
    for copy in fourth:
        copy.wait_recv()

    def finish(j, carry):
        mine = pl.ds(high * j, high)
        out[mine] = gskip[mine] + rext[pl.ds(start_r + high * j, high), pl.ds(start_c, cols)]
        return carry

    lax.fori_loop(0, STRIPS, finish, 0)
    grad_out = pltpu.make_async_copy(out, grad_hbm, out_sem.at[2])
    grad_out.start()
    for copy in first + second + third + fourth:
        copy.wait_send()
    skip_out.wait()
    coarse_out.wait()
    grad_out.wait()


def block(behind_lat, behind_lon, halo_lat, halo_lon, ident, args):
    (inputs, shift_lat, shift_lon, gain_attn, w_qkv, w_out, gain_merge, w_merge,
     cot_coarse, cot_skip) = args
    rows, cols, lev, feat = inputs.shape
    wide = (rows + halo_lat, cols + halo_lon, lev, feat)
    smem = pl.BlockSpec(memory_space=pltpu.SMEM)
    hbm = pl.BlockSpec(memory_space=pltpu.HBM)
    anyw = pl.BlockSpec(memory_space=pl.ANY)
    tile, coarse = pltpu.VMEM(inputs.shape, BF), pltpu.VMEM(cot_coarse.shape, BF)
    return pl.pallas_call(
        functools.partial(kernel, behind_lat, behind_lon, halo_lat, halo_lon),
        out_shape=(
            jax.ShapeDtypeStruct(cot_coarse.shape, BF),
            jax.ShapeDtypeStruct(inputs.shape, BF),
            jax.ShapeDtypeStruct(inputs.shape, BF),
        ),
        in_specs=[smem, smem] + [hbm] * 8,
        out_specs=(anyw, anyw, anyw),
        scratch_shapes=[
            pltpu.VMEM((1, feat), F32),
            pltpu.VMEM((1, 4 * feat), F32),
            tile,
            pltpu.VMEM(wide, BF),
            pltpu.VMEM(wide, BF),
            pltpu.VMEM(wide, BF),
            pltpu.VMEM(wide, BF),
            tile, tile, tile, coarse, coarse, tile,
            pltpu.VMEM(w_qkv.shape, BF),
            pltpu.VMEM(w_out.shape, BF),
            pltpu.VMEM(w_merge.shape, BF),
            pltpu.VMEM((STRIPS, TOK // STRIPS, 4 * FEAT), BF),
            pltpu.VMEM((STRIPS, TOK // STRIPS, 4 * FEAT), BF),
            pltpu.VMEM((TOK, FEAT), BF),
            pltpu.VMEM((4, TOK, FEAT), F32),
            pltpu.VMEM((4, TOK, 128), F32),
            pltpu.VMEM((4, TOK, 3 * FEAT), BF),
            pltpu.VMEM((TOK, FEAT), BF),
            pltpu.VMEM((4, PAIRS, TOK, 2 * TOK), BF),
            pltpu.VMEM((TOK, 3 * FEAT), BF),
            pltpu.VMEM((2, TOK, 2 * TOK), F32),
            pltpu.SemaphoreType.DMA((9,)),
            pltpu.SemaphoreType.DMA((3,)),
            pltpu.SemaphoreType.DMA((4, 5)),
            pltpu.SemaphoreType.DMA((4, 5)),
        ],
        compiler_params=pltpu.CompilerParams(
            collective_id=ident, has_side_effects=True, vmem_limit_bytes=VMEM
        ),
    )(
        shift_lat, shift_lon, gain_attn.reshape(1, -1), gain_merge.reshape(1, -1),
        inputs, w_qkv, w_out, w_merge, cot_coarse, cot_skip,
    )


def local(*args):
    half_lat, half_lon = WLAT // 2, WLON // 2
    behind_lat = (args[1][0] > half_lat).astype(jnp.int32)
    behind_lon = (args[2][0] > half_lon).astype(jnp.int32)
    return lax.switch(
        2 * behind_lat + behind_lon,
        [
            functools.partial(block, bool(i // 2), bool(i % 2), half_lat, half_lon, i)
            for i in range(4)
        ],
        args,
    )


def solution(mesh):
    tile = P("lat", "lon", None, None)
    return jax.shard_map(
        local,
        mesh=mesh,
        in_specs=(tile, P(), P(), P(), P(), P(), P(), P(), tile, tile),
        out_specs=(tile, tile, tile),
        check_vma=False,
    )
```

```python
import functools

import jax
import jax.numpy as jnp
from jax import lax
from jax.experimental import pallas as pl
from jax.experimental.pallas import tpu as pltpu
from jax.sharding import PartitionSpec as P

WLAT = 6
WLON = 12
PAIRS = 4
TOK = 144
FEAT = 512
EPS = 1e-05
BF = jnp.bfloat16
F32 = jnp.float32
MESH = pl.DeviceIdType.MESH
VMEM = 48 * 2**20
STRIPS = 3


def dot(a, b):
    return jnp.dot(a, b, preferred_element_type=F32)


def dot_t(a, b):
    return lax.dot_general(a, b, (((1,), (1,)), ((), ())), preferred_element_type=F32)


def t_dot(a, b):
    return lax.dot_general(a, b, (((0,), (0,)), ((), ())), preferred_element_type=F32)


def kernel(
    behind_lat, behind_lon, halo_lat, halo_lon,
    shift_lat, shift_lon, gain_attn_hbm, gain_merge_hbm,
    inputs, w_qkv_hbm, w_out_hbm, w_merge_hbm, cot_coarse_hbm, cot_skip_hbm,
    coarse_hbm, skip_hbm, grad_hbm,
    gain_attn, gain_merge,
    own, xtall, btall, gtall, ext, bext, gext, rext, gskip, skip, cot_skip, cot_coarse, coarse, out,
    w_qkv, w_out, w_merge,
    gm, merged, token, norm, rstd, proj, mixed, soft, dproj, bias,
    local_sem, out_sem, send_sem, recv_sem,
):
    rows, cols = own.shape[0], own.shape[1]
    lat, lon = lax.axis_index("lat"), lax.axis_index("lon")
    nlat, nlon = lax.axis_size("lat"), lax.axis_size("lon")
    band = rows * nlat
    li, lj = int(behind_lat), int(behind_lon)

    def device(step_lat, step_lon):
        return (lax.rem(lat + step_lat + nlat, nlat), lax.rem(lon + step_lon + nlon, nlon))

    dlat, dlon = 1 - 2 * li, 1 - 2 * lj
    steps = ((dlat, 0), (0, dlon), (dlat, dlon))
    own_r, own_c = li * halo_lat, lj * halo_lon
    halo_r, halo_c = (1 - li) * rows, (1 - lj) * cols
    back_r, back_c = (1 - li) * halo_lat, (1 - lj) * halo_lon
    bhalo_r, bhalo_c = li * rows, lj * cols
    edge_r, edge_c = li * (rows - halo_lat), lj * (cols - halo_lon)
    bedge_r, bedge_c = (1 - li) * (rows - halo_lat), (1 - lj) * (cols - halo_lon)

    def send(phase, i, source, src, target, dst, step_lat, step_lon):
        (r, c, n, m), (tr, tc) = src, dst
        return pltpu.make_async_remote_copy(
            src_ref=source.at[pl.ds(r, n), pl.ds(c, m)],
            dst_ref=target.at[pl.ds(tr, n), pl.ds(tc, m)],
            send_sem=send_sem.at[phase, i],
            recv_sem=recv_sem.at[phase, i],
            device_id=device(step_lat, step_lon),
            device_id_type=MESH,
        )

    def ahead(phase, source, r, c, tall, wide):
        er, ec = r + edge_r, c + edge_c
        return (
            send(phase, 0, source, (er, c, halo_lat, cols), tall, (halo_r, 0), -dlat, 0),
            send(phase, 1, source, (r, ec, rows, halo_lon), wide, (own_r, halo_c), 0, -dlon),
            send(phase, 2, source, (er, ec, halo_lat, halo_lon), wide, (halo_r, halo_c), -dlat, -dlon),
        )

    def back(phase, tall, at_c, wide):
        er, ec = back_r + bedge_r, back_c + bedge_c
        far_r, near_r = back_r + (1 - li) * WLAT, back_r + li * WLAT
        far_c, near_c = at_c + (1 - lj) * WLON, at_c + lj * WLON
        return (
            send(phase, 0, tall, (er, near_c, halo_lat, WLON), tall, (bhalo_r, near_c), dlat, 0),
            send(phase, 1, wide, (er, ec, halo_lat, halo_lon), wide, (bhalo_r, bhalo_c), dlat, dlon),
            send(phase, 2, wide, (far_r, ec, WLAT, halo_lon), wide, (far_r, bhalo_c), 0, dlon),
            send(phase, 3, tall, (er, far_c, halo_lat, WLON), tall, (bhalo_r, far_c), dlat, 0),
            send(phase, 4, wide, (near_r, ec, WLAT, halo_lon), wide, (near_r, bhalo_c), 0, dlon),
        )

    inner = (pl.ds(own_r, rows), pl.ds(own_c, cols))
    loads = [
        pltpu.make_async_copy(src, dst, local_sem.at[i])
        for i, (src, dst) in enumerate((
            (cot_coarse_hbm, cot_coarse),
            (w_merge_hbm, w_merge),
            (gain_attn_hbm, gain_attn),
            (inputs, own),
            (w_qkv_hbm, w_qkv),
            (w_out_hbm, w_out),
            (inputs, xtall.at[pl.ds(own_r, rows)]),
            (inputs, ext.at[inner]),
            (cot_skip_hbm, cot_skip),
            (gain_merge_hbm, gain_merge),
        ))
    ]
    barrier = pltpu.get_barrier_semaphore()
    for sr, sc in steps:
        pl.semaphore_signal(barrier, inc=1, device_id=device(sr, sc), device_id_type=MESH)
        pl.semaphore_signal(barrier, inc=1, device_id=device(-sr, -sc), device_id_type=MESH)
    for load in loads:
        load.start()
    pl.semaphore_wait(barrier, 6)
    first = ahead(0, inputs, 0, 0, xtall, ext)
    for turn in (1, 2, 0):
        first[turn].start()
    second = back(1, btall, 0, bext)
    third = ahead(2, gskip, 0, 0, gtall, gext)
    fourth = back(3, rext, back_c, rext)

    s_lat, s_lon = shift_lat[0], shift_lon[0]
    t_lat = jnp.clip(s_lat - li * (WLAT - halo_lat), 0, halo_lat)
    t_lon = jnp.clip(s_lon - lj * (WLON - halo_lon), 0, halo_lon)

    low = lax.broadcasted_iota(jnp.int32, (TOK, 128), 1) < 64
    zero = jnp.zeros((TOK, 128), BF)

    def both(x):
        return jnp.concatenate([jnp.where(low, x, zero), jnp.where(low, zero, x)], 0)

    def unite(x):
        return jnp.where(low, x[:TOK], x[TOK:])

    start = lax.rem(rows * lat + WLAT * (1 - 2 * li) + band, band)
    edge = 2 * WLON * (band - s_lat - start)
    row_in = lax.broadcasted_iota(jnp.int32, (TOK, TOK), 0) >= edge
    col_in = lax.broadcasted_iota(jnp.int32, (TOK, TOK), 1) >= edge
    apart = jnp.where(row_in != col_in, F32(-1e30), F32(0.0))
    bias[0] = jnp.zeros((TOK, 2 * TOK), F32)
    bias[1] = jnp.concatenate([apart, apart], 1)

    def attend(i, across, p):
        at = p * 128
        q = both(proj[i, :, pl.ds(at, 128)] * BF(0.125))
        k = proj[i, :, pl.ds(FEAT + at, 128)]
        v = proj[i, :, pl.ds(2 * FEAT + at, 128)]
        scores = dot_t(k, q) + bias[across]
        e = jnp.exp(scores - jnp.max(scores, 0, keepdims=True))
        w = (e * (1.0 / jnp.sum(e, 0, keepdims=True))).astype(BF)
        soft[i, p] = w
        mixed[:, pl.ds(at, 128)] = unite(t_dot(w, v)).astype(BF)

    def attend_back(i, p):
        at = p * 128
        q = both(proj[i, :, pl.ds(at, 128)] * BF(0.125))
        k = proj[i, :, pl.ds(FEAT + at, 128)]
        v = proj[i, :, pl.ds(2 * FEAT + at, 128)]
        g = both(mixed[:, pl.ds(at, 128)])
        w = soft[i, p]
        dw = dot_t(v, g)
        wf = w.astype(F32)
        ds = (wf * (dw - jnp.sum(dw * wf, 0, keepdims=True))).astype(BF)
        dproj[:, pl.ds(at, 128)] = (unite(t_dot(ds, k)) * 0.125).astype(BF)
        dproj[:, pl.ds(FEAT + at, 128)] = dot(ds, q).astype(BF)
        dproj[:, pl.ds(2 * FEAT + at, 128)] = dot(w, g).astype(BF)

    def windows(forward, ready, local_ref, tall, wide, results, copies):
        def step(i, carry):
            across_lat, across_lon = ((i + 1) // 2) % 2, i // 2
            wr = WLAT * (li + dlat * across_lat)
            wc = WLON * (lj + dlon * across_lon)

            @pl.when(i == 0)
            def _():
                x = local_ref[pl.ds(s_lat, WLAT), pl.ds(s_lon, WLON)]
                token[...] = x.reshape(TOK, FEAT)

            @pl.when(i == 1)
            def _():
                ready[0].wait_recv()
                x = tall[pl.ds(t_lat + wr, WLAT), pl.ds(s_lon, WLON)]
                token[...] = x.reshape(TOK, FEAT)

            @pl.when(i == 2)
            def _():
                ready[1].wait_recv()
                ready[2].wait_recv()
                wide[pl.ds(halo_r, halo_lat), pl.ds(own_c, cols)] = tall[pl.ds(halo_r, halo_lat)]

            @pl.when(i >= 2)
            def _():
                x = wide[pl.ds(t_lat + wr, WLAT), pl.ds(t_lon + wc, WLON)]
                token[...] = x.reshape(TOK, FEAT)

            if forward:
                x = token[...].astype(F32)
                mean = jnp.mean(x, -1, keepdims=True)
                x = x - mean
                inv = lax.rsqrt(jnp.mean(x * x, -1, keepdims=True) + EPS)
                x = x * inv
                norm[i] = x
                rstd[i] = jnp.broadcast_to(inv, (TOK, 128))
                proj[i] = dot((x * gain_attn[...]).astype(BF), w_qkv[...]).astype(BF)
                for p in range(PAIRS):
                    attend(i, across_lat, p)
                result = dot(mixed[...], w_out[...]).astype(BF)
            else:
                mixed[...] = dot_t(token[...], w_out[...]).astype(BF)
                for p in range(PAIRS):
                    attend_back(i, p)
                d = dot_t(dproj[...], w_qkv[...]).astype(BF).astype(F32) * gain_attn[...]
                nn = norm[i]
                inv = rstd[i][:, :1]
                result = (inv * (
                    d - jnp.mean(d, -1, keepdims=True) - nn * jnp.mean(d * nn, -1, keepdims=True)
                )).astype(BF)
            result = result.reshape(WLAT, WLON, 2, FEAT)
            for ref, at_c in results:
                ref[pl.ds(back_r + wr, WLAT), pl.ds(at_c + wc, WLON)] = result
            for turn, part in ((1, copies[:1]), (2, copies[1:4]), (3, copies[4:])):
                @pl.when(i == turn)
                def _(part=part):
                    for copy in part:
                        copy.start()
            return carry

        lax.fori_loop(0, 4, step, 0)

    loads[0].wait()
    loads[1].wait()
    strip, slim = TOK // STRIPS, cols // STRIPS
    thin = slim // 2

    def quarter_back(j, carry):
        at = pl.multiple_of(j * FEAT, FEAT)
        x = jnp.concatenate(
            [cot_coarse[:, k * thin:(k + 1) * thin].reshape(strip, 2 * FEAT) for k in range(STRIPS)], 0
        )
        y = dot_t(x, w_merge[pl.ds(at, FEAT), :]).astype(BF)
        gm[:, :, pl.ds(at, FEAT)] = y.reshape(STRIPS, strip, FEAT)
        return carry

    lax.fori_loop(0, 4, quarter_back, 0)
    for load in loads[2:8]:
        load.wait()
    windows(True, first, own, xtall, ext, ((btall, 0), (bext, back_c)), second)
    loads[8].wait()
    loads[9].wait()
    second[0].wait_recv()
    second[3].wait_recv()

    start_r, start_c = halo_lat - t_lat, halo_lon - t_lon
    width = 4 * FEAT
    patches = (rows // 2, 2, cols // 2, 2, 2, FEAT)
    quarters = [(a, b) for a in range(2) for b in range(2)]

    def merge(turn, carry):
        j = turn if lj else lax.rem(turn + 1, STRIPS)
        mine = pl.ds(slim * j, slim)

        @pl.when(turn < STRIPS - 1)
        def _():
            placed = btall[pl.ds(start_r, rows), pl.ds(start_c - back_c + slim * j, slim)]
            skip[:, mine] = (own[:, mine].astype(F32) + placed.astype(F32)).astype(BF)

        @pl.when(turn == STRIPS - 1)
        def _():
            for i in (1, 2, 4):
                second[i].wait_recv()
            bext[pl.ds(bhalo_r, halo_lat), pl.ds(back_c, cols)] = btall[pl.ds(bhalo_r, halo_lat)]
            placed = bext[pl.ds(start_r, rows), pl.ds(start_c + slim * j, slim)]
            skip[:, mine] = (own[:, mine].astype(F32) + placed.astype(F32)).astype(BF)

        def quarter(ref, a, b):
            return ref.reshape(*patches)[:, a, pl.ds(thin * j, thin), b].reshape(strip, FEAT)

        parts = [quarter(skip, a, b).astype(F32) for a, b in quarters]
        mean = sum(jnp.sum(x, -1, keepdims=True) for x in parts) / width
        parts = [x - mean for x in parts]
        inv = lax.rsqrt(sum(jnp.sum(x * x, -1, keepdims=True) for x in parts) / width + EPS)
        parts = [x * inv for x in parts]
        grads = []
        for i, x in enumerate(parts):
            gain = gain_merge[:, pl.ds(i * FEAT, FEAT)]
            merged[j, :, pl.ds(i * FEAT, FEAT)] = (x * gain).astype(BF)
            grads.append(gm[j, :, pl.ds(i * FEAT, FEAT)].astype(F32) * gain)
        mean_g = sum(jnp.sum(g, -1, keepdims=True) for g in grads) / width
        mean_gx = sum(jnp.sum(g * x, -1, keepdims=True) for g, x in zip(grads, parts)) / width
        for (a, b), g, x in zip(quarters, grads, parts):
            d = (inv * (g - mean_g - x * mean_gx)).astype(BF) + quarter(cot_skip, a, b)
            gskip.reshape(*patches)[:, a, pl.ds(thin * j, thin), b] = d.reshape(
                rows // 2, thin, 2, FEAT
            )
        return carry

    lax.fori_loop(0, STRIPS, merge, 0)
    for turn in (1, 2, 0):
        third[turn].start()
    gtall[pl.ds(own_r, rows)] = gskip[...]
    gext[inner] = gskip[...]
    skip_out = pltpu.make_async_copy(skip, skip_hbm, out_sem.at[0])
    skip_out.start()
    windows(False, third, gskip, gtall, gext, ((rext, back_c),), fourth)

    def coarse_part(j, carry):
        at = pl.multiple_of(j * FEAT, FEAT)
        x = merged.reshape(TOK, width)[...]
        y = dot(x, w_merge[:, pl.ds(at, FEAT)]).astype(BF)
        for k in range(STRIPS):
            coarse[:, k * thin:(k + 1) * thin, :, pl.ds(at, FEAT)] = y[
                k * strip:(k + 1) * strip
            ].reshape(rows // 2, thin, 2, FEAT)
        return carry

    lax.fori_loop(0, 2, coarse_part, 0)
    coarse_out = pltpu.make_async_copy(coarse, coarse_hbm, out_sem.at[1])
    coarse_out.start()
    for copy in fourth:
        copy.wait_recv()

    def finish(j, carry):
        mine = pl.ds(4 * j, 4)
        out[mine] = gskip[mine] + rext[pl.ds(start_r + 4 * j, 4), pl.ds(start_c, cols)]
        return carry

    lax.fori_loop(0, rows // 4, finish, 0)
    grad_out = pltpu.make_async_copy(out, grad_hbm, out_sem.at[2])
    grad_out.start()
    for copy in first + second + third + fourth:
        copy.wait_send()
    skip_out.wait()
    coarse_out.wait()
    grad_out.wait()


def block(behind_lat, behind_lon, halo_lat, halo_lon, ident, args):
    (inputs, shift_lat, shift_lon, gain_attn, w_qkv, w_out, gain_merge, w_merge,
     cot_coarse, cot_skip) = args
    rows, cols, lev, feat = inputs.shape
    wide = (rows + halo_lat, cols + halo_lon, lev, feat)
    smem = pl.BlockSpec(memory_space=pltpu.SMEM)
    hbm = pl.BlockSpec(memory_space=pltpu.HBM)
    anyw = pl.BlockSpec(memory_space=pl.ANY)
    tile, coarse = pltpu.VMEM(inputs.shape, BF), pltpu.VMEM(cot_coarse.shape, BF)
    tall = pltpu.VMEM((rows + halo_lat, cols, lev, feat), BF)
    return pl.pallas_call(
        functools.partial(kernel, behind_lat, behind_lon, halo_lat, halo_lon),
        out_shape=(
            jax.ShapeDtypeStruct(cot_coarse.shape, BF),
            jax.ShapeDtypeStruct(inputs.shape, BF),
            jax.ShapeDtypeStruct(inputs.shape, BF),
        ),
        in_specs=[smem, smem] + [hbm] * 8,
        out_specs=(anyw, anyw, anyw),
        scratch_shapes=[
            pltpu.VMEM((1, feat), F32),
            pltpu.VMEM((1, 4 * feat), F32),
            tile,
            tall, tall, tall,
            pltpu.VMEM(wide, BF),
            pltpu.VMEM(wide, BF),
            pltpu.VMEM(wide, BF),
            pltpu.VMEM(wide, BF),
            tile, tile, tile, coarse, coarse, tile,
            pltpu.VMEM(w_qkv.shape, BF),
            pltpu.VMEM(w_out.shape, BF),
            pltpu.VMEM(w_merge.shape, BF),
            pltpu.VMEM((STRIPS, TOK // STRIPS, 4 * FEAT), BF),
            pltpu.VMEM((STRIPS, TOK // STRIPS, 4 * FEAT), BF),
            pltpu.VMEM((TOK, FEAT), BF),
            pltpu.VMEM((4, TOK, FEAT), F32),
            pltpu.VMEM((4, TOK, 128), F32),
            pltpu.VMEM((4, TOK, 3 * FEAT), BF),
            pltpu.VMEM((TOK, FEAT), BF),
            pltpu.VMEM((4, PAIRS, TOK, 2 * TOK), BF),
            pltpu.VMEM((TOK, 3 * FEAT), BF),
            pltpu.VMEM((2, TOK, 2 * TOK), F32),
            pltpu.SemaphoreType.DMA((10,)),
            pltpu.SemaphoreType.DMA((3,)),
            pltpu.SemaphoreType.DMA((4, 5)),
            pltpu.SemaphoreType.DMA((4, 5)),
        ],
        compiler_params=pltpu.CompilerParams(
            collective_id=ident, has_side_effects=True, vmem_limit_bytes=VMEM
        ),
    )(
        shift_lat, shift_lon, gain_attn.reshape(1, -1), gain_merge.reshape(1, -1),
        inputs, w_qkv, w_out, w_merge, cot_coarse, cot_skip,
    )


def deliver(coarse, skip, grad, coarse_hbm, skip_hbm, grad_hbm, sem):
    copies = [
        pltpu.make_async_copy(src, dst, sem.at[i])
        for i, (src, dst) in enumerate(((coarse, coarse_hbm), (skip, skip_hbm), (grad, grad_hbm)))
    ]
    for copy in copies:
        copy.start()
    for copy in copies:
        copy.wait()


def hand_out(results):
    anyw = pl.BlockSpec(memory_space=pl.ANY)
    return pl.pallas_call(
        deliver,
        out_shape=tuple(jax.ShapeDtypeStruct(x.shape, x.dtype) for x in results),
        in_specs=[anyw] * 3,
        out_specs=(pl.BlockSpec(memory_space=pltpu.HBM),) * 3,
        scratch_shapes=[pltpu.SemaphoreType.DMA((3,))],
    )(*results)


def local(*args):
    half_lat, half_lon = WLAT // 2, WLON // 2
    behind_lat = (args[1][0] > half_lat).astype(jnp.int32)
    behind_lon = (args[2][0] > half_lon).astype(jnp.int32)
    results = lax.switch(
        2 * behind_lat + behind_lon,
        [
            functools.partial(block, bool(i // 2), bool(i % 2), half_lat, half_lon, i)
            for i in range(4)
        ],
        args,
    )
    return hand_out(results)


def solution(mesh):
    tile = P("lat", "lon", None, None)
    return jax.shard_map(
        local,
        mesh=mesh,
        in_specs=(tile, P(), P(), P(), P(), P(), P(), P(), tile, tile),
        out_specs=(tile, tile, tile),
        check_vma=False,
    )
```

```python
import functools

import jax
import jax.numpy as jnp
from jax import lax
from jax.experimental import pallas as pl
from jax.experimental.pallas import tpu as pltpu
from jax.sharding import PartitionSpec as P

WLAT = 6
WLON = 12
PAIRS = 4
TOK = 144
FEAT = 512
HALF = FEAT // 2
EPS = 1e-05
BF = jnp.bfloat16
F32 = jnp.float32
MESH = pl.DeviceIdType.MESH
VMEM = 48 * 2**20
STRIPS = 3


def dot(a, b):
    return jnp.dot(a, b, preferred_element_type=F32)


def dot_t(a, b):
    return lax.dot_general(a, b, (((1,), (1,)), ((), ())), preferred_element_type=F32)


def t_dot(a, b):
    return lax.dot_general(a, b, (((0,), (0,)), ((), ())), preferred_element_type=F32)


def kernel(
    behind_lat, behind_lon, halo_lat, halo_lon,
    shift_lat, shift_lon, gain_attn_hbm, gain_merge_hbm,
    inputs, w_qkv_hbm, w_out_hbm, w_merge_hbm, cot_coarse_hbm, cot_skip_hbm,
    coarse_hbm, skip_hbm, grad_hbm,
    gain_attn, gain_merge,
    own, xtall, btall, gtall, rtall, ext, bext, gext, rext, gskip, skip, cot_skip, cot_coarse, coarse, out,
    w_qkv, w_out, w_merge,
    gm, merged, token, norm, rstd, proj, mixed, soft, dproj, bias,
    local_sem, out_sem, send_sem, recv_sem,
):
    rows, cols = own.shape[0], own.shape[1]
    lat, lon = lax.axis_index("lat"), lax.axis_index("lon")
    nlat, nlon = lax.axis_size("lat"), lax.axis_size("lon")
    band = rows * nlat
    li, lj = int(behind_lat), int(behind_lon)

    def device(step_lat, step_lon):
        return (lax.rem(lat + step_lat + nlat, nlat), lax.rem(lon + step_lon + nlon, nlon))

    dlat, dlon = 1 - 2 * li, 1 - 2 * lj
    steps = ((dlat, 0), (0, dlon), (dlat, dlon))
    own_r, own_c = li * halo_lat, lj * halo_lon
    halo_r, halo_c = (1 - li) * rows, (1 - lj) * cols
    back_r, back_c = (1 - li) * halo_lat, (1 - lj) * halo_lon
    bhalo_r, bhalo_c = li * rows, lj * cols
    edge_r, edge_c = li * (rows - halo_lat), lj * (cols - halo_lon)
    bedge_r, bedge_c = (1 - li) * (rows - halo_lat), (1 - lj) * (cols - halo_lon)

    def send(phase, i, source, src, target, dst, step_lat, step_lon):
        (r, c, n, m), (tr, tc) = src, dst
        return pltpu.make_async_remote_copy(
            src_ref=source.at[pl.ds(r, n), pl.ds(c, m)],
            dst_ref=target.at[pl.ds(tr, n), pl.ds(tc, m)],
            send_sem=send_sem.at[phase, i],
            recv_sem=recv_sem.at[phase, i],
            device_id=device(step_lat, step_lon),
            device_id_type=MESH,
        )

    def ahead(phase, source, r, c, tall, wide):
        er, ec = r + edge_r, c + edge_c
        return (
            send(phase, 0, source, (er, c, halo_lat, cols), tall, (halo_r, 0), -dlat, 0),
            send(phase, 1, source, (r, ec, rows, halo_lon), wide, (own_r, halo_c), 0, -dlon),
            send(phase, 2, source, (er, ec, halo_lat, halo_lon), wide, (halo_r, halo_c), -dlat, -dlon),
        )

    def back(phase, tall, wide):
        er, ec = back_r + bedge_r, back_c + bedge_c
        near_c, far_c = lj * WLON, (1 - lj) * WLON
        return (
            send(phase, 0, tall, (er, near_c, halo_lat, WLON), tall, (bhalo_r, near_c), dlat, 0),
            send(phase, 1, wide, (er, ec, halo_lat, halo_lon), wide, (bhalo_r, bhalo_c), dlat, dlon),
            send(phase, 2, wide, (back_r, ec, rows, halo_lon), wide, (back_r, bhalo_c), 0, dlon),
            send(phase, 3, tall, (er, far_c, halo_lat, WLON), tall, (bhalo_r, far_c), dlat, 0),
        )

    inner = (pl.ds(own_r, rows), pl.ds(own_c, cols))
    loads = [
        pltpu.make_async_copy(src, dst, local_sem.at[i])
        for i, (src, dst) in enumerate((
            (cot_coarse_hbm, cot_coarse),
            (w_merge_hbm, w_merge),
            (gain_attn_hbm, gain_attn),
            (inputs, own),
            (w_qkv_hbm, w_qkv),
            (w_out_hbm, w_out),
            (inputs, xtall.at[pl.ds(own_r, rows)]),
            (inputs, ext.at[inner]),
            (cot_skip_hbm, cot_skip),
            (gain_merge_hbm, gain_merge),
        ))
    ]
    barrier = pltpu.get_barrier_semaphore()
    for sr, sc in steps:
        pl.semaphore_signal(barrier, inc=1, device_id=device(sr, sc), device_id_type=MESH)
        pl.semaphore_signal(barrier, inc=1, device_id=device(-sr, -sc), device_id_type=MESH)
    for load in loads:
        load.start()
    pl.semaphore_wait(barrier, 6)
    first = ahead(0, inputs, 0, 0, xtall, ext)
    first[1].start()
    first[2].start()
    second = back(1, btall, bext)
    third = ahead(2, gskip, 0, 0, gtall, gext)
    fourth = back(3, rtall, rext)

    s_lat, s_lon = shift_lat[0], shift_lon[0]
    t_lat = jnp.clip(s_lat - li * (WLAT - halo_lat), 0, halo_lat)
    t_lon = jnp.clip(s_lon - lj * (WLON - halo_lon), 0, halo_lon)

    low = lax.broadcasted_iota(jnp.int32, (TOK, 128), 1) < 64
    zero = jnp.zeros((TOK, 128), BF)

    def both(x):
        return jnp.concatenate([jnp.where(low, x, zero), jnp.where(low, zero, x)], 0)

    def unite(x):
        return jnp.where(low, x[:TOK], x[TOK:])

    start = lax.rem(rows * lat + WLAT * (1 - 2 * li) + band, band)
    edge = 2 * WLON * (band - s_lat - start)
    row_in = lax.broadcasted_iota(jnp.int32, (TOK, TOK), 0) >= edge
    col_in = lax.broadcasted_iota(jnp.int32, (TOK, TOK), 1) >= edge
    apart = jnp.where(row_in != col_in, F32(-1e30), F32(0.0))
    bias[0] = jnp.zeros((TOK, 2 * TOK), F32)
    bias[1] = jnp.concatenate([apart, apart], 1)

    def attend(i, u, across, p):
        at, rr = p * 128, pl.ds(u * TOK, TOK)
        q = both(proj[i, rr, pl.ds(at, 128)] * BF(0.125))
        k = proj[i, rr, pl.ds(FEAT + at, 128)]
        v = proj[i, rr, pl.ds(2 * FEAT + at, 128)]
        scores = dot_t(k, q) + bias[across]
        e = jnp.exp(scores - jnp.max(scores, 0, keepdims=True))
        w = (e * (1.0 / jnp.sum(e, 0, keepdims=True))).astype(BF)
        soft[i, u, p] = w
        mixed[rr, pl.ds(at, 128)] = unite(t_dot(w, v)).astype(BF)

    def attend_back(i, u, p):
        at, rr = p * 128, pl.ds(pl.multiple_of(u * TOK, 16), TOK)
        q = both(proj[i, rr, pl.ds(at, 128)] * BF(0.125))
        k = proj[i, rr, pl.ds(FEAT + at, 128)]
        v = proj[i, rr, pl.ds(2 * FEAT + at, 128)]
        g = both(mixed[rr, pl.ds(at, 128)])
        w = soft[i, u, p]
        dw = dot_t(v, g)
        wf = w.astype(F32)
        ds = (wf * (dw - jnp.sum(dw * wf, 0, keepdims=True))).astype(BF)
        dproj[rr, pl.ds(at, 128)] = (unite(t_dot(ds, k)) * 0.125).astype(BF)
        dproj[rr, pl.ds(FEAT + at, 128)] = dot(ds, q).astype(BF)
        dproj[rr, pl.ds(2 * FEAT + at, 128)] = dot(w, g).astype(BF)

    def windows(forward, ready, local_ref, tall, wide, results, copies):
        def step(i, carry):
            across = (i, 1 - i)
            wr = tuple(WLAT * (li + dlat * a) for a in across)
            wc = WLON * (lj + dlon * i)

            @pl.when(i == 0)
            def _():
                x = local_ref[pl.ds(s_lat, WLAT), pl.ds(s_lon, WLON)]
                token[pl.ds(0, TOK)] = x.reshape(TOK, FEAT)
                ready[0].wait_recv()
                x = tall[pl.ds(t_lat + wr[1], WLAT), pl.ds(s_lon, WLON)]
                token[pl.ds(TOK, TOK)] = x.reshape(TOK, FEAT)

            @pl.when(i == 1)
            def _():
                wide[pl.ds(halo_r, halo_lat), pl.ds(own_c, cols)] = tall[pl.ds(halo_r, halo_lat)]
                ready[1].wait_recv()
                ready[2].wait_recv()
                for u in range(2):
                    x = wide[pl.ds(t_lat + wr[u], WLAT), pl.ds(t_lon + wc, WLON)]
                    token[pl.ds(u * TOK, TOK)] = x.reshape(TOK, FEAT)

            if forward:
                x = token[...].astype(F32)
                mean = jnp.mean(x, -1, keepdims=True)
                x = x - mean
                inv = lax.rsqrt(jnp.mean(x * x, -1, keepdims=True) + EPS)
                x = x * inv
                norm[i] = x
                rstd[i] = jnp.broadcast_to(inv, (2 * TOK, 128))
                proj[i] = dot((x * gain_attn[...]).astype(BF), w_qkv[...]).astype(BF)
                for u in range(2):
                    for p in range(PAIRS):
                        attend(i, u, across[u], p)
                result = dot(mixed[...], w_out[...]).astype(BF)
            else:
                mixed[...] = dot_t(token[...], w_out[...]).astype(BF)

                def back_rows(u, carry):
                    for p in range(PAIRS):
                        attend_back(i, u, p)
                    return carry

                lax.fori_loop(0, 2, back_rows, 0)
                d = dot_t(dproj[...], w_qkv[...]).astype(BF).astype(F32) * gain_attn[...]
                nn = norm[i]
                inv = rstd[i][:, :1]
                result = (inv * (
                    d - jnp.mean(d, -1, keepdims=True) - nn * jnp.mean(d * nn, -1, keepdims=True)
                )).astype(BF)
            for u in range(2):
                part = result[u * TOK:(u + 1) * TOK].reshape(WLAT, WLON, 2, FEAT)
                for ref, at_c in results:
                    ref[pl.ds(back_r + wr[u], WLAT), pl.ds(at_c + wc, WLON)] = part

            @pl.when(i == 0)
            def _():
                copies[0].start()

            @pl.when(i == 1)
            def _():
                for copy in copies[1:]:
                    copy.start()

            return carry

        lax.fori_loop(0, 2, step, 0)

    loads[0].wait()
    loads[1].wait()
    strip, slim = TOK // STRIPS, cols // STRIPS
    thin = slim // 2

    def part_back(j, carry):
        at = pl.multiple_of(j * HALF, HALF)
        x = jnp.concatenate(
            [cot_coarse[:, k * thin:(k + 1) * thin].reshape(strip, 2 * FEAT) for k in range(STRIPS)], 0
        )
        y = dot_t(x, w_merge[pl.ds(at, HALF), :]).astype(BF)
        gm[:, :, pl.ds(at, HALF)] = y.reshape(STRIPS, strip, HALF)
        return carry

    lax.fori_loop(0, 4 * FEAT // HALF, part_back, 0)
    first[0].start()
    for load in loads[2:8]:
        load.wait()
    windows(True, first, own, xtall, ext, ((btall, 0), (bext, back_c)), second)
    loads[8].wait()
    loads[9].wait()
    second[0].wait_recv()
    second[3].wait_recv()

    start_r, start_c = halo_lat - t_lat, halo_lon - t_lon
    width = 4 * FEAT
    patches = (rows // 2, 2, cols // 2, 2, 2, FEAT)
    quarters = [(a, b) for a in range(2) for b in range(2)]

    def merge(turn, carry):
        j = turn if lj else lax.rem(turn + 1, STRIPS)
        mine = pl.ds(slim * j, slim)

        @pl.when(turn < STRIPS - 1)
        def _():
            placed = btall[pl.ds(start_r, rows), pl.ds(start_c - back_c + slim * j, slim)]
            skip[:, mine] = (own[:, mine].astype(F32) + placed.astype(F32)).astype(BF)

        @pl.when(turn == STRIPS - 1)
        def _():
            second[1].wait_recv()
            second[2].wait_recv()
            bext[pl.ds(bhalo_r, halo_lat), pl.ds(back_c, cols)] = btall[pl.ds(bhalo_r, halo_lat)]
            placed = bext[pl.ds(start_r, rows), pl.ds(start_c + slim * j, slim)]
            skip[:, mine] = (own[:, mine].astype(F32) + placed.astype(F32)).astype(BF)

        def quarter(ref, a, b):
            return ref.reshape(*patches)[:, a, pl.ds(thin * j, thin), b].reshape(strip, FEAT)

        parts = [quarter(skip, a, b).astype(F32) for a, b in quarters]
        mean = sum(jnp.sum(x, -1, keepdims=True) for x in parts) / width
        parts = [x - mean for x in parts]
        inv = lax.rsqrt(sum(jnp.sum(x * x, -1, keepdims=True) for x in parts) / width + EPS)
        parts = [x * inv for x in parts]
        grads = []
        for i, x in enumerate(parts):
            gain = gain_merge[:, pl.ds(i * FEAT, FEAT)]
            merged[j, :, pl.ds(i * FEAT, FEAT)] = (x * gain).astype(BF)
            grads.append(gm[j, :, pl.ds(i * FEAT, FEAT)].astype(F32) * gain)
        mean_g = sum(jnp.sum(g, -1, keepdims=True) for g in grads) / width
        mean_gx = sum(jnp.sum(g * x, -1, keepdims=True) for g, x in zip(grads, parts)) / width
        for (a, b), g, x in zip(quarters, grads, parts):
            d = (inv * (g - mean_g - x * mean_gx)).astype(BF) + quarter(cot_skip, a, b)
            gskip.reshape(*patches)[:, a, pl.ds(thin * j, thin), b] = d.reshape(
                rows // 2, thin, 2, FEAT
            )
        return carry

    lax.fori_loop(0, STRIPS, merge, 0)
    third[1].start()
    third[2].start()
    spread = [
        pltpu.make_async_copy(gskip, gtall.at[pl.ds(own_r, rows)], local_sem.at[10]),
        pltpu.make_async_copy(gskip, gext.at[inner], local_sem.at[11]),
    ]
    for copy in spread:
        copy.start()
    skip_out = pltpu.make_async_copy(skip, skip_hbm, out_sem.at[0])
    skip_out.start()

    def coarse_part(j, carry):
        @pl.when(j == 1)
        def _():
            third[0].start()

        at = pl.multiple_of(j * HALF, HALF)
        x = merged.reshape(TOK, width)[...]
        y = dot(x, w_merge[:, pl.ds(at, HALF)]).astype(BF)
        for k in range(STRIPS):
            coarse[:, k * thin:(k + 1) * thin, :, pl.ds(at, HALF)] = y[
                k * strip:(k + 1) * strip
            ].reshape(rows // 2, thin, 2, HALF)
        return carry

    lax.fori_loop(0, 2 * FEAT // HALF, coarse_part, 0)
    coarse_out = pltpu.make_async_copy(coarse, coarse_hbm, out_sem.at[1])
    coarse_out.start()
    for copy in spread:
        copy.wait()
    windows(False, third, gskip, gtall, gext, ((rtall, 0), (rext, back_c)), fourth)
    fourth[0].wait_recv()
    fourth[3].wait_recv()

    def grad_out(turn):
        j = turn if lj else lax.rem(turn + 1, STRIPS)
        mine = pl.ds(slim * j, slim)
        return pltpu.make_async_copy(out.at[:, mine], grad_hbm.at[:, mine], out_sem.at[2 + turn])

    def finish(turn, carry):
        j = turn if lj else lax.rem(turn + 1, STRIPS)
        mine = pl.ds(slim * j, slim)

        @pl.when(turn < STRIPS - 1)
        def _():
            placed = rtall[pl.ds(start_r, rows), pl.ds(start_c - back_c + slim * j, slim)]
            out[:, mine] = gskip[:, mine] + placed

        @pl.when(turn == STRIPS - 1)
        def _():
            rext[pl.ds(bhalo_r, halo_lat), pl.ds(back_c, cols)] = rtall[pl.ds(bhalo_r, halo_lat)]
            fourth[1].wait_recv()
            fourth[2].wait_recv()
            placed = rext[pl.ds(start_r, rows), pl.ds(start_c + slim * j, slim)]
            out[:, mine] = gskip[:, mine] + placed

        grad_out(turn).start()
        return carry

    lax.fori_loop(0, STRIPS, finish, 0)
    for copy in first + second + third + fourth:
        copy.wait_send()
    skip_out.wait()
    coarse_out.wait()
    for turn in range(STRIPS):
        grad_out(turn).wait()


def block(behind_lat, behind_lon, halo_lat, halo_lon, ident, args):
    (inputs, shift_lat, shift_lon, gain_attn, w_qkv, w_out, gain_merge, w_merge,
     cot_coarse, cot_skip) = args
    rows, cols, lev, feat = inputs.shape
    wide = (rows + halo_lat, cols + halo_lon, lev, feat)
    smem = pl.BlockSpec(memory_space=pltpu.SMEM)
    hbm = pl.BlockSpec(memory_space=pltpu.HBM)
    anyw = pl.BlockSpec(memory_space=pl.ANY)
    tile, coarse = pltpu.VMEM(inputs.shape, BF), pltpu.VMEM(cot_coarse.shape, BF)
    tall = pltpu.VMEM((rows + halo_lat, cols, lev, feat), BF)
    return pl.pallas_call(
        functools.partial(kernel, behind_lat, behind_lon, halo_lat, halo_lon),
        out_shape=(
            jax.ShapeDtypeStruct(cot_coarse.shape, BF),
            jax.ShapeDtypeStruct(inputs.shape, BF),
            jax.ShapeDtypeStruct(inputs.shape, BF),
        ),
        in_specs=[smem, smem] + [hbm] * 8,
        out_specs=(anyw, anyw, anyw),
        scratch_shapes=[
            pltpu.VMEM((1, feat), F32),
            pltpu.VMEM((1, 4 * feat), F32),
            tile,
            tall, tall, tall, tall,
            pltpu.VMEM(wide, BF),
            pltpu.VMEM(wide, BF),
            pltpu.VMEM(wide, BF),
            pltpu.VMEM(wide, BF),
            tile, tile, tile, coarse, coarse, tile,
            pltpu.VMEM(w_qkv.shape, BF),
            pltpu.VMEM(w_out.shape, BF),
            pltpu.VMEM(w_merge.shape, BF),
            pltpu.VMEM((STRIPS, TOK // STRIPS, 4 * FEAT), BF),
            pltpu.VMEM((STRIPS, TOK // STRIPS, 4 * FEAT), BF),
            pltpu.VMEM((2 * TOK, FEAT), BF),
            pltpu.VMEM((2, 2 * TOK, FEAT), F32),
            pltpu.VMEM((2, 2 * TOK, 128), F32),
            pltpu.VMEM((2, 2 * TOK, 3 * FEAT), BF),
            pltpu.VMEM((2 * TOK, FEAT), BF),
            pltpu.VMEM((2, 2, PAIRS, TOK, 2 * TOK), BF),
            pltpu.VMEM((2 * TOK, 3 * FEAT), BF),
            pltpu.VMEM((2, TOK, 2 * TOK), F32),
            pltpu.SemaphoreType.DMA((12,)),
            pltpu.SemaphoreType.DMA((2 + STRIPS,)),
            pltpu.SemaphoreType.DMA((4, 4)),
            pltpu.SemaphoreType.DMA((4, 4)),
        ],
        compiler_params=pltpu.CompilerParams(
            collective_id=ident, has_side_effects=True, vmem_limit_bytes=VMEM
        ),
    )(
        shift_lat, shift_lon, gain_attn.reshape(1, -1), gain_merge.reshape(1, -1),
        inputs, w_qkv, w_out, w_merge, cot_coarse, cot_skip,
    )


def deliver(coarse, skip, grad, coarse_hbm, skip_hbm, grad_hbm, sem):
    copies = [
        pltpu.make_async_copy(src, dst, sem.at[i])
        for i, (src, dst) in enumerate(((coarse, coarse_hbm), (skip, skip_hbm), (grad, grad_hbm)))
    ]
    for copy in copies:
        copy.start()
    for copy in copies:
        copy.wait()


def hand_out(results):
    anyw = pl.BlockSpec(memory_space=pl.ANY)
    return pl.pallas_call(
        deliver,
        out_shape=tuple(jax.ShapeDtypeStruct(x.shape, x.dtype) for x in results),
        in_specs=[anyw] * 3,
        out_specs=(pl.BlockSpec(memory_space=pltpu.HBM),) * 3,
        scratch_shapes=[pltpu.SemaphoreType.DMA((3,))],
    )(*results)


def local(*args):
    half_lat, half_lon = WLAT // 2, WLON // 2
    behind_lat = (args[1][0] > half_lat).astype(jnp.int32)
    behind_lon = (args[2][0] > half_lon).astype(jnp.int32)
    results = lax.switch(
        2 * behind_lat + behind_lon,
        [
            functools.partial(block, bool(i // 2), bool(i % 2), half_lat, half_lon, i)
            for i in range(4)
        ],
        args,
    )
    return hand_out(results)


def solution(mesh):
    tile = P("lat", "lon", None, None)
    return jax.shard_map(
        local,
        mesh=mesh,
        in_specs=(tile, P(), P(), P(), P(), P(), P(), P(), tile, tile),
        out_specs=(tile, tile, tile),
        check_vma=False,
    )
```

```python
import functools

import jax
import jax.numpy as jnp
from jax import lax
from jax.experimental import pallas as pl
from jax.experimental.pallas import tpu as pltpu
from jax.sharding import PartitionSpec as P

WLAT = 6
WLON = 12
PAIRS = 4
TOK = 144
FEAT = 512
EPS = 1e-05
BF = jnp.bfloat16
F32 = jnp.float32
MESH = pl.DeviceIdType.MESH
VMEM = 48 * 2**20
STRIPS = 3


def dot(a, b):
    return jnp.dot(a, b, preferred_element_type=F32)


def dot_t(a, b):
    return lax.dot_general(a, b, (((1,), (1,)), ((), ())), preferred_element_type=F32)


def t_dot(a, b):
    return lax.dot_general(a, b, (((0,), (0,)), ((), ())), preferred_element_type=F32)


def kernel(
    behind_lat, behind_lon, halo_lat, halo_lon,
    shift_lat, shift_lon, gain_attn_hbm, gain_merge_hbm,
    inputs, w_qkv_hbm, w_out_hbm, w_merge_hbm, cot_coarse_hbm, cot_skip_hbm,
    coarse_hbm, skip_hbm, grad_hbm,
    gain_attn, gain_merge,
    own, xtall, btall, gtall, xflat, gflat, xquad, gquad, bext, rext, gskip, skip, cot_skip, cot_coarse, coarse, out,
    w_qkv, w_out, w_merge,
    gm, merged, token, norm, rstd, proj, mixed, soft, dproj, bias,
    local_sem, out_sem, send_sem, recv_sem,
):
    rows, cols = own.shape[0], own.shape[1]
    lat, lon = lax.axis_index("lat"), lax.axis_index("lon")
    nlat, nlon = lax.axis_size("lat"), lax.axis_size("lon")
    band = rows * nlat
    li, lj = int(behind_lat), int(behind_lon)

    def device(step_lat, step_lon):
        return (lax.rem(lat + step_lat + nlat, nlat), lax.rem(lon + step_lon + nlon, nlon))

    dlat, dlon = 1 - 2 * li, 1 - 2 * lj
    steps = ((dlat, 0), (0, dlon), (dlat, dlon))
    own_r, own_c = li * halo_lat, lj * halo_lon
    halo_r, halo_c = (1 - li) * rows, (1 - lj) * cols
    back_r, back_c = (1 - li) * halo_lat, (1 - lj) * halo_lon
    bhalo_r, bhalo_c = li * rows, lj * cols
    edge_r, edge_c = li * (rows - halo_lat), lj * (cols - halo_lon)
    bedge_r, bedge_c = (1 - li) * (rows - halo_lat), (1 - lj) * (cols - halo_lon)

    def send(phase, i, source, src, target, dst, step_lat, step_lon):
        (r, c, n, m), (tr, tc) = src, dst
        return pltpu.make_async_remote_copy(
            src_ref=source.at[pl.ds(r, n), pl.ds(c, m)],
            dst_ref=target.at[pl.ds(tr, n), pl.ds(tc, m)],
            send_sem=send_sem.at[phase, i],
            recv_sem=recv_sem.at[phase, i],
            device_id=device(step_lat, step_lon),
            device_id_type=MESH,
        )

    far_r, far_c = (1 - li) * WLAT, (1 - lj) * WLON
    quad_r, quad_c = li * halo_lat, lj * halo_lon
    qhalo_r, qhalo_c = (1 - li) * WLAT, (1 - lj) * WLON

    def ahead(phase, source, tall, flat, quad):
        er, ec = edge_r, edge_c
        return (
            send(phase, 0, source, (er, 0, halo_lat, cols), tall, (halo_r, 0), -dlat, 0),
            send(phase, 1, source, (0, ec, rows, halo_lon), flat, (0, halo_c), 0, -dlon),
            send(phase, 2, source, (er, ec, halo_lat, halo_lon), quad, (qhalo_r, qhalo_c), -dlat, -dlon),
        )

    def back(phase, tall, at_c, wide):
        er, ec = back_r + bedge_r, back_c + bedge_c
        far_r, near_r = back_r + (1 - li) * WLAT, back_r + li * WLAT
        far_c, near_c = at_c + (1 - lj) * WLON, at_c + lj * WLON
        return (
            send(phase, 0, tall, (er, near_c, halo_lat, WLON), tall, (bhalo_r, near_c), dlat, 0),
            send(phase, 1, wide, (er, ec, halo_lat, halo_lon), wide, (bhalo_r, bhalo_c), dlat, dlon),
            send(phase, 2, wide, (far_r, ec, WLAT, halo_lon), wide, (far_r, bhalo_c), 0, dlon),
            send(phase, 3, tall, (er, far_c, halo_lat, WLON), tall, (bhalo_r, far_c), dlat, 0),
            send(phase, 4, wide, (near_r, ec, WLAT, halo_lon), wide, (near_r, bhalo_c), 0, dlon),
        )

    loads = [
        pltpu.make_async_copy(src, dst, local_sem.at[i])
        for i, (src, dst) in enumerate((
            (cot_coarse_hbm, cot_coarse),
            (w_merge_hbm, w_merge),
            (gain_attn_hbm, gain_attn),
            (inputs, own),
            (w_qkv_hbm, w_qkv),
            (w_out_hbm, w_out),
            (inputs, xtall.at[pl.ds(own_r, rows)]),
            (inputs, xflat.at[:, pl.ds(own_c, cols)]),
            (cot_skip_hbm, cot_skip),
            (gain_merge_hbm, gain_merge),
        ))
    ]
    barrier = pltpu.get_barrier_semaphore()
    for sr, sc in steps:
        pl.semaphore_signal(barrier, inc=1, device_id=device(sr, sc), device_id_type=MESH)
        pl.semaphore_signal(barrier, inc=1, device_id=device(-sr, -sc), device_id_type=MESH)
    for load in loads:
        load.start()
    pl.semaphore_wait(barrier, 6)
    first = ahead(0, inputs, xtall, xflat, xquad)
    first[1].start()
    first[0].start()
    second = back(1, btall, 0, bext)
    third = ahead(2, gskip, gtall, gflat, gquad)
    fourth = back(3, rext, back_c, rext)

    s_lat, s_lon = shift_lat[0], shift_lon[0]
    t_lat = jnp.clip(s_lat - li * (WLAT - halo_lat), 0, halo_lat)
    t_lon = jnp.clip(s_lon - lj * (WLON - halo_lon), 0, halo_lon)

    low = lax.broadcasted_iota(jnp.int32, (TOK, 128), 1) < 64
    zero = jnp.zeros((TOK, 128), BF)

    def both(x):
        return jnp.concatenate([jnp.where(low, x, zero), jnp.where(low, zero, x)], 0)

    def unite(x):
        return jnp.where(low, x[:TOK], x[TOK:])

    start = lax.rem(rows * lat + WLAT * (1 - 2 * li) + band, band)
    edge = 2 * WLON * (band - s_lat - start)
    row_in = lax.broadcasted_iota(jnp.int32, (TOK, TOK), 0) >= edge
    col_in = lax.broadcasted_iota(jnp.int32, (TOK, TOK), 1) >= edge
    apart = jnp.where(row_in != col_in, F32(-1e30), F32(0.0))
    bias[0] = jnp.zeros((TOK, 2 * TOK), F32)
    bias[1] = jnp.concatenate([apart, apart], 1)

    def attend(i, across, p):
        at = p * 128
        q = both(proj[i, :, pl.ds(at, 128)] * BF(0.125))
        k = proj[i, :, pl.ds(FEAT + at, 128)]
        v = proj[i, :, pl.ds(2 * FEAT + at, 128)]
        scores = dot_t(k, q) + bias[across]
        e = jnp.exp(scores - jnp.max(scores, 0, keepdims=True))
        w = (e * (1.0 / jnp.sum(e, 0, keepdims=True))).astype(BF)
        soft[i, p] = w
        mixed[:, pl.ds(at, 128)] = unite(t_dot(w, v)).astype(BF)

    def attend_back(i, p):
        at = p * 128
        q = both(proj[i, :, pl.ds(at, 128)] * BF(0.125))
        k = proj[i, :, pl.ds(FEAT + at, 128)]
        v = proj[i, :, pl.ds(2 * FEAT + at, 128)]
        g = both(mixed[:, pl.ds(at, 128)])
        w = soft[i, p]
        dw = dot_t(v, g)
        wf = w.astype(F32)
        ds = (wf * (dw - jnp.sum(dw * wf, 0, keepdims=True))).astype(BF)
        dproj[:, pl.ds(at, 128)] = (unite(t_dot(ds, k)) * 0.125).astype(BF)
        dproj[:, pl.ds(FEAT + at, 128)] = dot(ds, q).astype(BF)
        dproj[:, pl.ds(2 * FEAT + at, 128)] = dot(w, g).astype(BF)

    def windows(forward, ready, local_ref, tall, flat, quad, results, copies):
        def step(i, carry):
            across_lat, across_lon = i % 2, i // 2
            wr = WLAT * (li + dlat * across_lat)
            wc = WLON * (lj + dlon * across_lon)

            @pl.when(i == 0)
            def _():
                x = local_ref[pl.ds(s_lat, WLAT), pl.ds(s_lon, WLON)]
                token[...] = x.reshape(TOK, FEAT)

            @pl.when(i == 1)
            def _():
                ready[0].wait_recv()
                x = tall[pl.ds(t_lat + wr, WLAT), pl.ds(s_lon, WLON)]
                token[...] = x.reshape(TOK, FEAT)

            @pl.when(i == 2)
            def _():
                ready[1].wait_recv()
                x = flat[pl.ds(s_lat, WLAT), pl.ds(t_lon + wc, WLON)]
                token[...] = x.reshape(TOK, FEAT)

            @pl.when(i == 3)
            def _():
                mine = (pl.ds(quad_r, WLAT), pl.ds(quad_c, WLON))
                quad[mine] = local_ref[pl.ds(far_r, WLAT), pl.ds(far_c, WLON)]
                quad[pl.ds(qhalo_r, halo_lat), mine[1]] = tall[
                    pl.ds(halo_r, halo_lat), pl.ds(far_c, WLON)
                ]
                quad[mine[0], pl.ds(qhalo_c, halo_lon)] = flat[
                    pl.ds(far_r, WLAT), pl.ds(halo_c, halo_lon)
                ]
                ready[2].wait_recv()
                x = quad[pl.ds(t_lat, WLAT), pl.ds(t_lon, WLON)]
                token[...] = x.reshape(TOK, FEAT)

            if forward:
                x = token[...].astype(F32)
                mean = jnp.mean(x, -1, keepdims=True)
                x = x - mean
                inv = lax.rsqrt(jnp.mean(x * x, -1, keepdims=True) + EPS)
                x = x * inv
                norm[i] = x
                rstd[i] = jnp.broadcast_to(inv, (TOK, 128))
                proj[i] = dot((x * gain_attn[...]).astype(BF), w_qkv[...]).astype(BF)
                for p in range(PAIRS):
                    attend(i, across_lat, p)
                result = dot(mixed[...], w_out[...]).astype(BF)
            else:
                mixed[...] = dot_t(token[...], w_out[...]).astype(BF)
                for p in range(PAIRS):
                    attend_back(i, p)
                d = dot_t(dproj[...], w_qkv[...]).astype(BF).astype(F32) * gain_attn[...]
                nn = norm[i]
                inv = rstd[i][:, :1]
                result = (inv * (
                    d - jnp.mean(d, -1, keepdims=True) - nn * jnp.mean(d * nn, -1, keepdims=True)
                )).astype(BF)
            result = result.reshape(WLAT, WLON, 2, FEAT)
            for ref, at_c in results:
                ref[pl.ds(back_r + wr, WLAT), pl.ds(at_c + wc, WLON)] = result
            for turn, part in ((1, copies[:1]), (2, copies[4:]), (3, copies[1:4])):
                @pl.when(i == turn)
                def _(part=part):
                    for copy in part:
                        copy.start()
            return carry

        lax.fori_loop(0, 4, step, 0)

    loads[0].wait()
    loads[1].wait()
    strip, slim = TOK // STRIPS, cols // STRIPS
    thin = slim // 2

    def quarter_back(j, carry):
        at = pl.multiple_of(j * FEAT, FEAT)
        x = jnp.concatenate(
            [cot_coarse[:, k * thin:(k + 1) * thin].reshape(strip, 2 * FEAT) for k in range(STRIPS)], 0
        )
        y = dot_t(x, w_merge[pl.ds(at, FEAT), :]).astype(BF)
        gm[:, :, pl.ds(at, FEAT)] = y.reshape(STRIPS, strip, FEAT)
        return carry

    lax.fori_loop(0, 4, quarter_back, 0)
    first[2].start()
    for load in loads[2:8]:
        load.wait()
    windows(True, first, own, xtall, xflat, xquad, ((btall, 0), (bext, back_c)), second)
    loads[8].wait()
    loads[9].wait()
    second[0].wait_recv()
    second[3].wait_recv()

    start_r, start_c = halo_lat - t_lat, halo_lon - t_lon
    width = 4 * FEAT
    patches = (rows // 2, 2, cols // 2, 2, 2, FEAT)
    quarters = [(a, b) for a in range(2) for b in range(2)]

    def merge(turn, carry):
        j = turn if lj else lax.rem(turn + 1, STRIPS)
        mine = pl.ds(slim * j, slim)

        @pl.when(turn < STRIPS - 1)
        def _():
            placed = btall[pl.ds(start_r, rows), pl.ds(start_c - back_c + slim * j, slim)]
            skip[:, mine] = (own[:, mine].astype(F32) + placed.astype(F32)).astype(BF)

        @pl.when(turn == STRIPS - 1)
        def _():
            for i in (1, 2, 4):
                second[i].wait_recv()
            bext[pl.ds(bhalo_r, halo_lat), pl.ds(back_c, cols)] = btall[pl.ds(bhalo_r, halo_lat)]
            placed = bext[pl.ds(start_r, rows), pl.ds(start_c + slim * j, slim)]
            skip[:, mine] = (own[:, mine].astype(F32) + placed.astype(F32)).astype(BF)

        def quarter(ref, a, b):
            return ref.reshape(*patches)[:, a, pl.ds(thin * j, thin), b].reshape(strip, FEAT)

        parts = [quarter(skip, a, b).astype(F32) for a, b in quarters]
        mean = sum(jnp.sum(x, -1, keepdims=True) for x in parts) / width
        parts = [x - mean for x in parts]
        inv = lax.rsqrt(sum(jnp.sum(x * x, -1, keepdims=True) for x in parts) / width + EPS)
        parts = [x * inv for x in parts]
        grads = []
        for i, x in enumerate(parts):
            gain = gain_merge[:, pl.ds(i * FEAT, FEAT)]
            merged[j, :, pl.ds(i * FEAT, FEAT)] = (x * gain).astype(BF)
            grads.append(gm[j, :, pl.ds(i * FEAT, FEAT)].astype(F32) * gain)
        mean_g = sum(jnp.sum(g, -1, keepdims=True) for g in grads) / width
        mean_gx = sum(jnp.sum(g * x, -1, keepdims=True) for g, x in zip(grads, parts)) / width
        for (a, b), g, x in zip(quarters, grads, parts):
            d = (inv * (g - mean_g - x * mean_gx)).astype(BF) + quarter(cot_skip, a, b)
            gskip.reshape(*patches)[:, a, pl.ds(thin * j, thin), b] = d.reshape(
                rows // 2, thin, 2, FEAT
            )
        return carry

    lax.fori_loop(0, STRIPS, merge, 0)
    third[1].start()
    third[0].start()
    gtall[pl.ds(own_r, rows)] = gskip[...]
    gflat[:, pl.ds(own_c, cols)] = gskip[...]
    skip_out = pltpu.make_async_copy(skip, skip_hbm, out_sem.at[0])
    skip_out.start()
    def coarse_part(j, carry):
        at = pl.multiple_of(j * FEAT, FEAT)
        x = merged.reshape(TOK, width)[...]
        y = dot(x, w_merge[:, pl.ds(at, FEAT)]).astype(BF)
        for k in range(STRIPS):
            coarse[:, k * thin:(k + 1) * thin, :, pl.ds(at, FEAT)] = y[
                k * strip:(k + 1) * strip
            ].reshape(rows // 2, thin, 2, FEAT)
        return carry

    lax.fori_loop(0, 2, coarse_part, 0)
    coarse_out = pltpu.make_async_copy(coarse, coarse_hbm, out_sem.at[1])
    coarse_out.start()
    third[2].start()
    windows(False, third, gskip, gtall, gflat, gquad, ((rext, back_c),), fourth)
    for copy in fourth:
        copy.wait_recv()

    def finish(j, carry):
        mine = pl.ds(4 * j, 4)
        out[mine] = gskip[mine] + rext[pl.ds(start_r + 4 * j, 4), pl.ds(start_c, cols)]
        return carry

    lax.fori_loop(0, rows // 4, finish, 0)
    grad_out = pltpu.make_async_copy(out, grad_hbm, out_sem.at[2])
    grad_out.start()
    for copy in first + second + third + fourth:
        copy.wait_send()
    skip_out.wait()
    coarse_out.wait()
    grad_out.wait()


def block(behind_lat, behind_lon, halo_lat, halo_lon, ident, args):
    (inputs, shift_lat, shift_lon, gain_attn, w_qkv, w_out, gain_merge, w_merge,
     cot_coarse, cot_skip) = args
    rows, cols, lev, feat = inputs.shape
    wide = (rows + halo_lat, cols + halo_lon, lev, feat)
    smem = pl.BlockSpec(memory_space=pltpu.SMEM)
    hbm = pl.BlockSpec(memory_space=pltpu.HBM)
    anyw = pl.BlockSpec(memory_space=pl.ANY)
    tile, coarse = pltpu.VMEM(inputs.shape, BF), pltpu.VMEM(cot_coarse.shape, BF)
    tall = pltpu.VMEM((rows + halo_lat, cols, lev, feat), BF)
    flat = pltpu.VMEM((rows, cols + halo_lon, lev, feat), BF)
    quad = pltpu.VMEM((WLAT + halo_lat, WLON + halo_lon, lev, feat), BF)
    return pl.pallas_call(
        functools.partial(kernel, behind_lat, behind_lon, halo_lat, halo_lon),
        out_shape=(
            jax.ShapeDtypeStruct(cot_coarse.shape, BF),
            jax.ShapeDtypeStruct(inputs.shape, BF),
            jax.ShapeDtypeStruct(inputs.shape, BF),
        ),
        in_specs=[smem, smem] + [hbm] * 8,
        out_specs=(anyw, anyw, anyw),
        scratch_shapes=[
            pltpu.VMEM((1, feat), F32),
            pltpu.VMEM((1, 4 * feat), F32),
            tile,
            tall, tall, tall, flat, flat, quad, quad,
            pltpu.VMEM(wide, BF),
            pltpu.VMEM(wide, BF),
            tile, tile, tile, coarse, coarse, tile,
            pltpu.VMEM(w_qkv.shape, BF),
            pltpu.VMEM(w_out.shape, BF),
            pltpu.VMEM(w_merge.shape, BF),
            pltpu.VMEM((STRIPS, TOK // STRIPS, 4 * FEAT), BF),
            pltpu.VMEM((STRIPS, TOK // STRIPS, 4 * FEAT), BF),
            pltpu.VMEM((TOK, FEAT), BF),
            pltpu.VMEM((4, TOK, FEAT), F32),
            pltpu.VMEM((4, TOK, 128), F32),
            pltpu.VMEM((4, TOK, 3 * FEAT), BF),
            pltpu.VMEM((TOK, FEAT), BF),
            pltpu.VMEM((4, PAIRS, TOK, 2 * TOK), BF),
            pltpu.VMEM((TOK, 3 * FEAT), BF),
            pltpu.VMEM((2, TOK, 2 * TOK), F32),
            pltpu.SemaphoreType.DMA((10,)),
            pltpu.SemaphoreType.DMA((3,)),
            pltpu.SemaphoreType.DMA((4, 5)),
            pltpu.SemaphoreType.DMA((4, 5)),
        ],
        compiler_params=pltpu.CompilerParams(
            collective_id=ident, has_side_effects=True, vmem_limit_bytes=VMEM
        ),
    )(
        shift_lat, shift_lon, gain_attn.reshape(1, -1), gain_merge.reshape(1, -1),
        inputs, w_qkv, w_out, w_merge, cot_coarse, cot_skip,
    )


def deliver(coarse, skip, grad, coarse_hbm, skip_hbm, grad_hbm, sem):
    copies = [
        pltpu.make_async_copy(src, dst, sem.at[i])
        for i, (src, dst) in enumerate(((coarse, coarse_hbm), (skip, skip_hbm), (grad, grad_hbm)))
    ]
    for copy in copies:
        copy.start()
    for copy in copies:
        copy.wait()


def hand_out(results):
    anyw = pl.BlockSpec(memory_space=pl.ANY)
    return pl.pallas_call(
        deliver,
        out_shape=tuple(jax.ShapeDtypeStruct(x.shape, x.dtype) for x in results),
        in_specs=[anyw] * 3,
        out_specs=(pl.BlockSpec(memory_space=pltpu.HBM),) * 3,
        scratch_shapes=[pltpu.SemaphoreType.DMA((3,))],
    )(*results)


def local(*args):
    half_lat, half_lon = WLAT // 2, WLON // 2
    behind_lat = (args[1][0] > half_lat).astype(jnp.int32)
    behind_lon = (args[2][0] > half_lon).astype(jnp.int32)
    results = lax.switch(
        2 * behind_lat + behind_lon,
        [
            functools.partial(block, bool(i // 2), bool(i % 2), half_lat, half_lon, i)
            for i in range(4)
        ],
        args,
    )
    return hand_out(results)


def solution(mesh):
    tile = P("lat", "lon", None, None)
    return jax.shard_map(
        local,
        mesh=mesh,
        in_specs=(tile, P(), P(), P(), P(), P(), P(), P(), tile, tile),
        out_specs=(tile, tile, tile),
        check_vma=False,
    )
```

```python
import functools

import jax
import jax.numpy as jnp
from jax import lax
from jax.experimental import pallas as pl
from jax.experimental.pallas import tpu as pltpu
from jax.sharding import PartitionSpec as P

WLAT = 6
WLON = 12
PAIRS = 4
TOK = 144
FEAT = 512
EPS = 1e-05
BF = jnp.bfloat16
F32 = jnp.float32
MESH = pl.DeviceIdType.MESH
VMEM = 48 * 2**20
STRIPS = 3


def dot(a, b):
    return jnp.dot(a, b, preferred_element_type=F32)


def dot_t(a, b):
    return lax.dot_general(a, b, (((1,), (1,)), ((), ())), preferred_element_type=F32)


def t_dot(a, b):
    return lax.dot_general(a, b, (((0,), (0,)), ((), ())), preferred_element_type=F32)


def kernel(
    behind_lat, behind_lon, halo_lat, halo_lon,
    shift_lat_hbm, shift_lon, gain_attn_hbm, gain_merge_hbm,
    inputs, w_qkv_hbm, w_out_hbm, w_merge_hbm, cot_coarse_hbm, cot_skip_hbm,
    coarse_hbm, skip_hbm, grad_hbm,
    shift_lat, gain_attn, gain_merge,
    own, xtall, btall, gtall, xflat, gflat, xquad, gquad, bext, rext, gskip, skip, cot_skip, cot_coarse, coarse, out,
    w_qkv, w_out, w_merge,
    gm, merged, token, norm, rstd, proj, mixed, soft, dproj, bias,
    local_sem, out_sem, send_sem, recv_sem,
):
    rows, cols = own.shape[0], own.shape[1]
    lat, lon = lax.axis_index("lat"), lax.axis_index("lon")
    nlat, nlon = lax.axis_size("lat"), lax.axis_size("lon")
    band = rows * nlat
    li, lj = int(behind_lat), int(behind_lon)

    def device(step_lat, step_lon):
        return (lax.rem(lat + step_lat + nlat, nlat), lax.rem(lon + step_lon + nlon, nlon))

    dlat, dlon = 1 - 2 * li, 1 - 2 * lj
    steps = ((dlat, 0), (0, dlon), (dlat, dlon))
    own_r, own_c = li * halo_lat, lj * halo_lon
    halo_r, halo_c = (1 - li) * rows, (1 - lj) * cols
    back_r, back_c = (1 - li) * halo_lat, (1 - lj) * halo_lon
    bhalo_r, bhalo_c = li * rows, lj * cols
    edge_r, edge_c = li * (rows - halo_lat), lj * (cols - halo_lon)
    bedge_r, bedge_c = (1 - li) * (rows - halo_lat), (1 - lj) * (cols - halo_lon)

    def send(phase, i, source, src, target, dst, step_lat, step_lon):
        (r, c, n, m), (tr, tc) = src, dst
        return pltpu.make_async_remote_copy(
            src_ref=source.at[pl.ds(r, n), pl.ds(c, m)],
            dst_ref=target.at[pl.ds(tr, n), pl.ds(tc, m)],
            send_sem=send_sem.at[phase, i],
            recv_sem=recv_sem.at[phase, i],
            device_id=device(step_lat, step_lon),
            device_id_type=MESH,
        )

    far_r, far_c = (1 - li) * WLAT, (1 - lj) * WLON
    quad_r, quad_c = li * halo_lat, lj * halo_lon
    qhalo_r, qhalo_c = (1 - li) * WLAT, (1 - lj) * WLON

    def ahead(phase, source, tall, flat, quad):
        er, ec = edge_r, edge_c
        return (
            send(phase, 0, source, (er, 0, halo_lat, cols), tall, (halo_r, 0), -dlat, 0),
            send(phase, 1, source, (0, ec, rows, halo_lon), flat, (0, halo_c), 0, -dlon),
            send(phase, 2, source, (er, ec, halo_lat, halo_lon), quad, (qhalo_r, qhalo_c), -dlat, -dlon),
        )

    def back(phase, tall, at_c, wide):
        er, ec = back_r + bedge_r, back_c + bedge_c
        far_r, near_r = back_r + (1 - li) * WLAT, back_r + li * WLAT
        far_c, near_c = at_c + (1 - lj) * WLON, at_c + lj * WLON
        return (
            send(phase, 0, tall, (er, near_c, halo_lat, WLON), tall, (bhalo_r, near_c), dlat, 0),
            send(phase, 1, wide, (er, ec, halo_lat, halo_lon), wide, (bhalo_r, bhalo_c), dlat, dlon),
            send(phase, 2, wide, (far_r, ec, WLAT, halo_lon), wide, (far_r, bhalo_c), 0, dlon),
            send(phase, 3, tall, (er, far_c, halo_lat, WLON), tall, (bhalo_r, far_c), dlat, 0),
            send(phase, 4, wide, (near_r, ec, WLAT, halo_lon), wide, (near_r, bhalo_c), 0, dlon),
        )

    loads = [
        pltpu.make_async_copy(src, dst, local_sem.at[i])
        for i, (src, dst) in enumerate((
            (cot_coarse_hbm, cot_coarse),
            (w_merge_hbm, w_merge),
            (gain_attn_hbm, gain_attn),
            (inputs, own),
            (w_qkv_hbm, w_qkv),
            (w_out_hbm, w_out),
            (inputs, xtall.at[pl.ds(own_r, rows)]),
            (inputs, xflat.at[:, pl.ds(own_c, cols)]),
            (cot_skip_hbm, cot_skip),
            (gain_merge_hbm, gain_merge),
            (shift_lat_hbm, shift_lat),
        ))
    ]
    barrier = pltpu.get_barrier_semaphore()
    for sr, sc in steps:
        pl.semaphore_signal(barrier, inc=1, device_id=device(sr, sc), device_id_type=MESH)
        pl.semaphore_signal(barrier, inc=1, device_id=device(-sr, -sc), device_id_type=MESH)
    for load in loads:
        load.start()
    pl.semaphore_wait(barrier, 6)
    first = ahead(0, inputs, xtall, xflat, xquad)
    first[1].start()
    first[0].start()
    second = back(1, btall, 0, bext)
    third = ahead(2, gskip, gtall, gflat, gquad)
    fourth = back(3, rext, back_c, rext)

    loads[10].wait()
    s_lat, s_lon = shift_lat[0], shift_lon[0]
    t_lat = jnp.clip(s_lat - li * (WLAT - halo_lat), 0, halo_lat)
    t_lon = jnp.clip(s_lon - lj * (WLON - halo_lon), 0, halo_lon)

    low = lax.broadcasted_iota(jnp.int32, (TOK, 128), 1) < 64
    zero = jnp.zeros((TOK, 128), BF)

    def both(x):
        return jnp.concatenate([jnp.where(low, x, zero), jnp.where(low, zero, x)], 0)

    def unite(x):
        return jnp.where(low, x[:TOK], x[TOK:])

    start = lax.rem(rows * lat + WLAT * (1 - 2 * li) + band, band)
    edge = 2 * WLON * (band - s_lat - start)
    row_in = lax.broadcasted_iota(jnp.int32, (TOK, TOK), 0) >= edge
    col_in = lax.broadcasted_iota(jnp.int32, (TOK, TOK), 1) >= edge
    apart = jnp.where(row_in != col_in, F32(-1e30), F32(0.0))
    bias[0] = jnp.zeros((TOK, 2 * TOK), F32)
    bias[1] = jnp.concatenate([apart, apart], 1)

    def attend(i, across, p):
        at = p * 128
        q = both(proj[i, :, pl.ds(at, 128)] * BF(0.125))
        k = proj[i, :, pl.ds(FEAT + at, 128)]
        v = proj[i, :, pl.ds(2 * FEAT + at, 128)]
        scores = dot_t(k, q) + bias[across]
        e = jnp.exp(scores - jnp.max(scores, 0, keepdims=True))
        w = (e * (1.0 / jnp.sum(e, 0, keepdims=True))).astype(BF)
        soft[i, p] = w
        mixed[:, pl.ds(at, 128)] = unite(t_dot(w, v)).astype(BF)

    def attend_back(i, p):
        at = p * 128
        q = both(proj[i, :, pl.ds(at, 128)] * BF(0.125))
        k = proj[i, :, pl.ds(FEAT + at, 128)]
        v = proj[i, :, pl.ds(2 * FEAT + at, 128)]
        g = both(mixed[:, pl.ds(at, 128)])
        w = soft[i, p]
        dw = dot_t(v, g)
        wf = w.astype(F32)
        ds = (wf * (dw - jnp.sum(dw * wf, 0, keepdims=True))).astype(BF)
        dproj[:, pl.ds(at, 128)] = (unite(t_dot(ds, k)) * 0.125).astype(BF)
        dproj[:, pl.ds(FEAT + at, 128)] = dot(ds, q).astype(BF)
        dproj[:, pl.ds(2 * FEAT + at, 128)] = dot(w, g).astype(BF)

    def windows(forward, ready, local_ref, tall, flat, quad, results, copies):
        def step(i, carry):
            across_lat, across_lon = i % 2, i // 2
            wr = WLAT * (li + dlat * across_lat)
            wc = WLON * (lj + dlon * across_lon)

            @pl.when(i == 0)
            def _():
                x = local_ref[pl.ds(s_lat, WLAT), pl.ds(s_lon, WLON)]
                token[...] = x.reshape(TOK, FEAT)

            @pl.when(i == 1)
            def _():
                ready[0].wait_recv()
                x = tall[pl.ds(t_lat + wr, WLAT), pl.ds(s_lon, WLON)]
                token[...] = x.reshape(TOK, FEAT)

            @pl.when(i == 2)
            def _():
                ready[1].wait_recv()
                x = flat[pl.ds(s_lat, WLAT), pl.ds(t_lon + wc, WLON)]
                token[...] = x.reshape(TOK, FEAT)

            @pl.when(i == 3)
            def _():
                mine = (pl.ds(quad_r, WLAT), pl.ds(quad_c, WLON))
                quad[mine] = local_ref[pl.ds(far_r, WLAT), pl.ds(far_c, WLON)]
                quad[pl.ds(qhalo_r, halo_lat), mine[1]] = tall[
                    pl.ds(halo_r, halo_lat), pl.ds(far_c, WLON)
                ]
                quad[mine[0], pl.ds(qhalo_c, halo_lon)] = flat[
                    pl.ds(far_r, WLAT), pl.ds(halo_c, halo_lon)
                ]
                ready[2].wait_recv()
                x = quad[pl.ds(t_lat, WLAT), pl.ds(t_lon, WLON)]
                token[...] = x.reshape(TOK, FEAT)

            if forward:
                x = token[...].astype(F32)
                mean = jnp.mean(x, -1, keepdims=True)
                x = x - mean
                inv = lax.rsqrt(jnp.mean(x * x, -1, keepdims=True) + EPS)
                x = x * inv
                norm[i] = x
                rstd[i] = jnp.broadcast_to(inv, (TOK, 128))
                proj[i] = dot((x * gain_attn[...]).astype(BF), w_qkv[...]).astype(BF)
                for p in range(PAIRS):
                    attend(i, across_lat, p)
                result = dot(mixed[...], w_out[...]).astype(BF)
            else:
                mixed[...] = dot_t(token[...], w_out[...]).astype(BF)
                for p in range(PAIRS):
                    attend_back(i, p)
                d = dot_t(dproj[...], w_qkv[...]).astype(BF).astype(F32) * gain_attn[...]
                nn = norm[i]
                inv = rstd[i][:, :1]
                result = (inv * (
                    d - jnp.mean(d, -1, keepdims=True) - nn * jnp.mean(d * nn, -1, keepdims=True)
                )).astype(BF)
            result = result.reshape(WLAT, WLON, 2, FEAT)
            for ref, at_c in results:
                ref[pl.ds(back_r + wr, WLAT), pl.ds(at_c + wc, WLON)] = result
            for turn, part in ((1, copies[:1]), (2, copies[4:]), (3, copies[1:4])):
                @pl.when(i == turn)
                def _(part=part):
                    for copy in part:
                        copy.start()
            return carry

        lax.fori_loop(0, 4, step, 0)

    loads[0].wait()
    loads[1].wait()
    strip, slim = TOK // STRIPS, cols // STRIPS
    thin = slim // 2

    def quarter_back(j, carry):
        at = pl.multiple_of(j * FEAT, FEAT)
        x = jnp.concatenate(
            [cot_coarse[:, k * thin:(k + 1) * thin].reshape(strip, 2 * FEAT) for k in range(STRIPS)], 0
        )
        y = dot_t(x, w_merge[pl.ds(at, FEAT), :]).astype(BF)
        gm[:, :, pl.ds(at, FEAT)] = y.reshape(STRIPS, strip, FEAT)
        return carry

    lax.fori_loop(0, 4, quarter_back, 0)
    first[2].start()
    for load in loads[2:8]:
        load.wait()
    windows(True, first, own, xtall, xflat, xquad, ((btall, 0), (bext, back_c)), second)
    loads[8].wait()
    loads[9].wait()
    second[0].wait_recv()
    second[3].wait_recv()

    start_r, start_c = halo_lat - t_lat, halo_lon - t_lon
    width = 4 * FEAT
    patches = (rows // 2, 2, cols // 2, 2, 2, FEAT)
    quarters = [(a, b) for a in range(2) for b in range(2)]

    def merge(turn, carry):
        j = turn if lj else lax.rem(turn + 1, STRIPS)
        mine = pl.ds(slim * j, slim)

        @pl.when(turn < STRIPS - 1)
        def _():
            placed = btall[pl.ds(start_r, rows), pl.ds(start_c - back_c + slim * j, slim)]
            skip[:, mine] = (own[:, mine].astype(F32) + placed.astype(F32)).astype(BF)

        @pl.when(turn == STRIPS - 1)
        def _():
            for i in (1, 2, 4):
                second[i].wait_recv()
            bext[pl.ds(bhalo_r, halo_lat), pl.ds(back_c, cols)] = btall[pl.ds(bhalo_r, halo_lat)]
            placed = bext[pl.ds(start_r, rows), pl.ds(start_c + slim * j, slim)]
            skip[:, mine] = (own[:, mine].astype(F32) + placed.astype(F32)).astype(BF)

        def quarter(ref, a, b):
            return ref.reshape(*patches)[:, a, pl.ds(thin * j, thin), b].reshape(strip, FEAT)

        parts = [quarter(skip, a, b).astype(F32) for a, b in quarters]
        mean = sum(jnp.sum(x, -1, keepdims=True) for x in parts) / width
        parts = [x - mean for x in parts]
        inv = lax.rsqrt(sum(jnp.sum(x * x, -1, keepdims=True) for x in parts) / width + EPS)
        parts = [x * inv for x in parts]
        grads = []
        for i, x in enumerate(parts):
            gain = gain_merge[:, pl.ds(i * FEAT, FEAT)]
            merged[j, :, pl.ds(i * FEAT, FEAT)] = (x * gain).astype(BF)
            grads.append(gm[j, :, pl.ds(i * FEAT, FEAT)].astype(F32) * gain)
        mean_g = sum(jnp.sum(g, -1, keepdims=True) for g in grads) / width
        mean_gx = sum(jnp.sum(g * x, -1, keepdims=True) for g, x in zip(grads, parts)) / width
        for (a, b), g, x in zip(quarters, grads, parts):
            d = (inv * (g - mean_g - x * mean_gx)).astype(BF) + quarter(cot_skip, a, b)
            gskip.reshape(*patches)[:, a, pl.ds(thin * j, thin), b] = d.reshape(
                rows // 2, thin, 2, FEAT
            )
        return carry

    lax.fori_loop(0, STRIPS, merge, 0)
    third[1].start()
    third[0].start()
    gtall[pl.ds(own_r, rows)] = gskip[...]
    gflat[:, pl.ds(own_c, cols)] = gskip[...]
    skip_out = pltpu.make_async_copy(skip, skip_hbm, out_sem.at[0])
    skip_out.start()
    def coarse_part(j, carry):
        at = pl.multiple_of(j * FEAT, FEAT)
        x = merged.reshape(TOK, width)[...]
        y = dot(x, w_merge[:, pl.ds(at, FEAT)]).astype(BF)
        for k in range(STRIPS):
            coarse[:, k * thin:(k + 1) * thin, :, pl.ds(at, FEAT)] = y[
                k * strip:(k + 1) * strip
            ].reshape(rows // 2, thin, 2, FEAT)
        return carry

    lax.fori_loop(0, 2, coarse_part, 0)
    coarse_out = pltpu.make_async_copy(coarse, coarse_hbm, out_sem.at[1])
    coarse_out.start()
    third[2].start()
    windows(False, third, gskip, gtall, gflat, gquad, ((rext, back_c),), fourth)
    for copy in fourth:
        copy.wait_recv()

    def finish(j, carry):
        mine = pl.ds(4 * j, 4)
        out[mine] = gskip[mine] + rext[pl.ds(start_r + 4 * j, 4), pl.ds(start_c, cols)]
        return carry

    lax.fori_loop(0, rows // 4, finish, 0)
    grad_out = pltpu.make_async_copy(out, grad_hbm, out_sem.at[2])
    grad_out.start()
    for copy in first + second + third + fourth:
        copy.wait_send()
    skip_out.wait()
    coarse_out.wait()
    grad_out.wait()


def block(behind_lat, behind_lon, halo_lat, halo_lon, ident, args):
    (inputs, shift_lat, shift_lon, gain_attn, w_qkv, w_out, gain_merge, w_merge,
     cot_coarse, cot_skip) = args
    rows, cols, lev, feat = inputs.shape
    wide = (rows + halo_lat, cols + halo_lon, lev, feat)
    smem = pl.BlockSpec(memory_space=pltpu.SMEM)
    hbm = pl.BlockSpec(memory_space=pltpu.HBM)
    anyw = pl.BlockSpec(memory_space=pl.ANY)
    tile, coarse = pltpu.VMEM(inputs.shape, BF), pltpu.VMEM(cot_coarse.shape, BF)
    tall = pltpu.VMEM((rows + halo_lat, cols, lev, feat), BF)
    flat = pltpu.VMEM((rows, cols + halo_lon, lev, feat), BF)
    quad = pltpu.VMEM((WLAT + halo_lat, WLON + halo_lon, lev, feat), BF)
    return pl.pallas_call(
        functools.partial(kernel, behind_lat, behind_lon, halo_lat, halo_lon),
        out_shape=(
            jax.ShapeDtypeStruct(cot_coarse.shape, BF),
            jax.ShapeDtypeStruct(inputs.shape, BF),
            jax.ShapeDtypeStruct(inputs.shape, BF),
        ),
        in_specs=[hbm, smem] + [hbm] * 8,
        out_specs=(anyw, anyw, anyw),
        scratch_shapes=[
            pltpu.SMEM((1,), jnp.int32),
            pltpu.VMEM((1, feat), F32),
            pltpu.VMEM((1, 4 * feat), F32),
            tile,
            tall, tall, tall, flat, flat, quad, quad,
            pltpu.VMEM(wide, BF),
            pltpu.VMEM(wide, BF),
            tile, tile, tile, coarse, coarse, tile,
            pltpu.VMEM(w_qkv.shape, BF),
            pltpu.VMEM(w_out.shape, BF),
            pltpu.VMEM(w_merge.shape, BF),
            pltpu.VMEM((STRIPS, TOK // STRIPS, 4 * FEAT), BF),
            pltpu.VMEM((STRIPS, TOK // STRIPS, 4 * FEAT), BF),
            pltpu.VMEM((TOK, FEAT), BF),
            pltpu.VMEM((4, TOK, FEAT), F32),
            pltpu.VMEM((4, TOK, 128), F32),
            pltpu.VMEM((4, TOK, 3 * FEAT), BF),
            pltpu.VMEM((TOK, FEAT), BF),
            pltpu.VMEM((4, PAIRS, TOK, 2 * TOK), BF),
            pltpu.VMEM((TOK, 3 * FEAT), BF),
            pltpu.VMEM((2, TOK, 2 * TOK), F32),
            pltpu.SemaphoreType.DMA((11,)),
            pltpu.SemaphoreType.DMA((3,)),
            pltpu.SemaphoreType.DMA((4, 5)),
            pltpu.SemaphoreType.DMA((4, 5)),
        ],
        compiler_params=pltpu.CompilerParams(
            collective_id=ident, has_side_effects=True, vmem_limit_bytes=VMEM
        ),
    )(
        shift_lat, shift_lon, gain_attn.reshape(1, -1), gain_merge.reshape(1, -1),
        inputs, w_qkv, w_out, w_merge, cot_coarse, cot_skip,
    )


def deliver(coarse, skip, grad, coarse_hbm, skip_hbm, grad_hbm, sem):
    copies = [
        pltpu.make_async_copy(src, dst, sem.at[i])
        for i, (src, dst) in enumerate(((coarse, coarse_hbm), (skip, skip_hbm), (grad, grad_hbm)))
    ]
    for copy in copies:
        copy.start()
    for copy in copies:
        copy.wait()


def hand_out(results):
    anyw = pl.BlockSpec(memory_space=pl.ANY)
    return pl.pallas_call(
        deliver,
        out_shape=tuple(jax.ShapeDtypeStruct(x.shape, x.dtype) for x in results),
        in_specs=[anyw] * 3,
        out_specs=(pl.BlockSpec(memory_space=pltpu.HBM),) * 3,
        scratch_shapes=[pltpu.SemaphoreType.DMA((3,))],
    )(*results)


def local(*args):
    half = WLON // 2
    shift = args[2][0]
    behind = (shift > half).astype(jnp.int32)
    narrow = (jnp.minimum(shift, WLON - shift) <= half // 2).astype(jnp.int32)
    results = lax.switch(
        2 * narrow + behind,
        [
            functools.partial(block, False, bool(i % 2), WLAT - 1, half // (1 + i // 2), i)
            for i in range(4)
        ],
        args,
    )
    return hand_out(results)


def solution(mesh):
    tile = P("lat", "lon", None, None)
    return jax.shard_map(
        local,
        mesh=mesh,
        in_specs=(tile, P(), P(), P(), P(), P(), P(), P(), tile, tile),
        out_specs=(tile, tile, tile),
        check_vma=False,
    )
```

```python
import functools

import jax
import jax.numpy as jnp
from jax import lax
from jax.experimental import pallas as pl
from jax.experimental.pallas import tpu as pltpu
from jax.sharding import PartitionSpec as P

WLAT = 6
WLON = 12
PAIRS = 4
TOK = 144
FEAT = 512
EPS = 1e-05
BF = jnp.bfloat16
F32 = jnp.float32
MESH = pl.DeviceIdType.MESH
VMEM = 48 * 2**20
STRIPS = 3


def dot(a, b):
    return jnp.dot(a, b, preferred_element_type=F32)


def dot_t(a, b):
    return lax.dot_general(a, b, (((1,), (1,)), ((), ())), preferred_element_type=F32)


def t_dot(a, b):
    return lax.dot_general(a, b, (((0,), (0,)), ((), ())), preferred_element_type=F32)


def kernel(
    behind_lat, behind_lon, halo_lat, halo_lon,
    shift_lat_hbm, shift_lon, gain_attn_hbm, gain_merge_hbm,
    inputs, w_qkv_hbm, w_out_hbm, w_merge_hbm, cot_coarse_hbm, cot_skip_hbm,
    coarse_hbm, skip_hbm, grad_hbm,
    shift_lat, gain_attn, gain_merge,
    own, xtall, btall, gtall, xflat, gflat, xquad, gquad, bext, rext, gskip, skip, cot_skip, cot_coarse, coarse, out,
    w_qkv, w_out, w_merge,
    gm, merged, token, norm, rstd, proj, mixed, soft, dproj, bias,
    local_sem, out_sem, send_sem, recv_sem,
):
    rows, cols = own.shape[0], own.shape[1]
    lat, lon = lax.axis_index("lat"), lax.axis_index("lon")
    nlat, nlon = lax.axis_size("lat"), lax.axis_size("lon")
    band = rows * nlat
    li, lj = int(behind_lat), int(behind_lon)

    def device(step_lat, step_lon):
        return (lax.rem(lat + step_lat + nlat, nlat), lax.rem(lon + step_lon + nlon, nlon))

    dlat, dlon = 1 - 2 * li, 1 - 2 * lj
    steps = ((dlat, 0), (0, dlon), (dlat, dlon))
    own_r, own_c = li * halo_lat, lj * halo_lon
    halo_r, halo_c = (1 - li) * rows, (1 - lj) * cols
    back_r, back_c = (1 - li) * halo_lat, (1 - lj) * halo_lon
    bhalo_r, bhalo_c = li * rows, lj * cols
    edge_r, edge_c = li * (rows - halo_lat), lj * (cols - halo_lon)
    bedge_r, bedge_c = (1 - li) * (rows - halo_lat), (1 - lj) * (cols - halo_lon)

    def send(phase, i, source, src, target, dst, step_lat, step_lon):
        (r, c, n, m), (tr, tc) = src, dst
        return pltpu.make_async_remote_copy(
            src_ref=source.at[pl.ds(r, n), pl.ds(c, m)],
            dst_ref=target.at[pl.ds(tr, n), pl.ds(tc, m)],
            send_sem=send_sem.at[phase, i],
            recv_sem=recv_sem.at[phase, i],
            device_id=device(step_lat, step_lon),
            device_id_type=MESH,
        )

    far_r, far_c = (1 - li) * WLAT, (1 - lj) * WLON
    quad_r, quad_c = li * halo_lat, lj * halo_lon
    qhalo_r, qhalo_c = (1 - li) * WLAT, (1 - lj) * WLON

    def ahead(phase, source, tall, flat, quad):
        er, ec = edge_r, edge_c
        return (
            send(phase, 0, source, (er, 0, halo_lat, cols), tall, (halo_r, 0), -dlat, 0),
            send(phase, 1, source, (0, ec, rows, halo_lon), flat, (0, halo_c), 0, -dlon),
            send(phase, 2, source, (er, ec, halo_lat, halo_lon), quad, (qhalo_r, qhalo_c), -dlat, -dlon),
        )

    def back(phase, tall, at_c, wide):
        er, ec = back_r + bedge_r, back_c + bedge_c
        far_r, near_r = back_r + (1 - li) * WLAT, back_r + li * WLAT
        far_c, near_c = at_c + (1 - lj) * WLON, at_c + lj * WLON
        return (
            send(phase, 0, tall, (er, near_c, halo_lat, WLON), tall, (bhalo_r, near_c), dlat, 0),
            send(phase, 1, wide, (er, ec, halo_lat, halo_lon), wide, (bhalo_r, bhalo_c), dlat, dlon),
            send(phase, 2, wide, (far_r, ec, WLAT, halo_lon), wide, (far_r, bhalo_c), 0, dlon),
            send(phase, 3, tall, (er, far_c, halo_lat, WLON), tall, (bhalo_r, far_c), dlat, 0),
            send(phase, 4, wide, (near_r, ec, WLAT, halo_lon), wide, (near_r, bhalo_c), 0, dlon),
        )

    loads = [
        pltpu.make_async_copy(src, dst, local_sem.at[i])
        for i, (src, dst) in enumerate((
            (cot_coarse_hbm, cot_coarse),
            (w_merge_hbm, w_merge),
            (gain_attn_hbm, gain_attn),
            (inputs, own),
            (w_qkv_hbm, w_qkv),
            (w_out_hbm, w_out),
            (inputs, xtall.at[pl.ds(own_r, rows)]),
            (inputs, xflat.at[:, pl.ds(own_c, cols)]),
            (cot_skip_hbm, cot_skip),
            (gain_merge_hbm, gain_merge),
            (shift_lat_hbm, shift_lat),
        ))
    ]
    barrier = pltpu.get_barrier_semaphore()
    for sr, sc in steps:
        pl.semaphore_signal(barrier, inc=1, device_id=device(sr, sc), device_id_type=MESH)
        pl.semaphore_signal(barrier, inc=1, device_id=device(-sr, -sc), device_id_type=MESH)
    for load in loads:
        load.start()
    pl.semaphore_wait(barrier, 6)
    first = ahead(0, inputs, xtall, xflat, xquad)
    first[1].start()
    first[0].start()
    second = back(1, btall, 0, bext)
    third = ahead(2, gskip, gtall, gflat, gquad)
    fourth = back(3, rext, back_c, rext)

    loads[10].wait()
    s_lat, s_lon = shift_lat[0], shift_lon[0]
    t_lat = jnp.clip(s_lat - li * (WLAT - halo_lat), 0, halo_lat)
    t_lon = jnp.clip(s_lon - lj * (WLON - halo_lon), 0, halo_lon)

    low = lax.broadcasted_iota(jnp.int32, (TOK, 128), 1) < 64
    zero = jnp.zeros((TOK, 128), BF)

    def both(x):
        return jnp.concatenate([jnp.where(low, x, zero), jnp.where(low, zero, x)], 0)

    def unite(x):
        return jnp.where(low, x[:TOK], x[TOK:])

    start = lax.rem(rows * lat + WLAT * (1 - 2 * li) + band, band)
    edge = 2 * WLON * (band - s_lat - start)
    row_in = lax.broadcasted_iota(jnp.int32, (TOK, TOK), 0) >= edge
    col_in = lax.broadcasted_iota(jnp.int32, (TOK, TOK), 1) >= edge
    apart = jnp.where(row_in != col_in, F32(-1e30), F32(0.0))
    bias[0] = jnp.zeros((TOK, 2 * TOK), F32)
    bias[1] = jnp.concatenate([apart, apart], 1)

    def attend(i, across, p):
        at = p * 128
        q = both(proj[i, :, pl.ds(at, 128)] * BF(0.125))
        k = proj[i, :, pl.ds(FEAT + at, 128)]
        v = proj[i, :, pl.ds(2 * FEAT + at, 128)]
        scores = dot_t(k, q) + bias[across]
        e = jnp.exp(scores - jnp.max(scores, 0, keepdims=True))
        w = (e * (1.0 / jnp.sum(e, 0, keepdims=True))).astype(BF)
        soft[i, p // 2, :, pl.ds(p % 2 * 2 * TOK, 2 * TOK)] = w
        mixed[:, pl.ds(at, 128)] = unite(t_dot(w, v)).astype(BF)

    head_of = lax.broadcasted_iota(jnp.int32, (TOK, 256), 1) // 64
    zeros = jnp.zeros((TOK, 256), BF)

    def four(x):
        return jnp.concatenate([jnp.where(head_of == h, x, zeros) for h in range(4)], 0)

    def attend_back(i, p):
        at = p * 256
        q = four(proj[i, :, pl.ds(at, 256)] * BF(0.125))
        k = proj[i, :, pl.ds(FEAT + at, 256)]
        v = proj[i, :, pl.ds(2 * FEAT + at, 256)]
        g = four(mixed[:, pl.ds(at, 256)])
        w = soft[i, p]
        dw = dot_t(v, g)
        wf = w.astype(F32)
        ds = (wf * (dw - jnp.sum(dw * wf, 0, keepdims=True))).astype(BF)
        d = t_dot(ds, k)
        dq = d[:TOK]
        for h in range(1, 4):
            dq = jnp.where(head_of == h, d[h * TOK:(h + 1) * TOK], dq)
        dproj[:, pl.ds(at, 256)] = (dq * 0.125).astype(BF)
        dproj[:, pl.ds(FEAT + at, 256)] = dot(ds, q).astype(BF)
        dproj[:, pl.ds(2 * FEAT + at, 256)] = dot(w, g).astype(BF)

    def windows(forward, ready, local_ref, tall, flat, quad, results, copies):
        def step(i, carry):
            across_lat, across_lon = i % 2, i // 2
            wr = WLAT * (li + dlat * across_lat)
            wc = WLON * (lj + dlon * across_lon)

            @pl.when(i == 0)
            def _():
                x = local_ref[pl.ds(s_lat, WLAT), pl.ds(s_lon, WLON)]
                token[...] = x.reshape(TOK, FEAT)

            @pl.when(i == 1)
            def _():
                ready[0].wait_recv()
                x = tall[pl.ds(t_lat + wr, WLAT), pl.ds(s_lon, WLON)]
                token[...] = x.reshape(TOK, FEAT)

            @pl.when(i == 2)
            def _():
                ready[1].wait_recv()
                x = flat[pl.ds(s_lat, WLAT), pl.ds(t_lon + wc, WLON)]
                token[...] = x.reshape(TOK, FEAT)

            @pl.when(i == 3)
            def _():
                mine = (pl.ds(quad_r, WLAT), pl.ds(quad_c, WLON))
                quad[mine] = local_ref[pl.ds(far_r, WLAT), pl.ds(far_c, WLON)]
                quad[pl.ds(qhalo_r, halo_lat), mine[1]] = tall[
                    pl.ds(halo_r, halo_lat), pl.ds(far_c, WLON)
                ]
                quad[mine[0], pl.ds(qhalo_c, halo_lon)] = flat[
                    pl.ds(far_r, WLAT), pl.ds(halo_c, halo_lon)
                ]
                ready[2].wait_recv()
                x = quad[pl.ds(t_lat, WLAT), pl.ds(t_lon, WLON)]
                token[...] = x.reshape(TOK, FEAT)

            if forward:
                x = token[...].astype(F32)
                mean = jnp.mean(x, -1, keepdims=True)
                x = x - mean
                inv = lax.rsqrt(jnp.mean(x * x, -1, keepdims=True) + EPS)
                x = x * inv
                norm[i] = x
                rstd[i] = jnp.broadcast_to(inv, (TOK, 128))
                proj[i] = dot((x * gain_attn[...]).astype(BF), w_qkv[...]).astype(BF)
                for p in range(PAIRS):
                    attend(i, across_lat, p)
                result = dot(mixed[...], w_out[...]).astype(BF)
            else:
                mixed[...] = dot_t(token[...], w_out[...]).astype(BF)
                for p in range(PAIRS // 2):
                    attend_back(i, p)
                d = dot_t(dproj[...], w_qkv[...]).astype(BF).astype(F32) * gain_attn[...]
                nn = norm[i]
                inv = rstd[i][:, :1]
                result = (inv * (
                    d - jnp.mean(d, -1, keepdims=True) - nn * jnp.mean(d * nn, -1, keepdims=True)
                )).astype(BF)
            result = result.reshape(WLAT, WLON, 2, FEAT)
            for ref, at_c in results:
                ref[pl.ds(back_r + wr, WLAT), pl.ds(at_c + wc, WLON)] = result
            for turn, part in ((1, copies[:1]), (2, copies[4:]), (3, copies[1:4])):
                @pl.when(i == turn)
                def _(part=part):
                    for copy in part:
                        copy.start()
            return carry

        lax.fori_loop(0, 4, step, 0)

    loads[0].wait()
    loads[1].wait()
    strip, slim = TOK // STRIPS, cols // STRIPS
    thin = slim // 2

    def quarter_back(j, carry):
        at = pl.multiple_of(j * FEAT, FEAT)
        x = jnp.concatenate(
            [cot_coarse[:, k * thin:(k + 1) * thin].reshape(strip, 2 * FEAT) for k in range(STRIPS)], 0
        )
        y = dot_t(x, w_merge[pl.ds(at, FEAT), :]).astype(BF)
        gm[:, :, pl.ds(at, FEAT)] = y.reshape(STRIPS, strip, FEAT)
        return carry

    lax.fori_loop(0, 4, quarter_back, 0)
    first[2].start()
    for load in loads[2:8]:
        load.wait()
    windows(True, first, own, xtall, xflat, xquad, ((btall, 0), (bext, back_c)), second)
    loads[8].wait()
    loads[9].wait()
    second[0].wait_recv()
    second[3].wait_recv()

    start_r, start_c = halo_lat - t_lat, halo_lon - t_lon
    width = 4 * FEAT
    patches = (rows // 2, 2, cols // 2, 2, 2, FEAT)
    quarters = [(a, b) for a in range(2) for b in range(2)]

    def merge(turn, carry):
        j = turn if lj else lax.rem(turn + 1, STRIPS)
        mine = pl.ds(slim * j, slim)

        @pl.when(turn < STRIPS - 1)
        def _():
            placed = btall[pl.ds(start_r, rows), pl.ds(start_c - back_c + slim * j, slim)]
            skip[:, mine] = (own[:, mine].astype(F32) + placed.astype(F32)).astype(BF)

        @pl.when(turn == STRIPS - 1)
        def _():
            for i in (1, 2, 4):
                second[i].wait_recv()
            bext[pl.ds(bhalo_r, halo_lat), pl.ds(back_c, cols)] = btall[pl.ds(bhalo_r, halo_lat)]
            placed = bext[pl.ds(start_r, rows), pl.ds(start_c + slim * j, slim)]
            skip[:, mine] = (own[:, mine].astype(F32) + placed.astype(F32)).astype(BF)

        def quarter(ref, a, b):
            return ref.reshape(*patches)[:, a, pl.ds(thin * j, thin), b].reshape(strip, FEAT)

        parts = [quarter(skip, a, b).astype(F32) for a, b in quarters]
        mean = sum(jnp.sum(x, -1, keepdims=True) for x in parts) / width
        parts = [x - mean for x in parts]
        inv = lax.rsqrt(sum(jnp.sum(x * x, -1, keepdims=True) for x in parts) / width + EPS)
        parts = [x * inv for x in parts]
        grads = []
        for i, x in enumerate(parts):
            gain = gain_merge[:, pl.ds(i * FEAT, FEAT)]
            merged[j, :, pl.ds(i * FEAT, FEAT)] = (x * gain).astype(BF)
            grads.append(gm[j, :, pl.ds(i * FEAT, FEAT)].astype(F32) * gain)
        mean_g = sum(jnp.sum(g, -1, keepdims=True) for g in grads) / width
        mean_gx = sum(jnp.sum(g * x, -1, keepdims=True) for g, x in zip(grads, parts)) / width
        for (a, b), g, x in zip(quarters, grads, parts):
            d = (inv * (g - mean_g - x * mean_gx)).astype(BF) + quarter(cot_skip, a, b)
            gskip.reshape(*patches)[:, a, pl.ds(thin * j, thin), b] = d.reshape(
                rows // 2, thin, 2, FEAT
            )
        return carry

    lax.fori_loop(0, STRIPS, merge, 0)
    third[1].start()
    third[0].start()
    gtall[pl.ds(own_r, rows)] = gskip[...]
    gflat[:, pl.ds(own_c, cols)] = gskip[...]
    skip_out = pltpu.make_async_copy(skip, skip_hbm, out_sem.at[0])
    skip_out.start()
    def coarse_part(j, carry):
        at = pl.multiple_of(j * FEAT, FEAT)
        x = merged.reshape(TOK, width)[...]
        y = dot(x, w_merge[:, pl.ds(at, FEAT)]).astype(BF)
        for k in range(STRIPS):
            coarse[:, k * thin:(k + 1) * thin, :, pl.ds(at, FEAT)] = y[
                k * strip:(k + 1) * strip
            ].reshape(rows // 2, thin, 2, FEAT)
        return carry

    lax.fori_loop(0, 2, coarse_part, 0)
    coarse_out = pltpu.make_async_copy(coarse, coarse_hbm, out_sem.at[1])
    coarse_out.start()
    third[2].start()
    windows(False, third, gskip, gtall, gflat, gquad, ((rext, back_c),), fourth)
    for copy in fourth:
        copy.wait_recv()

    def grad_out(j):
        mine = pl.ds(4 * j, 4)
        return pltpu.make_async_copy(out.at[mine], grad_hbm.at[mine], out_sem.at[2 + j])

    def finish(j, carry):
        mine = pl.ds(4 * j, 4)
        out[mine] = gskip[mine] + rext[pl.ds(start_r + 4 * j, 4), pl.ds(start_c, cols)]
        grad_out(j).start()
        return carry

    lax.fori_loop(0, rows // 4, finish, 0)
    for copy in first + second + third + fourth:
        copy.wait_send()
    skip_out.wait()
    coarse_out.wait()
    for j in range(rows // 4):
        grad_out(j).wait()


def block(behind_lat, behind_lon, halo_lat, halo_lon, ident, args):
    (inputs, shift_lat, shift_lon, gain_attn, w_qkv, w_out, gain_merge, w_merge,
     cot_coarse, cot_skip) = args
    rows, cols, lev, feat = inputs.shape
    wide = (rows + halo_lat, cols + halo_lon, lev, feat)
    smem = pl.BlockSpec(memory_space=pltpu.SMEM)
    hbm = pl.BlockSpec(memory_space=pltpu.HBM)
    anyw = pl.BlockSpec(memory_space=pl.ANY)
    tile, coarse = pltpu.VMEM(inputs.shape, BF), pltpu.VMEM(cot_coarse.shape, BF)
    tall = pltpu.VMEM((rows + halo_lat, cols, lev, feat), BF)
    flat = pltpu.VMEM((rows, cols + halo_lon, lev, feat), BF)
    quad = pltpu.VMEM((WLAT + halo_lat, WLON + halo_lon, lev, feat), BF)
    return pl.pallas_call(
        functools.partial(kernel, behind_lat, behind_lon, halo_lat, halo_lon),
        out_shape=(
            jax.ShapeDtypeStruct(cot_coarse.shape, BF),
            jax.ShapeDtypeStruct(inputs.shape, BF),
            jax.ShapeDtypeStruct(inputs.shape, BF),
        ),
        in_specs=[hbm, smem] + [hbm] * 8,
        out_specs=(anyw, anyw, anyw),
        scratch_shapes=[
            pltpu.SMEM((1,), jnp.int32),
            pltpu.VMEM((1, feat), F32),
            pltpu.VMEM((1, 4 * feat), F32),
            tile,
            tall, tall, tall, flat, flat, quad, quad,
            pltpu.VMEM(wide, BF),
            pltpu.VMEM(wide, BF),
            tile, tile, tile, coarse, coarse, tile,
            pltpu.VMEM(w_qkv.shape, BF),
            pltpu.VMEM(w_out.shape, BF),
            pltpu.VMEM(w_merge.shape, BF),
            pltpu.VMEM((STRIPS, TOK // STRIPS, 4 * FEAT), BF),
            pltpu.VMEM((STRIPS, TOK // STRIPS, 4 * FEAT), BF),
            pltpu.VMEM((TOK, FEAT), BF),
            pltpu.VMEM((4, TOK, FEAT), F32),
            pltpu.VMEM((4, TOK, 128), F32),
            pltpu.VMEM((4, TOK, 3 * FEAT), BF),
            pltpu.VMEM((TOK, FEAT), BF),
            pltpu.VMEM((4, PAIRS // 2, TOK, 4 * TOK), BF),
            pltpu.VMEM((TOK, 3 * FEAT), BF),
            pltpu.VMEM((2, TOK, 2 * TOK), F32),
            pltpu.SemaphoreType.DMA((11,)),
            pltpu.SemaphoreType.DMA((2 + rows // 4,)),
            pltpu.SemaphoreType.DMA((4, 5)),
            pltpu.SemaphoreType.DMA((4, 5)),
        ],
        compiler_params=pltpu.CompilerParams(
            collective_id=ident, has_side_effects=True, vmem_limit_bytes=VMEM
        ),
    )(
        shift_lat, shift_lon, gain_attn.reshape(1, -1), gain_merge.reshape(1, -1),
        inputs, w_qkv, w_out, w_merge, cot_coarse, cot_skip,
    )


def deliver(coarse, skip, grad, coarse_hbm, skip_hbm, grad_hbm, sem):
    copies = [
        pltpu.make_async_copy(src, dst, sem.at[i])
        for i, (src, dst) in enumerate(((coarse, coarse_hbm), (skip, skip_hbm), (grad, grad_hbm)))
    ]
    for copy in copies:
        copy.start()
    for copy in copies:
        copy.wait()


def hand_out(results):
    anyw = pl.BlockSpec(memory_space=pl.ANY)
    return pl.pallas_call(
        deliver,
        out_shape=tuple(jax.ShapeDtypeStruct(x.shape, x.dtype) for x in results),
        in_specs=[anyw] * 3,
        out_specs=(pl.BlockSpec(memory_space=pltpu.HBM),) * 3,
        scratch_shapes=[pltpu.SemaphoreType.DMA((3,))],
    )(*results)


def local(*args):
    half = WLON // 2
    shift = args[2][0]
    behind = (shift > half).astype(jnp.int32)
    narrow = (jnp.minimum(shift, WLON - shift) <= half // 2).astype(jnp.int32)
    results = lax.switch(
        2 * narrow + behind,
        [
            functools.partial(block, False, bool(i % 2), WLAT - 1, half // (1 + i // 2), i)
            for i in range(4)
        ],
        args,
    )
    return hand_out(results)


def solution(mesh):
    tile = P("lat", "lon", None, None)
    return jax.shard_map(
        local,
        mesh=mesh,
        in_specs=(tile, P(), P(), P(), P(), P(), P(), P(), tile, tile),
        out_specs=(tile, tile, tile),
        check_vma=False,
    )
```

```python
import functools

import jax
import jax.numpy as jnp
from jax import lax
from jax.experimental import pallas as pl
from jax.experimental.pallas import tpu as pltpu
from jax.sharding import PartitionSpec as P

WLAT = 6
WLON = 12
PAIRS = 4
TOK = 144
FEAT = 512
EPS = 1e-05
BF = jnp.bfloat16
F32 = jnp.float32
MESH = pl.DeviceIdType.MESH
VMEM = 48 * 2**20
STRIPS = 3


def dot(a, b):
    return jnp.dot(a, b, preferred_element_type=F32)


def dot_t(a, b):
    return lax.dot_general(a, b, (((1,), (1,)), ((), ())), preferred_element_type=F32)


def t_dot(a, b):
    return lax.dot_general(a, b, (((0,), (0,)), ((), ())), preferred_element_type=F32)


def kernel(
    behind_lat, behind_lon, halo_lat, halo_lon,
    shift_lat_hbm, shift_lon, gain_attn_hbm, gain_merge_hbm,
    inputs, w_qkv_hbm, w_out_hbm, w_merge_hbm, cot_coarse_hbm, cot_skip_hbm,
    coarse_hbm, skip_hbm, grad_hbm,
    shift_lat, gain_attn, gain_merge,
    own, xtall, btall, gtall, xflat, gflat, xquad, gquad, bext, rext, gskip, skip, cot_skip, cot_coarse, coarse, out,
    w_qkv, w_out, w_merge,
    gm, merged, token, norm, rstd, proj, mixed, soft, dproj, bias,
    local_sem, out_sem, send_sem, recv_sem,
):
    rows, cols = own.shape[0], own.shape[1]
    lat, lon = lax.axis_index("lat"), lax.axis_index("lon")
    nlat, nlon = lax.axis_size("lat"), lax.axis_size("lon")
    band = rows * nlat
    li, lj = int(behind_lat), int(behind_lon)

    def device(step_lat, step_lon):
        return (lax.rem(lat + step_lat + nlat, nlat), lax.rem(lon + step_lon + nlon, nlon))

    dlat, dlon = 1 - 2 * li, 1 - 2 * lj
    steps = ((dlat, 0), (0, dlon), (dlat, dlon))
    own_r, own_c = li * halo_lat, lj * halo_lon
    halo_r, halo_c = (1 - li) * rows, (1 - lj) * cols
    back_r, back_c = (1 - li) * halo_lat, (1 - lj) * halo_lon
    bhalo_r, bhalo_c = li * rows, lj * cols
    edge_r, edge_c = li * (rows - halo_lat), lj * (cols - halo_lon)
    bedge_r, bedge_c = (1 - li) * (rows - halo_lat), (1 - lj) * (cols - halo_lon)

    def send(phase, i, source, src, target, dst, step_lat, step_lon):
        (r, c, n, m), (tr, tc) = src, dst
        return pltpu.make_async_remote_copy(
            src_ref=source.at[pl.ds(r, n), pl.ds(c, m)],
            dst_ref=target.at[pl.ds(tr, n), pl.ds(tc, m)],
            send_sem=send_sem.at[phase, i],
            recv_sem=recv_sem.at[phase, i],
            device_id=device(step_lat, step_lon),
            device_id_type=MESH,
        )

    far_r, far_c = (1 - li) * WLAT, (1 - lj) * WLON
    quad_r, quad_c = li * halo_lat, lj * halo_lon
    qhalo_r, qhalo_c = (1 - li) * WLAT, (1 - lj) * WLON

    def ahead(phase, source, tall, flat, quad):
        er, ec = edge_r, edge_c
        return (
            send(phase, 0, source, (er, 0, halo_lat, cols), tall, (halo_r, 0), -dlat, 0),
            send(phase, 1, source, (0, ec, rows, halo_lon), flat, (0, halo_c), 0, -dlon),
            send(phase, 2, source, (er, ec, halo_lat, halo_lon), quad, (qhalo_r, qhalo_c), -dlat, -dlon),
        )

    def back(phase, tall, at_c, wide):
        er, ec = back_r + bedge_r, back_c + bedge_c
        far_r, near_r = back_r + (1 - li) * WLAT, back_r + li * WLAT
        far_c, near_c = at_c + (1 - lj) * WLON, at_c + lj * WLON
        return (
            send(phase, 0, tall, (er, near_c, halo_lat, WLON), tall, (bhalo_r, near_c), dlat, 0),
            send(phase, 1, wide, (er, ec, halo_lat, halo_lon), wide, (bhalo_r, bhalo_c), dlat, dlon),
            send(phase, 2, wide, (far_r, ec, WLAT, halo_lon), wide, (far_r, bhalo_c), 0, dlon),
            send(phase, 3, tall, (er, far_c, halo_lat, WLON), tall, (bhalo_r, far_c), dlat, 0),
            send(phase, 4, wide, (near_r, ec, WLAT, halo_lon), wide, (near_r, bhalo_c), 0, dlon),
        )

    loads = [
        pltpu.make_async_copy(src, dst, local_sem.at[i])
        for i, (src, dst) in enumerate((
            (cot_coarse_hbm, cot_coarse),
            (w_merge_hbm, w_merge),
            (gain_attn_hbm, gain_attn),
            (inputs, own),
            (w_qkv_hbm, w_qkv),
            (w_out_hbm, w_out),
            (inputs, xtall.at[pl.ds(own_r, rows)]),
            (inputs, xflat.at[:, pl.ds(own_c, cols)]),
            (cot_skip_hbm, cot_skip),
            (gain_merge_hbm, gain_merge),
            (shift_lat_hbm, shift_lat),
        ))
    ]
    barrier = pltpu.get_barrier_semaphore()
    for sr, sc in steps:
        pl.semaphore_signal(barrier, inc=1, device_id=device(sr, sc), device_id_type=MESH)
        pl.semaphore_signal(barrier, inc=1, device_id=device(-sr, -sc), device_id_type=MESH)
    for load in loads:
        load.start()
    pl.semaphore_wait(barrier, 6)
    first = ahead(0, inputs, xtall, xflat, xquad)
    first[1].start()
    first[0].start()
    second = back(1, btall, 0, bext)
    third = ahead(2, gskip, gtall, gflat, gquad)
    fourth = back(3, rext, back_c, rext)

    loads[10].wait()
    s_lat, s_lon = shift_lat[0], shift_lon[0]
    t_lat = jnp.clip(s_lat - li * (WLAT - halo_lat), 0, halo_lat)
    t_lon = jnp.clip(s_lon - lj * (WLON - halo_lon), 0, halo_lon)

    low = lax.broadcasted_iota(jnp.int32, (TOK, 128), 1) < 64
    zero = jnp.zeros((TOK, 128), BF)

    def both(x):
        return jnp.concatenate([jnp.where(low, x, zero), jnp.where(low, zero, x)], 0)

    def unite(x):
        return jnp.where(low, x[:TOK], x[TOK:])

    start = lax.rem(rows * lat + WLAT * (1 - 2 * li) + band, band)
    edge = 2 * WLON * (band - s_lat - start)
    row_in = lax.broadcasted_iota(jnp.int32, (TOK, TOK), 0) >= edge
    col_in = lax.broadcasted_iota(jnp.int32, (TOK, TOK), 1) >= edge
    apart = jnp.where(row_in != col_in, F32(-1e30), F32(0.0))
    bias[0] = jnp.zeros((TOK, 2 * TOK), F32)
    bias[1] = jnp.concatenate([apart, apart], 1)

    def attend(i, across, p):
        at = p * 128
        q = both(proj[i, :, pl.ds(at, 128)] * BF(0.125))
        k = proj[i, :, pl.ds(FEAT + at, 128)]
        v = proj[i, :, pl.ds(2 * FEAT + at, 128)]
        scores = dot_t(k, q) + bias[across]
        e = jnp.exp(scores - jnp.max(scores, 0, keepdims=True))
        w = (e * (1.0 / jnp.sum(e, 0, keepdims=True))).astype(BF)
        soft[i, p // 2, :, pl.ds(p % 2 * 2 * TOK, 2 * TOK)] = w
        mixed[:, pl.ds(at, 128)] = unite(t_dot(w, v)).astype(BF)

    head_of = lax.broadcasted_iota(jnp.int32, (TOK, 256), 1) // 64
    zeros = jnp.zeros((TOK, 256), BF)

    def four(x):
        return jnp.concatenate([jnp.where(head_of == h, x, zeros) for h in range(4)], 0)

    def attend_back(i, p):
        at = p * 256
        q = four(proj[i, :, pl.ds(at, 256)] * BF(0.125))
        k = proj[i, :, pl.ds(FEAT + at, 256)]
        v = proj[i, :, pl.ds(2 * FEAT + at, 256)]
        g = four(mixed[:, pl.ds(at, 256)])
        w = soft[i, p]
        dw = dot_t(v, g)
        wf = w.astype(F32)
        ds = (wf * (dw - jnp.sum(dw * wf, 0, keepdims=True))).astype(BF)
        d = t_dot(ds, k)
        dq = d[:TOK]
        for h in range(1, 4):
            dq = jnp.where(head_of == h, d[h * TOK:(h + 1) * TOK], dq)
        dproj[:, pl.ds(at, 256)] = (dq * 0.125).astype(BF)
        dproj[:, pl.ds(FEAT + at, 256)] = dot(ds, q).astype(BF)
        dproj[:, pl.ds(2 * FEAT + at, 256)] = dot(w, g).astype(BF)

    def windows(forward, ready, local_ref, tall, flat, quad, results, copies):
        def step(i, carry):
            across_lat, across_lon = i % 2, i // 2
            wr = WLAT * (li + dlat * across_lat)
            wc = WLON * (lj + dlon * across_lon)

            @pl.when(i == 0)
            def _():
                x = local_ref[pl.ds(s_lat, WLAT), pl.ds(s_lon, WLON)]
                token[...] = x.reshape(TOK, FEAT)

            @pl.when(i == 1)
            def _():
                ready[0].wait_recv()
                x = tall[pl.ds(t_lat + wr, WLAT), pl.ds(s_lon, WLON)]
                token[...] = x.reshape(TOK, FEAT)

            @pl.when(i == 2)
            def _():
                ready[1].wait_recv()
                x = flat[pl.ds(s_lat, WLAT), pl.ds(t_lon + wc, WLON)]
                token[...] = x.reshape(TOK, FEAT)

            @pl.when(i == 3)
            def _():
                mine = (pl.ds(quad_r, WLAT), pl.ds(quad_c, WLON))
                quad[mine] = local_ref[pl.ds(far_r, WLAT), pl.ds(far_c, WLON)]
                quad[pl.ds(qhalo_r, halo_lat), mine[1]] = tall[
                    pl.ds(halo_r, halo_lat), pl.ds(far_c, WLON)
                ]
                quad[mine[0], pl.ds(qhalo_c, halo_lon)] = flat[
                    pl.ds(far_r, WLAT), pl.ds(halo_c, halo_lon)
                ]
                ready[2].wait_recv()
                x = quad[pl.ds(t_lat, WLAT), pl.ds(t_lon, WLON)]
                token[...] = x.reshape(TOK, FEAT)

            if forward:
                x = token[...].astype(F32)
                mean = jnp.mean(x, -1, keepdims=True)
                x = x - mean
                inv = lax.rsqrt(jnp.mean(x * x, -1, keepdims=True) + EPS)
                x = x * inv
                norm[i] = x
                rstd[i] = jnp.broadcast_to(inv, (TOK, 128))
                proj[i] = dot((x * gain_attn[...]).astype(BF), w_qkv[...]).astype(BF)
                for p in range(PAIRS):
                    attend(i, across_lat, p)
                result = dot(mixed[...], w_out[...]).astype(BF)
            else:
                mixed[...] = dot_t(token[...], w_out[...]).astype(BF)
                for p in range(PAIRS // 2):
                    attend_back(i, p)
                d = dot_t(dproj[...], w_qkv[...]).astype(BF).astype(F32) * gain_attn[...]
                nn = norm[i]
                inv = rstd[i][:, :1]
                result = (inv * (
                    d - jnp.mean(d, -1, keepdims=True) - nn * jnp.mean(d * nn, -1, keepdims=True)
                )).astype(BF)
            result = result.reshape(WLAT, WLON, 2, FEAT)
            for ref, at_c in results:
                ref[pl.ds(back_r + wr, WLAT), pl.ds(at_c + wc, WLON)] = result
            for turn, part in ((1, copies[:1]), (2, copies[4:]), (3, copies[1:4])):
                @pl.when(i == turn)
                def _(part=part):
                    for copy in part:
                        copy.start()
            return carry

        lax.fori_loop(0, 4, step, 0)

    loads[0].wait()
    loads[1].wait()
    strip, slim = TOK // STRIPS, cols // STRIPS
    thin = slim // 2

    def quarter_back(j, carry):
        at = pl.multiple_of(j * FEAT, FEAT)
        x = jnp.concatenate(
            [cot_coarse[:, k * thin:(k + 1) * thin].reshape(strip, 2 * FEAT) for k in range(STRIPS)], 0
        )
        y = dot_t(x, w_merge[pl.ds(at, FEAT), :]).astype(BF)
        gm[:, :, pl.ds(at, FEAT)] = y.reshape(STRIPS, strip, FEAT)
        return carry

    lax.fori_loop(0, 4, quarter_back, 0)
    first[2].start()
    for load in loads[2:8]:
        load.wait()
    windows(True, first, own, xtall, xflat, xquad, ((btall, 0), (bext, back_c)), second)
    loads[8].wait()
    loads[9].wait()
    second[0].wait_recv()
    second[3].wait_recv()

    start_r, start_c = halo_lat - t_lat, halo_lon - t_lon
    width = 4 * FEAT
    patches = (rows // 2, 2, cols // 2, 2, 2, FEAT)
    quarters = [(a, b) for a in range(2) for b in range(2)]

    def merge(turn, carry):
        j = turn if lj else lax.rem(turn + 1, STRIPS)
        mine = pl.ds(slim * j, slim)

        @pl.when(turn < STRIPS - 1)
        def _():
            placed = btall[pl.ds(start_r, rows), pl.ds(start_c - back_c + slim * j, slim)]
            skip[:, mine] = (own[:, mine].astype(F32) + placed.astype(F32)).astype(BF)

        @pl.when(turn == STRIPS - 1)
        def _():
            for i in (1, 2, 4):
                second[i].wait_recv()
            bext[pl.ds(bhalo_r, halo_lat), pl.ds(back_c, cols)] = btall[pl.ds(bhalo_r, halo_lat)]
            placed = bext[pl.ds(start_r, rows), pl.ds(start_c + slim * j, slim)]
            skip[:, mine] = (own[:, mine].astype(F32) + placed.astype(F32)).astype(BF)

        def quarter(ref, a, b):
            return ref.reshape(*patches)[:, a, pl.ds(thin * j, thin), b].reshape(strip, FEAT)

        parts = [quarter(skip, a, b).astype(F32) for a, b in quarters]
        mean = sum(jnp.sum(x, -1, keepdims=True) for x in parts) / width
        parts = [x - mean for x in parts]
        inv = lax.rsqrt(sum(jnp.sum(x * x, -1, keepdims=True) for x in parts) / width + EPS)
        parts = [x * inv for x in parts]
        grads = []
        for i, x in enumerate(parts):
            gain = gain_merge[:, pl.ds(i * FEAT, FEAT)]
            merged[j, :, pl.ds(i * FEAT, FEAT)] = (x * gain).astype(BF)
            grads.append(gm[j, :, pl.ds(i * FEAT, FEAT)].astype(F32) * gain)
        mean_g = sum(jnp.sum(g, -1, keepdims=True) for g in grads) / width
        mean_gx = sum(jnp.sum(g * x, -1, keepdims=True) for g, x in zip(grads, parts)) / width
        for (a, b), g, x in zip(quarters, grads, parts):
            d = (inv * (g - mean_g - x * mean_gx)).astype(BF) + quarter(cot_skip, a, b)
            gskip.reshape(*patches)[:, a, pl.ds(thin * j, thin), b] = d.reshape(
                rows // 2, thin, 2, FEAT
            )
        return carry

    lax.fori_loop(0, STRIPS, merge, 0)
    third[1].start()
    third[0].start()
    gtall[pl.ds(own_r, rows)] = gskip[...]
    gflat[:, pl.ds(own_c, cols)] = gskip[...]
    skip_out = pltpu.make_async_copy(skip, skip_hbm, out_sem.at[0])
    skip_out.start()
    def coarse_part(j, carry):
        at = pl.multiple_of(j * FEAT, FEAT)
        x = merged.reshape(TOK, width)[...]
        y = dot(x, w_merge[:, pl.ds(at, FEAT)]).astype(BF)
        for k in range(STRIPS):
            coarse[:, k * thin:(k + 1) * thin, :, pl.ds(at, FEAT)] = y[
                k * strip:(k + 1) * strip
            ].reshape(rows // 2, thin, 2, FEAT)
        return carry

    lax.fori_loop(0, 2, coarse_part, 0)
    coarse_out = pltpu.make_async_copy(coarse, coarse_hbm, out_sem.at[1])
    coarse_out.start()
    third[2].start()
    windows(False, third, gskip, gtall, gflat, gquad, ((rext, back_c),), fourth)
    for copy in fourth:
        copy.wait_recv()

    def grad_out(j):
        mine = pl.ds(4 * j, 4)
        return pltpu.make_async_copy(out.at[mine], grad_hbm.at[mine], out_sem.at[2 + j])

    def finish(j, carry):
        mine = pl.ds(4 * j, 4)
        out[mine] = gskip[mine] + rext[pl.ds(start_r + 4 * j, 4), pl.ds(start_c, cols)]
        grad_out(j).start()
        return carry

    lax.fori_loop(0, rows // 4, finish, 0)
    for copy in first + second + third + fourth:
        copy.wait_send()
    skip_out.wait()
    coarse_out.wait()
    for j in range(rows // 4):
        grad_out(j).wait()


def block(behind_lat, behind_lon, halo_lat, halo_lon, ident, args):
    (inputs, shift_lat, shift_lon, gain_attn, w_qkv, w_out, gain_merge, w_merge,
     cot_coarse, cot_skip) = args
    rows, cols, lev, feat = inputs.shape
    wide = (rows + halo_lat, cols + halo_lon, lev, feat)
    smem = pl.BlockSpec(memory_space=pltpu.SMEM)
    hbm = pl.BlockSpec(memory_space=pltpu.HBM)
    anyw = pl.BlockSpec(memory_space=pl.ANY)
    tile, coarse = pltpu.VMEM(inputs.shape, BF), pltpu.VMEM(cot_coarse.shape, BF)
    tall = pltpu.VMEM((rows + halo_lat, cols, lev, feat), BF)
    flat = pltpu.VMEM((rows, cols + halo_lon, lev, feat), BF)
    quad = pltpu.VMEM((WLAT + halo_lat, WLON + halo_lon, lev, feat), BF)
    return pl.pallas_call(
        functools.partial(kernel, behind_lat, behind_lon, halo_lat, halo_lon),
        out_shape=(
            jax.ShapeDtypeStruct(cot_coarse.shape, BF),
            jax.ShapeDtypeStruct(inputs.shape, BF),
            jax.ShapeDtypeStruct(inputs.shape, BF),
        ),
        in_specs=[hbm, smem] + [hbm] * 8,
        out_specs=(anyw, anyw, anyw),
        scratch_shapes=[
            pltpu.SMEM((1,), jnp.int32),
            pltpu.VMEM((1, feat), F32),
            pltpu.VMEM((1, 4 * feat), F32),
            tile,
            tall, tall, tall, flat, flat, quad, quad,
            pltpu.VMEM(wide, BF),
            pltpu.VMEM(wide, BF),
            tile, tile, tile, coarse, coarse, tile,
            pltpu.VMEM(w_qkv.shape, BF),
            pltpu.VMEM(w_out.shape, BF),
            pltpu.VMEM(w_merge.shape, BF),
            pltpu.VMEM((STRIPS, TOK // STRIPS, 4 * FEAT), BF),
            pltpu.VMEM((STRIPS, TOK // STRIPS, 4 * FEAT), BF),
            pltpu.VMEM((TOK, FEAT), BF),
            pltpu.VMEM((4, TOK, FEAT), F32),
            pltpu.VMEM((4, TOK, 128), F32),
            pltpu.VMEM((4, TOK, 3 * FEAT), BF),
            pltpu.VMEM((TOK, FEAT), BF),
            pltpu.VMEM((4, PAIRS // 2, TOK, 4 * TOK), BF),
            pltpu.VMEM((TOK, 3 * FEAT), BF),
            pltpu.VMEM((2, TOK, 2 * TOK), F32),
            pltpu.SemaphoreType.DMA((11,)),
            pltpu.SemaphoreType.DMA((2 + rows // 4,)),
            pltpu.SemaphoreType.DMA((4, 5)),
            pltpu.SemaphoreType.DMA((4, 5)),
        ],
        compiler_params=pltpu.CompilerParams(
            collective_id=ident, has_side_effects=True, vmem_limit_bytes=VMEM
        ),
    )(
        shift_lat, shift_lon, gain_attn.reshape(1, -1), gain_merge.reshape(1, -1),
        inputs, w_qkv, w_out, w_merge, cot_coarse, cot_skip,
    )


def deliver(coarse, skip, grad, coarse_hbm, skip_hbm, grad_hbm, sem):
    copies = [
        pltpu.make_async_copy(src, dst, sem.at[i])
        for i, (src, dst) in enumerate(((coarse, coarse_hbm), (skip, skip_hbm), (grad, grad_hbm)))
    ]
    for copy in copies:
        copy.start()
    for copy in copies:
        copy.wait()


def hand_out(results):
    anyw = pl.BlockSpec(memory_space=pl.ANY)
    return pl.pallas_call(
        deliver,
        out_shape=tuple(jax.ShapeDtypeStruct(x.shape, x.dtype) for x in results),
        in_specs=[anyw] * 3,
        out_specs=(pl.BlockSpec(memory_space=pltpu.HBM),) * 3,
        scratch_shapes=[pltpu.SemaphoreType.DMA((3,))],
    )(*results)


def local(*args):
    shift = args[2][0]
    kinds = ((False, 3), (False, 5), (True, 6), (True, 3))
    which = sum((shift > last).astype(jnp.int32) for last in (3, 5, 8))
    results = lax.switch(
        which,
        [
            functools.partial(block, False, behind, WLAT - 1, halo, i)
            for i, (behind, halo) in enumerate(kinds)
        ],
        args,
    )
    return hand_out(results)


def solution(mesh):
    tile = P("lat", "lon", None, None)
    return jax.shard_map(
        local,
        mesh=mesh,
        in_specs=(tile, P(), P(), P(), P(), P(), P(), P(), tile, tile),
        out_specs=(tile, tile, tile),
        check_vma=False,
    )
```

```python
import functools

import jax
import jax.numpy as jnp
from jax import lax
from jax.experimental import pallas as pl
from jax.experimental.pallas import tpu as pltpu
from jax.sharding import PartitionSpec as P

WLAT = 6
WLON = 12
PAIRS = 4
TOK = 144
FEAT = 512
EPS = 1e-05
BF = jnp.bfloat16
F32 = jnp.float32
MESH = pl.DeviceIdType.MESH
VMEM = 48 * 2**20
STRIPS = 3


def dot(a, b):
    return jnp.dot(a, b, preferred_element_type=F32)


def dot_t(a, b):
    return lax.dot_general(a, b, (((1,), (1,)), ((), ())), preferred_element_type=F32)


def t_dot(a, b):
    return lax.dot_general(a, b, (((0,), (0,)), ((), ())), preferred_element_type=F32)


def kernel(
    behind_lat, behind_lon, halo_lat, halo_lon,
    shift_lat_hbm, shift_lon, gain_attn_hbm, gain_merge_hbm,
    inputs, w_qkv_hbm, w_out_hbm, w_merge_hbm, cot_coarse_hbm, cot_skip_hbm,
    coarse_hbm, skip_hbm, grad_hbm,
    shift_lat, gain_attn, gain_merge,
    own, xtall, btall, gtall, xflat, gflat, xquad, gquad, bext, rext, gskip, skip, cot_skip, cot_coarse, coarse, out,
    w_qkv, w_out, w_merge,
    gm, merged, token, norm, rstd, proj, mixed, soft, dproj, bias,
    local_sem, out_sem, send_sem, recv_sem,
):
    rows, cols = own.shape[0], own.shape[1]
    lat, lon = lax.axis_index("lat"), lax.axis_index("lon")
    nlat, nlon = lax.axis_size("lat"), lax.axis_size("lon")
    band = rows * nlat
    li, lj = int(behind_lat), int(behind_lon)

    def device(step_lat, step_lon):
        return (lax.rem(lat + step_lat + nlat, nlat), lax.rem(lon + step_lon + nlon, nlon))

    dlat, dlon = 1 - 2 * li, 1 - 2 * lj
    steps = ((dlat, 0), (0, dlon), (dlat, dlon))
    own_r, own_c = li * halo_lat, lj * halo_lon
    halo_r, halo_c = (1 - li) * rows, (1 - lj) * cols
    back_r, back_c = (1 - li) * halo_lat, (1 - lj) * halo_lon
    bhalo_r, bhalo_c = li * rows, lj * cols
    edge_r, edge_c = li * (rows - halo_lat), lj * (cols - halo_lon)
    bedge_r, bedge_c = (1 - li) * (rows - halo_lat), (1 - lj) * (cols - halo_lon)

    def send(phase, i, source, src, target, dst, step_lat, step_lon):
        (r, c, n, m), (tr, tc) = src, dst
        return pltpu.make_async_remote_copy(
            src_ref=source.at[pl.ds(r, n), pl.ds(c, m)],
            dst_ref=target.at[pl.ds(tr, n), pl.ds(tc, m)],
            send_sem=send_sem.at[phase, i],
            recv_sem=recv_sem.at[phase, i],
            device_id=device(step_lat, step_lon),
            device_id_type=MESH,
        )

    far_r, far_c = (1 - li) * WLAT, (1 - lj) * WLON
    quad_r, quad_c = li * halo_lat, lj * halo_lon
    qhalo_r, qhalo_c = (1 - li) * WLAT, (1 - lj) * WLON

    def ahead(phase, source, tall, flat, quad):
        er, ec = edge_r, edge_c
        return (
            send(phase, 0, source, (er, 0, halo_lat, cols), tall, (halo_r, 0), -dlat, 0),
            send(phase, 1, source, (0, ec, rows, halo_lon), flat, (0, halo_c), 0, -dlon),
            send(phase, 2, source, (er, ec, halo_lat, halo_lon), quad, (qhalo_r, qhalo_c), -dlat, -dlon),
        )

    def back(phase, tall, at_c, wide):
        er, ec = back_r + bedge_r, back_c + bedge_c
        far_r, near_r = back_r + (1 - li) * WLAT, back_r + li * WLAT
        far_c, near_c = at_c + (1 - lj) * WLON, at_c + lj * WLON
        return (
            send(phase, 0, tall, (er, near_c, halo_lat, WLON), tall, (bhalo_r, near_c), dlat, 0),
            send(phase, 1, wide, (er, ec, halo_lat, halo_lon), wide, (bhalo_r, bhalo_c), dlat, dlon),
            send(phase, 2, wide, (far_r, ec, WLAT, halo_lon), wide, (far_r, bhalo_c), 0, dlon),
            send(phase, 3, tall, (er, far_c, halo_lat, WLON), tall, (bhalo_r, far_c), dlat, 0),
            send(phase, 4, wide, (near_r, ec, WLAT, halo_lon), wide, (near_r, bhalo_c), 0, dlon),
        )

    loads = [
        pltpu.make_async_copy(src, dst, local_sem.at[i])
        for i, (src, dst) in enumerate((
            (cot_coarse_hbm, cot_coarse),
            (w_merge_hbm, w_merge),
            (gain_attn_hbm, gain_attn),
            (inputs, own),
            (w_qkv_hbm, w_qkv),
            (w_out_hbm, w_out),
            (inputs, xtall.at[pl.ds(own_r, rows)]),
            (inputs, xflat.at[:, pl.ds(own_c, cols)]),
            (cot_skip_hbm, cot_skip),
            (gain_merge_hbm, gain_merge),
            (shift_lat_hbm, shift_lat),
        ))
    ]
    barrier = pltpu.get_barrier_semaphore()
    for sr, sc in steps:
        pl.semaphore_signal(barrier, inc=1, device_id=device(sr, sc), device_id_type=MESH)
        pl.semaphore_signal(barrier, inc=1, device_id=device(-sr, -sc), device_id_type=MESH)
    early = (loads[0], loads[1], loads[10])
    for load in early:
        load.start()
    pl.semaphore_wait(barrier, 6)
    first = ahead(0, inputs, xtall, xflat, xquad)
    first[1].start()
    first[0].start()
    for load in loads[2:10]:
        load.start()
    second = back(1, btall, 0, bext)
    third = ahead(2, gskip, gtall, gflat, gquad)
    fourth = back(3, rext, back_c, rext)

    loads[10].wait()
    s_lat, s_lon = shift_lat[0], shift_lon[0]
    t_lat = jnp.clip(s_lat - li * (WLAT - halo_lat), 0, halo_lat)
    t_lon = jnp.clip(s_lon - lj * (WLON - halo_lon), 0, halo_lon)

    low = lax.broadcasted_iota(jnp.int32, (TOK, 128), 1) < 64
    zero = jnp.zeros((TOK, 128), BF)

    def both(x):
        return jnp.concatenate([jnp.where(low, x, zero), jnp.where(low, zero, x)], 0)

    def unite(x):
        return jnp.where(low, x[:TOK], x[TOK:])

    start = lax.rem(rows * lat + WLAT * (1 - 2 * li) + band, band)
    edge = 2 * WLON * (band - s_lat - start)
    row_in = lax.broadcasted_iota(jnp.int32, (TOK, TOK), 0) >= edge
    col_in = lax.broadcasted_iota(jnp.int32, (TOK, TOK), 1) >= edge
    apart = jnp.where(row_in != col_in, F32(-1e30), F32(0.0))
    bias[0] = jnp.zeros((TOK, 2 * TOK), F32)
    bias[1] = jnp.concatenate([apart, apart], 1)

    def attend(i, across, p):
        at = p * 128
        q = both(proj[i, :, pl.ds(at, 128)] * BF(0.125))
        k = proj[i, :, pl.ds(FEAT + at, 128)]
        v = proj[i, :, pl.ds(2 * FEAT + at, 128)]
        scores = dot_t(k, q) + bias[across]
        e = jnp.exp(scores - jnp.max(scores, 0, keepdims=True))
        w = (e * (1.0 / jnp.sum(e, 0, keepdims=True))).astype(BF)
        soft[i, p // 2, :, pl.ds(p % 2 * 2 * TOK, 2 * TOK)] = w
        mixed[:, pl.ds(at, 128)] = unite(t_dot(w, v)).astype(BF)

    head_of = lax.broadcasted_iota(jnp.int32, (TOK, 256), 1) // 64
    zeros = jnp.zeros((TOK, 256), BF)

    def four(x):
        return jnp.concatenate([jnp.where(head_of == h, x, zeros) for h in range(4)], 0)

    def attend_back(i, p):
        at = p * 256
        q = four(proj[i, :, pl.ds(at, 256)] * BF(0.125))
        k = proj[i, :, pl.ds(FEAT + at, 256)]
        v = proj[i, :, pl.ds(2 * FEAT + at, 256)]
        g = four(mixed[:, pl.ds(at, 256)])
        w = soft[i, p]
        dw = dot_t(v, g)
        wf = w.astype(F32)
        ds = (wf * (dw - jnp.sum(dw * wf, 0, keepdims=True))).astype(BF)
        d = t_dot(ds, k)
        dq = d[:TOK]
        for h in range(1, 4):
            dq = jnp.where(head_of == h, d[h * TOK:(h + 1) * TOK], dq)
        dproj[:, pl.ds(at, 256)] = (dq * 0.125).astype(BF)
        dproj[:, pl.ds(FEAT + at, 256)] = dot(ds, q).astype(BF)
        dproj[:, pl.ds(2 * FEAT + at, 256)] = dot(w, g).astype(BF)

    def windows(forward, ready, local_ref, tall, flat, quad, results, copies):
        def step(i, carry):
            across_lat, across_lon = i % 2, i // 2
            wr = WLAT * (li + dlat * across_lat)
            wc = WLON * (lj + dlon * across_lon)

            @pl.when(i == 0)
            def _():
                x = local_ref[pl.ds(s_lat, WLAT), pl.ds(s_lon, WLON)]
                token[...] = x.reshape(TOK, FEAT)

            @pl.when(i == 1)
            def _():
                ready[0].wait_recv()
                x = tall[pl.ds(t_lat + wr, WLAT), pl.ds(s_lon, WLON)]
                token[...] = x.reshape(TOK, FEAT)

            @pl.when(i == 2)
            def _():
                ready[1].wait_recv()
                x = flat[pl.ds(s_lat, WLAT), pl.ds(t_lon + wc, WLON)]
                token[...] = x.reshape(TOK, FEAT)

            @pl.when(i == 3)
            def _():
                mine = (pl.ds(quad_r, WLAT), pl.ds(quad_c, WLON))
                quad[mine] = local_ref[pl.ds(far_r, WLAT), pl.ds(far_c, WLON)]
                quad[pl.ds(qhalo_r, halo_lat), mine[1]] = tall[
                    pl.ds(halo_r, halo_lat), pl.ds(far_c, WLON)
                ]
                quad[mine[0], pl.ds(qhalo_c, halo_lon)] = flat[
                    pl.ds(far_r, WLAT), pl.ds(halo_c, halo_lon)
                ]
                ready[2].wait_recv()
                x = quad[pl.ds(t_lat, WLAT), pl.ds(t_lon, WLON)]
                token[...] = x.reshape(TOK, FEAT)

            if forward:
                x = token[...].astype(F32)
                mean = jnp.mean(x, -1, keepdims=True)
                x = x - mean
                inv = lax.rsqrt(jnp.mean(x * x, -1, keepdims=True) + EPS)
                x = x * inv
                norm[i] = x
                rstd[i] = jnp.broadcast_to(inv, (TOK, 128))
                proj[i] = dot((x * gain_attn[...]).astype(BF), w_qkv[...]).astype(BF)
                for p in range(PAIRS):
                    attend(i, across_lat, p)
                result = dot(mixed[...], w_out[...]).astype(BF)
            else:
                mixed[...] = dot_t(token[...], w_out[...]).astype(BF)
                for p in range(PAIRS // 2):
                    attend_back(i, p)
                d = dot_t(dproj[...], w_qkv[...]).astype(BF).astype(F32) * gain_attn[...]
                nn = norm[i]
                inv = rstd[i][:, :1]
                result = (inv * (
                    d - jnp.mean(d, -1, keepdims=True) - nn * jnp.mean(d * nn, -1, keepdims=True)
                )).astype(BF)
            result = result.reshape(WLAT, WLON, 2, FEAT)
            for ref, at_c in results:
                ref[pl.ds(back_r + wr, WLAT), pl.ds(at_c + wc, WLON)] = result
            for turn, part in ((1, copies[:1]), (2, copies[4:]), (3, (copies[2], copies[1], copies[3]))):
                @pl.when(i == turn)
                def _(part=part):
                    for copy in part:
                        copy.start()
            return carry

        lax.fori_loop(0, 4, step, 0)

    loads[0].wait()
    loads[1].wait()
    strip, slim = TOK // STRIPS, cols // STRIPS
    thin = slim // 2

    def quarter_back(j, carry):
        at = pl.multiple_of(j * FEAT, FEAT)
        x = jnp.concatenate(
            [cot_coarse[:, k * thin:(k + 1) * thin].reshape(strip, 2 * FEAT) for k in range(STRIPS)], 0
        )
        y = dot_t(x, w_merge[pl.ds(at, FEAT), :]).astype(BF)
        gm[:, :, pl.ds(at, FEAT)] = y.reshape(STRIPS, strip, FEAT)
        return carry

    lax.fori_loop(0, 4, quarter_back, 0)
    first[2].start()
    for load in loads[2:8]:
        load.wait()
    windows(True, first, own, xtall, xflat, xquad, ((btall, 0), (bext, back_c)), second)
    loads[8].wait()
    loads[9].wait()
    second[0].wait_recv()
    second[3].wait_recv()

    start_r, start_c = halo_lat - t_lat, halo_lon - t_lon
    width = 4 * FEAT
    patches = (rows // 2, 2, cols // 2, 2, 2, FEAT)
    quarters = [(a, b) for a in range(2) for b in range(2)]

    def merge(turn, carry):
        j = turn if lj else lax.rem(turn + 1, STRIPS)
        mine = pl.ds(slim * j, slim)

        @pl.when(turn < STRIPS - 1)
        def _():
            placed = btall[pl.ds(start_r, rows), pl.ds(start_c - back_c + slim * j, slim)]
            skip[:, mine] = (own[:, mine].astype(F32) + placed.astype(F32)).astype(BF)

        @pl.when(turn == STRIPS - 1)
        def _():
            for i in (1, 2, 4):
                second[i].wait_recv()
            bext[pl.ds(bhalo_r, halo_lat), pl.ds(back_c, cols)] = btall[pl.ds(bhalo_r, halo_lat)]
            placed = bext[pl.ds(start_r, rows), pl.ds(start_c + slim * j, slim)]
            skip[:, mine] = (own[:, mine].astype(F32) + placed.astype(F32)).astype(BF)

        def quarter(ref, a, b):
            return ref.reshape(*patches)[:, a, pl.ds(thin * j, thin), b].reshape(strip, FEAT)

        parts = [quarter(skip, a, b).astype(F32) for a, b in quarters]
        mean = sum(jnp.sum(x, -1, keepdims=True) for x in parts) / width
        parts = [x - mean for x in parts]
        inv = lax.rsqrt(sum(jnp.sum(x * x, -1, keepdims=True) for x in parts) / width + EPS)
        parts = [x * inv for x in parts]
        grads = []
        for i, x in enumerate(parts):
            gain = gain_merge[:, pl.ds(i * FEAT, FEAT)]
            merged[j, :, pl.ds(i * FEAT, FEAT)] = (x * gain).astype(BF)
            grads.append(gm[j, :, pl.ds(i * FEAT, FEAT)].astype(F32) * gain)
        mean_g = sum(jnp.sum(g, -1, keepdims=True) for g in grads) / width
        mean_gx = sum(jnp.sum(g * x, -1, keepdims=True) for g, x in zip(grads, parts)) / width
        for (a, b), g, x in zip(quarters, grads, parts):
            d = (inv * (g - mean_g - x * mean_gx)).astype(BF) + quarter(cot_skip, a, b)
            gskip.reshape(*patches)[:, a, pl.ds(thin * j, thin), b] = d.reshape(
                rows // 2, thin, 2, FEAT
            )
        return carry

    lax.fori_loop(0, STRIPS, merge, 0)
    third[1].start()
    third[0].start()
    gtall[pl.ds(own_r, rows)] = gskip[...]
    gflat[:, pl.ds(own_c, cols)] = gskip[...]
    skip_out = pltpu.make_async_copy(skip, skip_hbm, out_sem.at[0])
    skip_out.start()
    def coarse_part(j, carry):
        at = pl.multiple_of(j * FEAT, FEAT)
        x = merged.reshape(TOK, width)[...]
        y = dot(x, w_merge[:, pl.ds(at, FEAT)]).astype(BF)
        for k in range(STRIPS):
            coarse[:, k * thin:(k + 1) * thin, :, pl.ds(at, FEAT)] = y[
                k * strip:(k + 1) * strip
            ].reshape(rows // 2, thin, 2, FEAT)
        return carry

    lax.fori_loop(0, 2, coarse_part, 0)
    coarse_out = pltpu.make_async_copy(coarse, coarse_hbm, out_sem.at[1])
    coarse_out.start()
    third[2].start()
    windows(False, third, gskip, gtall, gflat, gquad, ((rext, back_c),), fourth)
    for copy in fourth:
        copy.wait_recv()

    def grad_out(j):
        mine = pl.ds(4 * j, 4)
        return pltpu.make_async_copy(out.at[mine], grad_hbm.at[mine], out_sem.at[2 + j])

    def finish(j, carry):
        mine = pl.ds(4 * j, 4)
        out[mine] = gskip[mine] + rext[pl.ds(start_r + 4 * j, 4), pl.ds(start_c, cols)]
        grad_out(j).start()
        return carry

    lax.fori_loop(0, rows // 4, finish, 0)
    for copy in first + second + third + fourth:
        copy.wait_send()
    skip_out.wait()
    coarse_out.wait()
    for j in range(rows // 4):
        grad_out(j).wait()


def block(behind_lat, behind_lon, halo_lat, halo_lon, ident, args):
    (inputs, shift_lat, shift_lon, gain_attn, w_qkv, w_out, gain_merge, w_merge,
     cot_coarse, cot_skip) = args
    rows, cols, lev, feat = inputs.shape
    wide = (rows + halo_lat, cols + halo_lon, lev, feat)
    smem = pl.BlockSpec(memory_space=pltpu.SMEM)
    hbm = pl.BlockSpec(memory_space=pltpu.HBM)
    anyw = pl.BlockSpec(memory_space=pl.ANY)
    tile, coarse = pltpu.VMEM(inputs.shape, BF), pltpu.VMEM(cot_coarse.shape, BF)
    tall = pltpu.VMEM((rows + halo_lat, cols, lev, feat), BF)
    flat = pltpu.VMEM((rows, cols + halo_lon, lev, feat), BF)
    quad = pltpu.VMEM((WLAT + halo_lat, WLON + halo_lon, lev, feat), BF)
    return pl.pallas_call(
        functools.partial(kernel, behind_lat, behind_lon, halo_lat, halo_lon),
        out_shape=(
            jax.ShapeDtypeStruct(cot_coarse.shape, BF),
            jax.ShapeDtypeStruct(inputs.shape, BF),
            jax.ShapeDtypeStruct(inputs.shape, BF),
        ),
        in_specs=[hbm, smem] + [hbm] * 8,
        out_specs=(anyw, anyw, anyw),
        scratch_shapes=[
            pltpu.SMEM((1,), jnp.int32),
            pltpu.VMEM((1, feat), F32),
            pltpu.VMEM((1, 4 * feat), F32),
            tile,
            tall, tall, tall, flat, flat, quad, quad,
            pltpu.VMEM(wide, BF),
            pltpu.VMEM(wide, BF),
            tile, tile, tile, coarse, coarse, tile,
            pltpu.VMEM(w_qkv.shape, BF),
            pltpu.VMEM(w_out.shape, BF),
            pltpu.VMEM(w_merge.shape, BF),
            pltpu.VMEM((STRIPS, TOK // STRIPS, 4 * FEAT), BF),
            pltpu.VMEM((STRIPS, TOK // STRIPS, 4 * FEAT), BF),
            pltpu.VMEM((TOK, FEAT), BF),
            pltpu.VMEM((4, TOK, FEAT), F32),
            pltpu.VMEM((4, TOK, 128), F32),
            pltpu.VMEM((4, TOK, 3 * FEAT), BF),
            pltpu.VMEM((TOK, FEAT), BF),
            pltpu.VMEM((4, PAIRS // 2, TOK, 4 * TOK), BF),
            pltpu.VMEM((TOK, 3 * FEAT), BF),
            pltpu.VMEM((2, TOK, 2 * TOK), F32),
            pltpu.SemaphoreType.DMA((11,)),
            pltpu.SemaphoreType.DMA((2 + rows // 4,)),
            pltpu.SemaphoreType.DMA((4, 5)),
            pltpu.SemaphoreType.DMA((4, 5)),
        ],
        compiler_params=pltpu.CompilerParams(
            collective_id=ident, has_side_effects=True, vmem_limit_bytes=VMEM
        ),
    )(
        shift_lat, shift_lon, gain_attn.reshape(1, -1), gain_merge.reshape(1, -1),
        inputs, w_qkv, w_out, w_merge, cot_coarse, cot_skip,
    )


def deliver(coarse, skip, grad, coarse_hbm, skip_hbm, grad_hbm, sem):
    copies = [
        pltpu.make_async_copy(src, dst, sem.at[i])
        for i, (src, dst) in enumerate(((coarse, coarse_hbm), (skip, skip_hbm), (grad, grad_hbm)))
    ]
    for copy in copies:
        copy.start()
    for copy in copies:
        copy.wait()


def hand_out(results):
    anyw = pl.BlockSpec(memory_space=pl.ANY)
    return pl.pallas_call(
        deliver,
        out_shape=tuple(jax.ShapeDtypeStruct(x.shape, x.dtype) for x in results),
        in_specs=[anyw] * 3,
        out_specs=(pl.BlockSpec(memory_space=pltpu.HBM),) * 3,
        scratch_shapes=[pltpu.SemaphoreType.DMA((3,))],
    )(*results)


def local(*args):
    shift = args[2][0]
    kinds = ((False, 3), (False, 5), (True, 6), (True, 3))
    which = sum((shift > last).astype(jnp.int32) for last in (3, 5, 8))
    results = lax.switch(
        which,
        [
            functools.partial(block, False, behind, WLAT - 1, halo, i)
            for i, (behind, halo) in enumerate(kinds)
        ],
        args,
    )
    return hand_out(results)


def solution(mesh):
    tile = P("lat", "lon", None, None)
    return jax.shard_map(
        local,
        mesh=mesh,
        in_specs=(tile, P(), P(), P(), P(), P(), P(), P(), tile, tile),
        out_specs=(tile, tile, tile),
        check_vma=False,
    )
```
